256 devices in a mesh: ky: 16 (over x, y_hi, core), kx: 16 (over z, y_lo).
Axes of the slice: x: 4, y: 4 (y_hi: 2, y_lo: 2; y = y_hi * 2 + y_lo), z: 8, core: 2. Of those that a mesh axis runs over, the one named last changes fastest.
Arguments:
- spectrum: bfloat16 [2, 8192, 8192], P(None, 'ky', 'kx'), may hold values from -6 to 6
- pupil_field: bfloat16 [2, 1024, 1024], replicated, may hold values from -3 to 3
- amplitude: bfloat16 [16384, 16384], P('ky', 'kx'), may hold values from 0 to 2
- offsets: int32 [16, 16, 2], P('ky', 'kx'), may hold values from -384 to 7552, as said below
Outputs:
- spectrum_grad: float32 [2, 8192, 8192], P(None, 'ky', 'kx')
- pupil_grad: float32 [2097152], P(('ky', 'kx'))
The draws below stay inside these ranges and needn't reach their ends.
Inputs may be any that keep to these rules, and one draw needn't show every extreme that they name: offsets[i, j] = (i * 512 - 512/2 + dy, j * 512 - 512/2 + dx) with whole numbers dy, dx from -128 to 128; both ends of this range are taken in every draw.
All inputs are finite; a program needn't handle non-finite values.
Results may differ from the reference program's by a relative error of at most 0.0028.
Values may be sent and summed in bfloat16 or wider, within the bound.
No kernel may reach another device: no remote copies, remote signals or barrier semaphores. Data moves between devices by JAX's collectives and lax.ppermute only.
A program may use at most 192 MiB of HBM per device.

```python
import jax
import jax.numpy as jnp
from jax import lax

WIN = 1024
TILE = 512
SPEC_Y = 8192
SPEC_X = 8192
LEDS = 256
N_KY = 16
N_KX = 16


def draw_offsets(key, part):
    key = jax.random.fold_in(key, 11)
    subkeys = jax.random.split(key, 5)
    reach = TILE // 4
    jitter = jax.random.randint(subkeys[0], (N_KY, N_KX, 2), -reach, reach + 1).astype(jnp.int32)
    first_col = jax.random.randint(subkeys[1], (), 0, N_KX)
    second_col = jax.random.randint(subkeys[2], (), 0, N_KX)
    first_row = jax.random.randint(subkeys[3], (), 0, N_KY)
    second_row = jax.random.randint(subkeys[4], (), 0, N_KY)
    jitter = jitter.at[0, first_col, 0].set(-reach)
    jitter = jitter.at[N_KY - 1, second_col, 0].set(reach)
    jitter = jitter.at[first_row, 0, 1].set(-reach)
    jitter = jitter.at[second_row, N_KX - 1, 1].set(reach)
    row_base = jnp.arange(N_KY, dtype=jnp.int32)[:, None] * TILE - TILE // 2
    col_base = jnp.arange(N_KX, dtype=jnp.int32)[None, :] * TILE - TILE // 2
    row_part = row_base + jitter[:, :, 0]
    col_part = col_base + jitter[:, :, 1]
    return jnp.stack([row_part, col_part], axis=-1).astype(jnp.int32)


def levels(stream_key, dims, cuts, least, largest):
    loudness, own = 1.0, jax.random.fold_in(stream_key, 6)
    for dim, parts in cuts:
        draws = jnp.exp(jax.random.uniform(jax.random.fold_in(own, dim), (parts,), jnp.float32, least / len(cuts), largest / len(cuts)))
        loudness = loudness * jnp.repeat(draws, dims[dim] // parts).reshape([-1 if axis == dim else 1 for axis in range(len(dims))])
    return loudness


def normal_values(rng, dims, width, bound, cuts=(), kind=jnp.bfloat16):
    values = jax.random.normal(rng, dims, jnp.float32) * width
    if len(cuts) > 0:
        values = levels(rng, dims, cuts, -0.22, 0.18) * values
    return jnp.clip(values, min=-bound, max=bound).astype(kind)


def setup_inputs(seed: int = 0) -> dict:
    keys = jax.random.split(jax.random.key(seed), 5)
    spectrum = normal_values(keys[0], (2, SPEC_Y, SPEC_X), 1.0, 6.0, ((1, 16), (2, 16)))
    pupil_field = normal_values(keys[1], (2, WIN, WIN), 0.5, 3.0)
    amplitude = jnp.clip(2.0 * jax.random.uniform(keys[2], (WIN * N_KY, WIN * N_KX), jnp.float32) ** levels(keys[2], (WIN * N_KY, WIN * N_KX), ((0, 16), (1, 16)), -0.2, 0.2), 0.0, 2.0).astype(jnp.bfloat16)
    offsets = draw_offsets(jax.random.fold_in(keys[4], 71), 0)
    return dict(spectrum=spectrum, pupil_field=pupil_field, amplitude=amplitude, offsets=offsets)


AMP_FLOOR = 0.25


def reference(spectrum, pupil_field, amplitude, offsets):
    padding = TILE
    padded = jnp.pad(spectrum, ((0, 0), (padding, padding), (padding, padding)))
    pupil_complex = lax.complex(pupil_field[0].astype(jnp.float32), pupil_field[1].astype(jnp.float32))

    def one_led(carried, led_index):
        spec_sum, pupil_sum = carried
        led_row = led_index // N_KX
        led_col = led_index % N_KX
        row_start = (offsets[led_row, led_col, 0] + padding).astype(jnp.int32)
        col_start = (offsets[led_row, led_col, 1] + padding).astype(jnp.int32)
        zero_index = jnp.zeros((), jnp.int32)
        window = lax.dynamic_slice(padded, (zero_index, row_start, col_start), (2, WIN, WIN)).astype(jnp.float32)
        window_complex = lax.complex(window[0], window[1])
        amp_block = lax.dynamic_slice(amplitude, ((led_row * WIN).astype(jnp.int32), (led_col * WIN).astype(jnp.int32)), (WIN, WIN)).astype(jnp.float32)
        image_field = jnp.fft.ifft2(pupil_complex * window_complex, norm="ortho")
        magnitude = jnp.abs(image_field)
        residual = image_field - amp_block * image_field / jnp.maximum(magnitude, AMP_FLOOR)
        spec_residual = jnp.fft.fft2(residual, norm="ortho")
        window_grad = jnp.conj(pupil_complex) * spec_residual
        rounded = lax.optimization_barrier(jnp.stack([jnp.real(window_grad), jnp.imag(window_grad)]).astype(jnp.bfloat16))
        current = lax.dynamic_slice(spec_sum, (zero_index, row_start, col_start), (2, WIN, WIN))
        spec_sum = lax.dynamic_update_slice(spec_sum, current + rounded.astype(spec_sum.dtype), (zero_index, row_start, col_start))
        pupil_term = jnp.conj(window_complex) * spec_residual
        pupil_sum = pupil_sum + jnp.stack([jnp.real(pupil_term), jnp.imag(pupil_term)])
        return (spec_sum, pupil_sum), None

    start_state = (jnp.zeros(padded.shape, jnp.float32), jnp.zeros((2, WIN, WIN), jnp.float32))
    (spec_sum, pupil_sum), unused = lax.scan(one_led, start_state, jnp.arange(LEDS, dtype=jnp.int32))
    spectrum_grad = spec_sum[:, padding:padding + SPEC_Y, padding:padding + SPEC_X]
    pupil_grad = (pupil_sum / LEDS).reshape(-1)
    return spectrum_grad, pupil_grad
```

```python
import math

import jax
import jax.numpy as jnp
import ml_dtypes
import numpy as np
from jax import lax
from jax.experimental import pallas as pl
from jax.experimental.pallas import tpu as pltpu
from jax.sharding import Mesh
from jax.sharding import PartitionSpec as P

F32 = jnp.float32
BF16 = jnp.bfloat16
N = 1024
TILE = 512
RIM = 384
REGION = TILE + 2 * RIM
FLOOR2 = 0.0625


def split_np(t):
    hi = t.astype(np.float32).astype(ml_dtypes.bfloat16)
    lo = (t - hi.astype(np.float64)).astype(np.float32).astype(ml_dtypes.bfloat16)
    return hi, lo


def tables():
    b = np.arange(128)
    ang = 2.0 * np.pi / 128 * ((b[:, None] * b[None, :]) % 128)
    out = {}
    for name, sign in (("inv", 1.0), ("fwd", -1.0)):
        cr, ci = np.cos(ang) / 32.0, sign * np.sin(ang) / 32.0
        block = np.block([[cr, ci], [-ci, cr]])
        hi, lo = split_np(block)
        out["lane_" + name] = np.concatenate([hi, hi, lo], axis=0)
        out["row_" + name] = np.concatenate([hi.T, hi.T, lo.T], axis=1)
    tw = 2.0 * np.pi / N * (np.arange(8)[:, None] * b[None, :])
    tw = np.stack([np.cos(tw), np.sin(tw)]).astype(np.float32)
    out["tw_lane"] = tw.reshape(2, 8, 1, 128)
    out["tw_row"] = np.ascontiguousarray(np.broadcast_to(tw[:, :, :, None], (2, 8, 128, 128)))
    s = np.arange(N)
    perm = np.zeros((N, N), ml_dtypes.bfloat16)
    perm[s, (s // 128) + 8 * (s % 128)] = 1
    out["perm"] = perm
    return out


def cadd(p, q):
    return (p[0] + q[0], p[1] + q[1])


def csub(p, q):
    return (p[0] - q[0], p[1] - q[1])


def crot(p, sign):
    return (-p[1], p[0]) if sign > 0 else (p[1], -p[0])


def fft4(x0, x1, x2, x3, sign):
    t0, t1 = cadd(x0, x2), csub(x0, x2)
    t2, t3 = cadd(x1, x3), crot(csub(x1, x3), sign)
    return [cadd(t0, t2), cadd(t1, t3), csub(t0, t2), csub(t1, t3)]


def fft8(x, sign):
    even = fft4(x[0], x[2], x[4], x[6], sign)
    odd = fft4(x[1], x[3], x[5], x[7], sign)
    h = math.sqrt(0.5)
    r, i = odd[1]
    odd[1] = ((r - i) * h, (r + i) * h) if sign > 0 else ((r + i) * h, (i - r) * h)
    odd[2] = crot(odd[2], sign)
    r, i = odd[3]
    odd[3] = ((-r - i) * h, (r - i) * h) if sign > 0 else ((i - r) * h, (-r - i) * h)
    return [cadd(e, o) for e, o in zip(even, odd)] + [csub(e, o) for e, o in zip(even, odd)]


def split(x):
    hi = x.astype(BF16)
    return hi, (x - hi.astype(F32)).astype(BF16)


def dot(a, b):
    return jnp.dot(a, b, preferred_element_type=F32)


RB = 256
CB = 256


def led_body(
    pos_ref, own_ref, l_ref, r_ref, v_ref, vl_ref, vr_ref, i_ref, il_ref, ir_ref, pup_ref, ampl_ref,
    li_ref, lf_ref, ri_ref, rf_ref, twl_ref, twr_ref,
    oc_ref, ol_ref, or_ref, ov_ref, ovl_ref, ovr_ref, oi_ref, oil_ref, oir_ref, mine_ref, other_ref,
    w_ref, p_ref, amp_ref, a_ref, s_ref, s2_ref, z_ref, z2_ref, t_ref, in_sem, out_sem,
):
    r0, c0, core = pos_ref[0], pos_ref[1], pos_ref[2]
    outer = pl.multiple_of((RIM + TILE) * core, 128)
    inner = pl.multiple_of((RIM + TILE) * (1 - core), 128)
    places = []
    for start, count in ((RIM, TILE), (outer, RIM), (inner, RIM)):
        for col, wide in ((RIM, TILE), (0, RIM), (RIM + TILE, RIM)):
            places.append(w_ref.at[:, pl.ds(start, count), pl.ds(col, wide)])
    arrivals = (own_ref, l_ref, r_ref, v_ref, vl_ref, vr_ref, i_ref, il_ref, ir_ref)
    loads = [pltpu.make_async_copy(x, y, in_sem.at[k]) for k, (x, y) in enumerate(zip(arrivals, places))]
    loads.append(pltpu.make_async_copy(pup_ref, p_ref, in_sem.at[9]))
    amp_load = pltpu.make_async_copy(ampl_ref, amp_ref, in_sem.at[10])
    for load in loads:
        load.start()
    amp_load.start()

    def lane_tile(k):
        return pl.ds(k * 128, 128)

    lane = lax.broadcasted_iota(jnp.int32, (16, 128), 1)
    line = lax.broadcasted_iota(jnp.int32, (16, 128), 0)
    for load in loads:
        load.wait()

    @pl.loop(0, REGION // 16)
    def _(i):
        rows = pl.ds(pl.multiple_of(i * 16, 16), 16)
        for q in range(2):
            for a in range(2):
                here, there = w_ref[q, rows, lane_tile(a)].astype(F32), w_ref[q, rows, lane_tile(a + 8)].astype(F32)
                w_ref[q, rows, lane_tile(a)] = jnp.where(lane + 128 * a >= c0, here, there).astype(BF16)

    @pl.loop(0, 16)
    def _(i):
        k = pl.multiple_of(i * 16, 16)
        for q in range(2):
            for a in range(8):
                here = w_ref[q, pl.ds(k, 16), lane_tile(a)].astype(F32)
                there = w_ref[q, pl.ds(k + N, 16), lane_tile(a)].astype(F32)
                w_ref[q, pl.ds(k, 16), lane_tile(a)] = jnp.where(line + k >= r0, here, there).astype(BF16)

    @pl.loop(0, N // RB)
    def _(rb):
        @pl.loop(0, RB // 16)
        def _(i):
            rows = pl.ds(pl.multiple_of(rb * RB + i * 16, 16), 16)
            sub = pl.ds(pl.multiple_of(i * 16, 16), 16)
            x = []
            for a in range(8):
                pr, pi = p_ref[0, rows, lane_tile(a)].astype(F32), p_ref[1, rows, lane_tile(a)].astype(F32)
                wr, wi = w_ref[0, rows, lane_tile(a)].astype(F32), w_ref[1, rows, lane_tile(a)].astype(F32)
                x.append((pr * wr - pi * wi, pr * wi + pi * wr))
            for c, (yr, yi) in enumerate(fft8(x, 1)):
                if c > 0:
                    tr, ti = twl_ref[0, c], twl_ref[1, c]
                    yr, yi = yr * tr - yi * ti, yr * ti + yi * tr
                (hr, lr), (hi, li) = split(yr), split(yi)
                s_ref[c, sub, 0:128] = hr
                s_ref[c, sub, 128:256] = hi
                s_ref[c, sub, 256:384] = lr
                s_ref[c, sub, 384:512] = li

        rows = pl.ds(pl.multiple_of(rb * RB, RB), RB)
        for c in range(8):
            acc = dot(s_ref[c], li_ref[0:512]) + dot(s_ref[c, :, 0:256], li_ref[512:768])
            a_ref[0, rows, lane_tile(c)] = acc[:, 0:128]
            a_ref[1, rows, lane_tile(c)] = acc[:, 128:256]

    amp_load.wait()

    @pl.loop(0, N // CB)
    def _(cb):
        def lanes(h):
            return pl.ds(pl.multiple_of(cb * CB + h * 128, 128), 128)

        @pl.loop(0, 8)
        def _(i):
            b = pl.multiple_of(i * 16, 16)
            for h in range(CB // 128):
                hs = pl.ds(h * 128, 128)
                x = [tuple(a_ref[q, pl.ds(a * 128 + b, 16), lanes(h)] for q in range(2)) for a in range(8)]
                for c, (yr, yi) in enumerate(fft8(x, 1)):
                    if c > 0:
                        tr, ti = twr_ref[0, c, pl.ds(b, 16)], twr_ref[1, c, pl.ds(b, 16)]
                        yr, yi = yr * tr - yi * ti, yr * ti + yi * tr
                    (hr, lr), (hi, li) = split(yr), split(yi)
                    s2_ref[c, pl.ds(b, 16), hs] = hr
                    s2_ref[c, pl.ds(128 + b, 16), hs] = hi
                    s2_ref[c, pl.ds(256 + b, 16), hs] = lr
                    s2_ref[c, pl.ds(384 + b, 16), hs] = li

        wide = pl.ds(pl.multiple_of(cb * CB, CB), CB)
        for c in range(8):
            acc = dot(ri_ref[:, 0:512], s2_ref[c]) + dot(ri_ref[:, 512:768], s2_ref[c, 0:256])
            ir, ii = acc[0:128], acc[128:256]
            amp = amp_ref[pl.ds(c * 128, 128), wide].astype(F32)
            keep = 1.0 - amp * lax.rsqrt(jnp.maximum(ir * ir + ii * ii, FLOOR2))
            (hr, lr), (hi, li) = split(ir * keep), split(ii * keep)
            s3 = jnp.concatenate([hr, hi, lr, li], axis=0)
            acc = dot(rf_ref[:, 0:512], s3) + dot(rf_ref[:, 512:768], s3[0:256])
            z2_ref[c] = acc

        @pl.loop(0, 16)
        def _(i):
            b = pl.multiple_of(i * 8, 8)
            for h in range(CB // 128):
                hs = pl.ds(h * 128, 128)
                x = []
                for c in range(8):
                    zr, zi = z2_ref[c, pl.ds(b, 8), hs], z2_ref[c, pl.ds(128 + b, 8), hs]
                    if c > 0:
                        tr, ti = twr_ref[0, c, pl.ds(b, 8)], twr_ref[1, c, pl.ds(b, 8)]
                        zr, zi = zr * tr + zi * ti, zi * tr - zr * ti
                    x.append((zr, zi))
                for a, (yr, yi) in enumerate(fft8(x, -1)):
                    a_ref[0, pl.ds(a * 128 + b, 8), lanes(h)] = yr
                    a_ref[1, pl.ds(a * 128 + b, 8), lanes(h)] = yi

    back = jnp.bitwise_and(N - c0, N - 1)

    @pl.loop(0, N // RB)
    def _(rb):
        rows = pl.ds(pl.multiple_of(rb * RB, RB), RB)
        for c in range(8):
            (hr, lr), (hi, li) = split(a_ref[0, rows, lane_tile(c)]), split(a_ref[1, rows, lane_tile(c)])
            h = jnp.concatenate([hr, hi], axis=1)
            acc = dot(h, lf_ref[0:256]) + dot(jnp.concatenate([lr, li], axis=1), lf_ref[256:512])
            z_ref[c] = acc + dot(h, lf_ref[512:768])

        @pl.loop(0, RB // 16)
        def _(i):
            rows = pl.ds(pl.multiple_of(rb * RB + i * 16, 16), 16)
            sub = pl.ds(pl.multiple_of(i * 16, 16), 16)
            x = []
            for c in range(8):
                zr, zi = z_ref[c, sub, 0:128], z_ref[c, sub, 128:256]
                if c > 0:
                    tr, ti = twl_ref[0, c], twl_ref[1, c]
                    zr, zi = zr * tr + zi * ti, zi * tr - zr * ti
                x.append((zr, zi))
            for a, (sr, si) in enumerate(fft8(x, -1)):
                pr, pi = p_ref[0, rows, lane_tile(a)].astype(F32), p_ref[1, rows, lane_tile(a)].astype(F32)
                wr, wi = w_ref[0, rows, lane_tile(a)].astype(F32), w_ref[1, rows, lane_tile(a)].astype(F32)
                w_ref[0, rows, lane_tile(a)] = (pr * sr + pi * si).astype(BF16)
                w_ref[1, rows, lane_tile(a)] = (pr * si - pi * sr).astype(BF16)
                a_ref[0, rows, lane_tile(a)] = (wr * sr + wi * si) * (1.0 / 256)
                a_ref[1, rows, lane_tile(a)] = (wr * si - wi * sr) * (1.0 / 256)
            for q in range(2):
                a_ref[q, rows, :] = pltpu.roll(a_ref[q, rows, :], back, 1)

    @pl.loop(0, N // 16)
    def _(i):
        rows = pl.ds(pl.multiple_of(i * 16, 16), 16)
        for q in range(2):
            for a in range(2):
                x = w_ref[q, rows, lane_tile(a)].astype(F32)
                ahead = lane + 128 * a >= c0
                w_ref[q, rows, lane_tile(a)] = jnp.where(ahead, x, 0.0).astype(BF16)
                w_ref[q, rows, lane_tile(a + 8)] = jnp.where(ahead, 0.0, x).astype(BF16)

    @pl.loop(0, 16)
    def _(i):
        k = pl.multiple_of(i * 16, 16)
        for q in range(2):
            for a in range(10):
                x = w_ref[q, pl.ds(k, 16), lane_tile(a)].astype(F32)
                ahead = line + k >= r0
                w_ref[q, pl.ds(k, 16), lane_tile(a)] = jnp.where(ahead, x, 0.0).astype(BF16)
                w_ref[q, pl.ds(k + N, 16), lane_tile(a)] = jnp.where(ahead, 0.0, x).astype(BF16)

    results = (oc_ref, ol_ref, or_ref, ov_ref, ovl_ref, ovr_ref, oi_ref, oil_ref, oir_ref)
    stores = [pltpu.make_async_copy(x, y, out_sem.at[k]) for k, (x, y) in enumerate(zip(places, results))]
    for store in stores:
        store.start()

    a_ref[:, N:N + 256, :] = a_ref[:, 0:256, :]
    shift = jnp.bitwise_and(r0, 7)
    base = r0 - shift
    up = jnp.bitwise_and(8 - shift, 7)
    inside = lax.broadcasted_iota(jnp.int32, (8, N), 0) < 8 - shift
    for s, (out_ref, bit) in enumerate(((other_ref, 1 - core), (mine_ref, core))):
        @pl.loop(0, 8)
        def _(i):
            u = jnp.right_shift(i, 1) * 256 + bit * 128 + jnp.bitwise_and(i, 1) * 64
            start = pl.multiple_of(u + base, 8)
            for q in range(2):
                to = pl.multiple_of(q * 512 + i * 64, 64)
                turned = [pltpu.roll(a_ref[q, pl.ds(start + 8 * j, 8), :], up, 0) for j in range(9)]
                for j in range(8):
                    t_ref[s, pl.ds(to + 8 * j, 8), :] = jnp.where(inside, turned[j], turned[j + 1])

        store = pltpu.make_async_copy(t_ref.at[s], out_ref, out_sem.at[9 + s])
        store.start()
        stores.append(store)
    for store in stores:
        store.wait()


def led(pos, pieces, p, amp, tb):
    vm = pl.BlockSpec(memory_space=pltpu.VMEM)
    hbm = pl.BlockSpec(memory_space=pl.ANY)

    def rims(rows):
        return [jax.ShapeDtypeStruct((2, rows, cols), BF16) for cols in (TILE, RIM, RIM)]

    return pl.pallas_call(
        led_body,
        out_shape=rims(TILE) + rims(RIM) + rims(RIM) + [jax.ShapeDtypeStruct((N, N), F32)] * 2,
        in_specs=[pl.BlockSpec(memory_space=pltpu.SMEM)] + [hbm] * 11 + [vm] * 6,
        out_specs=[hbm] * 11,
        scratch_shapes=[
            pltpu.VMEM((2, REGION, REGION), BF16),
            pltpu.VMEM((2, N, N), BF16),
            pltpu.VMEM((N, N), BF16),
            pltpu.VMEM((2, N + 264, N), F32),
            pltpu.VMEM((8, RB, 512), BF16),
            pltpu.VMEM((8, 512, CB), BF16),
            pltpu.VMEM((8, RB, 256), F32),
            pltpu.VMEM((8, 256, CB), F32),
            pltpu.VMEM((2, N, N), F32),
            pltpu.SemaphoreType.DMA((11,)),
            pltpu.SemaphoreType.DMA((11,)),
        ],
        compiler_params=pltpu.CompilerParams(vmem_limit_bytes=60 * 2**20),
        cost_estimate=pl.CostEstimate(flops=13 * 10**9, bytes_accessed=30 * 2**20, transcendentals=N * N),
        name="led",
    )(pos, *pieces, p, amp, tb["lane_inv"], tb["lane_fwd"], tb["row_inv"], tb["row_fwd"], tb["tw_lane"], tb["tw_row"])


def turn_body(pos_ref, p_ref, po_ref, x_ref):
    r0, c0 = pos_ref[0], pos_ref[1]

    @pl.loop(0, N // 16)
    def _(i):
        u = pl.multiple_of(i * 16, 16)
        for q in range(2):
            x_ref[q, pl.ds(u + 256, 16), :] = pltpu.roll(p_ref[q, pl.ds(u, 16), :].astype(F32), c0, 1)

    x_ref[:, 0:256, :] = x_ref[:, N:N + 256, :]
    start = 256 - r0
    shift = jnp.bitwise_and(start, 7)
    base = start - shift
    up = jnp.bitwise_and(8 - shift, 7)
    inside = lax.broadcasted_iota(jnp.int32, (8, N), 0) < 8 - shift

    @pl.loop(0, N // 64)
    def _(i):
        u = pl.multiple_of(i * 64, 64)
        first = pl.multiple_of(u + base, 8)
        for q in range(2):
            turned = [pltpu.roll(x_ref[q, pl.ds(first + 8 * j, 8), :], up, 0) for j in range(9)]
            rows = [jnp.where(inside, turned[j], turned[j + 1]) for j in range(8)]
            po_ref[q, pl.ds(u, 64), :] = jnp.concatenate(rows, axis=0).astype(BF16)


def turn(pos, pupil):
    vm = pl.BlockSpec(memory_space=pltpu.VMEM)
    return pl.pallas_call(
        turn_body,
        out_shape=jax.ShapeDtypeStruct((2, N, N), BF16),
        in_specs=[pl.BlockSpec(memory_space=pltpu.SMEM), vm],
        out_specs=vm,
        scratch_shapes=[pltpu.VMEM((2, N + 264, N), F32)],
        compiler_params=pltpu.CompilerParams(vmem_limit_bytes=40 * 2**20),
        cost_estimate=pl.CostEstimate(flops=N**3, bytes_accessed=24 * 2**20, transcendentals=0),
        name="turn",
    )(pos, pupil)


def order_body(pos_ref, amp_ref, perm_ref, spec_ref, ao_ref, v_ref, vl_ref, vr_ref, i_ref, sem):
    core = pos_ref[2]
    gap = TILE - RIM
    outer = pl.multiple_of(core * gap, 128)
    inner = pl.multiple_of((1 - core) * gap, 128)
    ends = ((v_ref, outer, 0, TILE), (vl_ref, outer, gap, RIM), (vr_ref, outer, 0, RIM), (i_ref, inner, 0, TILE))
    copies = [
        pltpu.make_async_copy(spec_ref.at[:, pl.ds(row, RIM), pl.ds(col, wide)], out, sem.at[k])
        for k, (out, row, col, wide) in enumerate(ends)
    ]
    for copy in copies:
        copy.start()
    for i in range(4):
        part = dot(perm_ref[i * 256:(i + 1) * 256, :], amp_ref[...]).astype(BF16)
        part = lax.dot_general(part, perm_ref[...], (((1,), (1,)), ((), ())), preferred_element_type=F32)
        ao_ref[i * 256:(i + 1) * 256, :] = part.astype(BF16)
    for copy in copies:
        copy.wait()


def order(pos, amplitude, perm, spectrum):
    vm = pl.BlockSpec(memory_space=pltpu.VMEM)
    hbm = pl.BlockSpec(memory_space=pl.ANY)
    ends = [jax.ShapeDtypeStruct((2, RIM, wide), BF16) for wide in (TILE, RIM, RIM, TILE)]
    return pl.pallas_call(
        order_body,
        out_shape=[jax.ShapeDtypeStruct((N, N), BF16)] + ends,
        in_specs=[pl.BlockSpec(memory_space=pltpu.SMEM), vm, vm, hbm],
        out_specs=[vm] + [hbm] * 4,
        scratch_shapes=[pltpu.SemaphoreType.DMA((4,))],
        compiler_params=pltpu.CompilerParams(vmem_limit_bytes=40 * 2**20),
        cost_estimate=pl.CostEstimate(flops=4 * N**3, bytes_accessed=12 * 2**20, transcendentals=0),
        name="order",
    )(pos, amplitude, perm, spectrum)


def sides_body(pos_ref, l_ref, r_ref, il_ref, ir_ref, ol_ref, or_ref):
    at = (1 - pos_ref[2]) * (TILE - RIM)
    for mid_ref, add_ref, out_ref in ((l_ref, il_ref, ol_ref), (r_ref, ir_ref, or_ref)):
        out_ref[...] = mid_ref[...]

        @pl.loop(0, RIM // 32)
        def _(i):
            src = pl.ds(pl.multiple_of(i * 32, 32), 32)
            dst = pl.ds(pl.multiple_of(at + i * 32, 32), 32)
            for q in range(2):
                out_ref[q, dst, :] = (mid_ref[q, dst, :].astype(F32) + add_ref[q, src, :].astype(F32)).astype(BF16)


def sides(pos, l, r, il, ir):
    vm = pl.BlockSpec(memory_space=pltpu.VMEM)
    return pl.pallas_call(
        sides_body,
        out_shape=[jax.ShapeDtypeStruct(l.shape, BF16)] * 2,
        in_specs=[pl.BlockSpec(memory_space=pltpu.SMEM)] + [vm] * 4,
        out_specs=[vm] * 2,
        compiler_params=pltpu.CompilerParams(vmem_limit_bytes=32 * 2**20),
        cost_estimate=pl.CostEstimate(flops=2**20, bytes_accessed=6 * 2**20, transcendentals=0),
        name="sides",
    )(pos, l, r, il, ir)


def tile_body(pos_ref, c_ref, i_ref, v_ref, l_ref, r_ref, vl_ref, vr_ref, out_ref):
    core = pos_ref[2]
    gap = TILE - RIM
    out_ref[...] = c_ref[...].astype(F32)
    out_ref[0, :, gap:] += l_ref[0].astype(F32)
    out_ref[0, :, :RIM] += r_ref[0].astype(F32)
    at_i = (1 - core) * gap
    at_v = core * gap

    @pl.loop(0, RIM // 32)
    def _(i):
        src = pl.ds(pl.multiple_of(i * 32, 32), 32)
        out_ref[0, pl.ds(pl.multiple_of(at_i + i * 32, 32), 32), :] += i_ref[0, src, :].astype(F32)
        dst = pl.ds(pl.multiple_of(at_v + i * 32, 32), 32)
        out_ref[0, dst, :] += v_ref[0, src, :].astype(F32)
        out_ref[0, dst, gap:] += vl_ref[0, src, :].astype(F32)
        out_ref[0, dst, :RIM] += vr_ref[0, src, :].astype(F32)


def tile_sum(pos, parts):
    def block(x):
        return pl.BlockSpec((1,) + x.shape[1:], lambda q: (q, 0, 0))

    return pl.pallas_call(
        tile_body,
        grid=(2,),
        out_shape=jax.ShapeDtypeStruct((2, TILE, TILE), F32),
        in_specs=[pl.BlockSpec(memory_space=pltpu.SMEM)] + [block(x) for x in parts],
        out_specs=pl.BlockSpec((1, TILE, TILE), lambda q: (q, 0, 0)),
        compiler_params=pltpu.CompilerParams(vmem_limit_bytes=32 * 2**20),
        cost_estimate=pl.CostEstimate(flops=2**21, bytes_accessed=8 * 2**20, transcendentals=0),
        name="tile_sum",
    )(pos, *parts)


CUT = 640


def pair_body(mine_ref, other_ref, token_ref, a_ref, b_ref):
    total = mine_ref[...] + other_ref[...]
    a_ref[...] = total[:, :CUT].astype(BF16)
    for z in range(8):
        b_ref[z, 0] = total[z * 16:(z + 1) * 16, CUT:].astype(BF16)


def pair_sum(mine, other, token):
    rows = pl.BlockSpec((128, N), lambda i: (i, 0))
    return pl.pallas_call(
        pair_body,
        grid=(8,),
        out_shape=[jax.ShapeDtypeStruct((N, CUT), BF16), jax.ShapeDtypeStruct((8, 8, 16, N - CUT), BF16)],
        in_specs=[rows, rows, pl.BlockSpec(memory_space=pl.ANY)],
        out_specs=[pl.BlockSpec((128, CUT), lambda i: (i, 0)), pl.BlockSpec((8, 1, 16, N - CUT), lambda i: (0, i, 0, 0))],
        cost_estimate=pl.CostEstimate(flops=N * N, bytes_accessed=10 * 2**20, transcendentals=0),
        name="pair_sum",
    )(mine, other, token)


KY, KX = ("x", "yh", "core"), ("z", "yl")
ALL = KY + KX


def chain(n):
    up = [(i, i + 1) for i in range(n - 1)]
    return up, [(j, i) for i, j in up]


def between_chips(n):
    return [(i, i + 1) for i in range(1, n - 1, 2)] + [(i, i - 1) for i in range(2, n, 2)]


def both(rows, cols, n_cols):
    return [(a * n_cols + b, c * n_cols + d) for a, c in rows for b, d in cols]


def body(spectrum, pupil, amplitude, offsets):
    tb = {k: jnp.asarray(v) for k, v in tables().items()}
    n_ky, n_kx = lax.axis_size(KY), lax.axis_size(KX)
    iy, ix, core = lax.axis_index(KY), lax.axis_index(KX), lax.axis_index("core")
    first = core == 0
    r0 = offsets[0, 0, 0] - (iy * TILE - RIM)
    c0 = offsets[0, 0, 1] - (ix * TILE - RIM)
    pos = jnp.stack([r0, c0, core])
    right, left = chain(n_kx)
    vert = between_chips(n_ky)
    vert_l, vert_r = both(vert, left, n_kx), both(vert, right, n_kx)
    swap = [(0, 1), (1, 0)]

    in_l = lax.ppermute(spectrum[:, :, TILE - RIM:], KX, right)
    in_r = lax.ppermute(spectrum[:, :, :RIM], KX, left)
    amp, out_v, out_vl, out_vr, out_i = order(pos, amplitude, tb["perm"], spectrum)
    in_v = lax.ppermute(out_v, KY, vert)
    in_vl = lax.ppermute(out_vl, ALL, vert_r)
    in_vr = lax.ppermute(out_vr, ALL, vert_l)
    in_i = lax.ppermute(out_i, "core", swap)
    pupil = turn(pos, pupil)
    in_il = lax.ppermute(jnp.where(first, in_l[:, TILE - RIM:], in_l[:, :RIM]), "core", swap)
    in_ir = lax.ppermute(jnp.where(first, in_r[:, TILE - RIM:], in_r[:, :RIM]), "core", swap)
    pieces = (spectrum, in_l, in_r, in_v, in_vl, in_vr, in_i, in_il, in_ir)
    c, l, r, v, vl, vr, i, il, ir, mine, other = led(pos, pieces, pupil, amp, tb)

    il = lax.ppermute(il, "core", swap)
    ir = lax.ppermute(ir, "core", swap)
    v = lax.ppermute(v, KY, vert)
    vl = lax.ppermute(vl, ALL, vert_l)
    vr = lax.ppermute(vr, ALL, vert_r)
    i = lax.ppermute(i, "core", swap)
    other = lax.ppermute(other, "core", swap)
    l, r = sides(pos, l, r, il, ir)
    part_a, part_b = pair_sum(mine, other, l)
    l = lax.ppermute(l, KX, left)
    r = lax.ppermute(r, KX, right)

    part_a = lax.all_to_all(part_a.reshape(4, N // 4, CUT), "x", 0, 0)
    part_b = lax.all_to_all(part_b.reshape(8, N // 8, N - CUT), "z", 0, 0)
    part_a = jnp.sum(part_a.astype(F32), axis=0).reshape(2, 8, 16, CUT).transpose(1, 0, 2, 3).reshape(8, 32, CUT)
    part_b = jnp.sum(part_b.astype(F32), axis=0).reshape(4, 32, N - CUT)
    part_a = jnp.sum(lax.all_to_all(part_a, "z", 0, 0), axis=0)
    part_b = jnp.sum(lax.all_to_all(part_b, "x", 0, 0), axis=0)
    rest = jnp.concatenate([part_a, part_b], axis=1).reshape(4, 8, N)
    pupil_grad = jnp.sum(lax.all_to_all(rest, ("yh", "yl"), 0, 0), axis=0).reshape(-1)
    return tile_sum(pos, (c, i, v, l, r, vl, vr)), pupil_grad


def solution(mesh):
    fine = Mesh(mesh.devices.reshape(4, 2, 2, 8, 2), ALL)
    return jax.shard_map(
        body,
        mesh=fine,
        in_specs=(P(None, KY, KX), P(), P(KY, KX), P(KY, KX, None)),
        out_specs=(P(None, KY, KX), P(ALL)),
        check_vma=False,
    )
```

```python
import math

import jax
import jax.numpy as jnp
import ml_dtypes
import numpy as np
from jax import lax
from jax.experimental import pallas as pl
from jax.experimental.pallas import tpu as pltpu
from jax.sharding import Mesh
from jax.sharding import PartitionSpec as P

F32 = jnp.float32
BF16 = jnp.bfloat16
N = 1024
TILE = 512
RIM = 384
REGION = TILE + 2 * RIM
FLOOR2 = 0.0625


def split_np(t):
    hi = t.astype(np.float32).astype(ml_dtypes.bfloat16)
    lo = (t - hi.astype(np.float64)).astype(np.float32).astype(ml_dtypes.bfloat16)
    return hi, lo


def tables():
    b = np.arange(128)
    ang = 2.0 * np.pi / 128 * ((b[:, None] * b[None, :]) % 128)
    out = {}
    for name, sign in (("inv", 1.0), ("fwd", -1.0)):
        cr, ci = np.cos(ang) / 32.0, sign * np.sin(ang) / 32.0
        block = np.block([[cr, ci], [-ci, cr]])
        hi, lo = split_np(block)
        out["lane_" + name] = np.concatenate([hi, hi, lo], axis=0)
        out["row_" + name] = np.concatenate([hi.T, hi.T, lo.T], axis=1)
    tw = 2.0 * np.pi / N * (np.arange(8)[:, None] * b[None, :])
    tw = np.stack([np.cos(tw), np.sin(tw)]).astype(np.float32)
    out["tw_lane"] = tw.reshape(2, 8, 1, 128)
    out["tw_row"] = np.ascontiguousarray(np.broadcast_to(tw[:, :, :, None], (2, 8, 128, 128)))
    s = np.arange(N)
    perm = np.zeros((N, N), ml_dtypes.bfloat16)
    perm[s, (s // 128) + 8 * (s % 128)] = 1
    out["perm"] = perm
    return out


def cadd(p, q):
    return (p[0] + q[0], p[1] + q[1])


def csub(p, q):
    return (p[0] - q[0], p[1] - q[1])


def crot(p, sign):
    return (-p[1], p[0]) if sign > 0 else (p[1], -p[0])


def fft4(x0, x1, x2, x3, sign):
    t0, t1 = cadd(x0, x2), csub(x0, x2)
    t2, t3 = cadd(x1, x3), crot(csub(x1, x3), sign)
    return [cadd(t0, t2), cadd(t1, t3), csub(t0, t2), csub(t1, t3)]


def fft8(x, sign):
    even = fft4(x[0], x[2], x[4], x[6], sign)
    odd = fft4(x[1], x[3], x[5], x[7], sign)
    h = math.sqrt(0.5)
    r, i = odd[1]
    odd[1] = ((r - i) * h, (r + i) * h) if sign > 0 else ((r + i) * h, (i - r) * h)
    odd[2] = crot(odd[2], sign)
    r, i = odd[3]
    odd[3] = ((-r - i) * h, (r - i) * h) if sign > 0 else ((i - r) * h, (-r - i) * h)
    return [cadd(e, o) for e, o in zip(even, odd)] + [csub(e, o) for e, o in zip(even, odd)]


def split(x):
    hi = x.astype(BF16)
    return hi, (x - hi.astype(F32)).astype(BF16)


def dot(a, b):
    return jnp.dot(a, b, preferred_element_type=F32)


RB = 256
CB = 256


def led_body(
    pos_ref, own_ref, l_ref, r_ref, v_ref, vl_ref, vr_ref, i_ref, c_ref, pup_ref, ampl_ref,
    li_ref, lf_ref, ri_ref, rf_ref, twl_ref, twr_ref,
    oc_ref, ol_ref, or_ref, ov_ref, ovl_ref, ovr_ref, oi_ref, mine_ref, other_ref,
    w_ref, p_ref, amp_ref, a_ref, s_ref, s2_ref, z_ref, z2_ref, to_ref, tm_ref, in_sem, out_sem,
):
    r0, c0, core = pos_ref[0], pos_ref[1], pos_ref[2]
    outer = pl.multiple_of((RIM + TILE) * core, 128)
    inner = pl.multiple_of((RIM + TILE) * (1 - core), 128)
    places = []
    for start, count in ((RIM, TILE), (outer, RIM)):
        for col, wide in ((RIM, TILE), (0, RIM), (RIM + TILE, RIM)):
            places.append(w_ref.at[:, pl.ds(start, count), pl.ds(col, wide)])
    arrivals = [own_ref, l_ref, r_ref, v_ref, vl_ref, vr_ref]
    arrivals.append(i_ref.at[:, pl.ds(pl.multiple_of(core * (TILE - RIM), 128), RIM), :])
    arrivals += [c_ref.at[:, :, pl.ds(0, RIM)], c_ref.at[:, :, pl.ds(RIM, RIM)]]
    sides = [w_ref.at[:, pl.ds(inner, RIM), pl.ds(col, wide)] for col, wide in ((RIM, TILE), (0, RIM), (RIM + TILE, RIM))]
    loads = [pltpu.make_async_copy(x, y, in_sem.at[k]) for k, (x, y) in enumerate(zip(arrivals, places + sides))]
    places.append(w_ref.at[:, pl.ds(inner, RIM), :])
    loads.append(pltpu.make_async_copy(pup_ref, p_ref, in_sem.at[9]))
    amp_load = pltpu.make_async_copy(ampl_ref, amp_ref, in_sem.at[10])
    for load in loads:
        load.start()
    amp_load.start()

    def lane_tile(k):
        return pl.ds(k * 128, 128)

    lane = lax.broadcasted_iota(jnp.int32, (16, 128), 1)
    line = lax.broadcasted_iota(jnp.int32, (16, 128), 0)
    for load in loads:
        load.wait()

    @pl.loop(0, REGION // 16)
    def _(i):
        rows = pl.ds(pl.multiple_of(i * 16, 16), 16)
        for q in range(2):
            for a in range(2):
                here, there = w_ref[q, rows, lane_tile(a)].astype(F32), w_ref[q, rows, lane_tile(a + 8)].astype(F32)
                w_ref[q, rows, lane_tile(a)] = jnp.where(lane + 128 * a >= c0, here, there).astype(BF16)

    @pl.loop(0, 16)
    def _(i):
        k = pl.multiple_of(i * 16, 16)
        for q in range(2):
            for a in range(8):
                here = w_ref[q, pl.ds(k, 16), lane_tile(a)].astype(F32)
                there = w_ref[q, pl.ds(k + N, 16), lane_tile(a)].astype(F32)
                w_ref[q, pl.ds(k, 16), lane_tile(a)] = jnp.where(line + k >= r0, here, there).astype(BF16)

    @pl.loop(0, N // RB)
    def _(rb):
        @pl.loop(0, RB // 16)
        def _(i):
            rows = pl.ds(pl.multiple_of(rb * RB + i * 16, 16), 16)
            sub = pl.ds(pl.multiple_of(i * 16, 16), 16)
            x = []
            for a in range(8):
                pr, pi = p_ref[0, rows, lane_tile(a)].astype(F32), p_ref[1, rows, lane_tile(a)].astype(F32)
                wr, wi = w_ref[0, rows, lane_tile(a)].astype(F32), w_ref[1, rows, lane_tile(a)].astype(F32)
                x.append((pr * wr - pi * wi, pr * wi + pi * wr))
            for c, (yr, yi) in enumerate(fft8(x, 1)):
                if c > 0:
                    tr, ti = twl_ref[0, c], twl_ref[1, c]
                    yr, yi = yr * tr - yi * ti, yr * ti + yi * tr
                (hr, lr), (hi, li) = split(yr), split(yi)
                s_ref[c, sub, 0:128] = hr
                s_ref[c, sub, 128:256] = hi
                s_ref[c, sub, 256:384] = lr
                s_ref[c, sub, 384:512] = li

        rows = pl.ds(pl.multiple_of(rb * RB, RB), RB)
        for c in range(8):
            acc = dot(s_ref[c], li_ref[0:512]) + dot(s_ref[c, :, 0:256], li_ref[512:768])
            a_ref[0, rows, lane_tile(c)] = acc[:, 0:128]
            a_ref[1, rows, lane_tile(c)] = acc[:, 128:256]

    amp_load.wait()

    @pl.loop(0, N // CB)
    def _(cb):
        def lanes(h):
            return pl.ds(pl.multiple_of(cb * CB + h * 128, 128), 128)

        @pl.loop(0, 8)
        def _(i):
            b = pl.multiple_of(i * 16, 16)
            for h in range(CB // 128):
                hs = pl.ds(h * 128, 128)
                x = [tuple(a_ref[q, pl.ds(a * 128 + b, 16), lanes(h)] for q in range(2)) for a in range(8)]
                for c, (yr, yi) in enumerate(fft8(x, 1)):
                    if c > 0:
                        tr, ti = twr_ref[0, c, pl.ds(b, 16)], twr_ref[1, c, pl.ds(b, 16)]
                        yr, yi = yr * tr - yi * ti, yr * ti + yi * tr
                    (hr, lr), (hi, li) = split(yr), split(yi)
                    s2_ref[c, pl.ds(b, 16), hs] = hr
                    s2_ref[c, pl.ds(128 + b, 16), hs] = hi
                    s2_ref[c, pl.ds(256 + b, 16), hs] = lr
                    s2_ref[c, pl.ds(384 + b, 16), hs] = li

        wide = pl.ds(pl.multiple_of(cb * CB, CB), CB)
        for c in range(8):
            acc = dot(ri_ref[:, 0:512], s2_ref[c]) + dot(ri_ref[:, 512:768], s2_ref[c, 0:256])
            ir, ii = acc[0:128], acc[128:256]
            amp = amp_ref[pl.ds(c * 128, 128), wide].astype(F32)
            keep = 1.0 - amp * lax.rsqrt(jnp.maximum(ir * ir + ii * ii, FLOOR2))
            (hr, lr), (hi, li) = split(ir * keep), split(ii * keep)
            s3 = jnp.concatenate([hr, hi, lr, li], axis=0)
            acc = dot(rf_ref[:, 0:512], s3) + dot(rf_ref[:, 512:768], s3[0:256])
            z2_ref[c] = acc

        @pl.loop(0, 16)
        def _(i):
            b = pl.multiple_of(i * 8, 8)
            for h in range(CB // 128):
                hs = pl.ds(h * 128, 128)
                x = []
                for c in range(8):
                    zr, zi = z2_ref[c, pl.ds(b, 8), hs], z2_ref[c, pl.ds(128 + b, 8), hs]
                    if c > 0:
                        tr, ti = twr_ref[0, c, pl.ds(b, 8)], twr_ref[1, c, pl.ds(b, 8)]
                        zr, zi = zr * tr + zi * ti, zi * tr - zr * ti
                    x.append((zr, zi))
                for a, (yr, yi) in enumerate(fft8(x, -1)):
                    a_ref[0, pl.ds(a * 128 + b, 8), lanes(h)] = yr
                    a_ref[1, pl.ds(a * 128 + b, 8), lanes(h)] = yi

    back = jnp.bitwise_and(N - c0, N - 1)

    @pl.loop(0, N // RB)
    def _(rb):
        rows = pl.ds(pl.multiple_of(rb * RB, RB), RB)
        for c in range(8):
            (hr, lr), (hi, li) = split(a_ref[0, rows, lane_tile(c)]), split(a_ref[1, rows, lane_tile(c)])
            h = jnp.concatenate([hr, hi], axis=1)
            acc = dot(h, lf_ref[0:256]) + dot(jnp.concatenate([lr, li], axis=1), lf_ref[256:512])
            z_ref[c] = acc + dot(h, lf_ref[512:768])

        @pl.loop(0, RB // 16)
        def _(i):
            rows = pl.ds(pl.multiple_of(rb * RB + i * 16, 16), 16)
            sub = pl.ds(pl.multiple_of(i * 16, 16), 16)
            x = []
            for c in range(8):
                zr, zi = z_ref[c, sub, 0:128], z_ref[c, sub, 128:256]
                if c > 0:
                    tr, ti = twl_ref[0, c], twl_ref[1, c]
                    zr, zi = zr * tr + zi * ti, zi * tr - zr * ti
                x.append((zr, zi))
            for a, (sr, si) in enumerate(fft8(x, -1)):
                pr, pi = p_ref[0, rows, lane_tile(a)].astype(F32), p_ref[1, rows, lane_tile(a)].astype(F32)
                wr, wi = w_ref[0, rows, lane_tile(a)].astype(F32), w_ref[1, rows, lane_tile(a)].astype(F32)
                w_ref[0, rows, lane_tile(a)] = (pr * sr + pi * si).astype(BF16)
                w_ref[1, rows, lane_tile(a)] = (pr * si - pi * sr).astype(BF16)
                a_ref[0, rows, lane_tile(a)] = (wr * sr + wi * si) * (1.0 / 256)
                a_ref[1, rows, lane_tile(a)] = (wr * si - wi * sr) * (1.0 / 256)
            for q in range(2):
                a_ref[q, rows, :] = pltpu.roll(a_ref[q, rows, :], back, 1)

    @pl.loop(0, N // 16)
    def _(i):
        rows = pl.ds(pl.multiple_of(i * 16, 16), 16)
        for q in range(2):
            for a in range(2):
                x = w_ref[q, rows, lane_tile(a)].astype(F32)
                ahead = lane + 128 * a >= c0
                w_ref[q, rows, lane_tile(a)] = jnp.where(ahead, x, 0.0).astype(BF16)
                w_ref[q, rows, lane_tile(a + 8)] = jnp.where(ahead, 0.0, x).astype(BF16)

    @pl.loop(0, 16)
    def _(i):
        k = pl.multiple_of(i * 16, 16)
        for q in range(2):
            for a in range(10):
                x = w_ref[q, pl.ds(k, 16), lane_tile(a)].astype(F32)
                ahead = line + k >= r0
                w_ref[q, pl.ds(k, 16), lane_tile(a)] = jnp.where(ahead, x, 0.0).astype(BF16)
                w_ref[q, pl.ds(k + N, 16), lane_tile(a)] = jnp.where(ahead, 0.0, x).astype(BF16)

    results = (oc_ref, ol_ref, or_ref, ov_ref, ovl_ref, ovr_ref, oi_ref)
    stores = [pltpu.make_async_copy(x, y, out_sem.at[k]) for k, (x, y) in enumerate(zip(places, results))]
    for store in stores:
        store.start()

    a_ref[:, N:N + 256, :] = a_ref[:, 0:256, :]
    shift = jnp.bitwise_and(r0, 7)
    base = r0 - shift
    up = jnp.bitwise_and(8 - shift, 7)
    inside = lax.broadcasted_iota(jnp.int32, (8, N), 0) < 8 - shift
    for s, (out_ref, t_ref, bit) in enumerate(((other_ref, to_ref, 1 - core), (mine_ref, tm_ref, core))):
        @pl.loop(0, 8)
        def _(i):
            u = jnp.right_shift(i, 1) * 256 + bit * 128 + jnp.bitwise_and(i, 1) * 64
            start = pl.multiple_of(u + base, 8)
            for q in range(2):
                to = pl.multiple_of(q * 512 + i * 64, 64)
                turned = [pltpu.roll(a_ref[q, pl.ds(start + 8 * j, 8), :], up, 0) for j in range(9)]
                lines = [jnp.where(inside, turned[j], turned[j + 1]) for j in range(8)]
                for j in range(0, 8, 2):
                    t_ref[pl.ds(to + 8 * j, 16), :] = jnp.concatenate(lines[j:j + 2], axis=0).astype(t_ref.dtype)

        store = pltpu.make_async_copy(t_ref, out_ref, out_sem.at[7 + s])
        store.start()
        stores.append(store)
    for store in stores:
        store.wait()


def led(pos, pieces, p, amp, tb):
    vm = pl.BlockSpec(memory_space=pltpu.VMEM)
    hbm = pl.BlockSpec(memory_space=pl.ANY)

    def rims(rows):
        return [jax.ShapeDtypeStruct((2, rows, cols), BF16) for cols in (TILE, RIM, RIM)]

    return pl.pallas_call(
        led_body,
        out_shape=rims(TILE) + rims(RIM) + [jax.ShapeDtypeStruct((2, RIM, REGION), BF16)]
        + [jax.ShapeDtypeStruct((N, N), F32), jax.ShapeDtypeStruct((N, N), BF16)],
        in_specs=[pl.BlockSpec(memory_space=pltpu.SMEM)] + [hbm] * 10 + [vm] * 6,
        out_specs=[hbm] * 9,
        scratch_shapes=[
            pltpu.VMEM((2, REGION, REGION), BF16),
            pltpu.VMEM((2, N, N), BF16),
            pltpu.VMEM((N, N), BF16),
            pltpu.VMEM((2, N + 264, N), F32),
            pltpu.VMEM((8, RB, 512), BF16),
            pltpu.VMEM((8, 512, CB), BF16),
            pltpu.VMEM((8, RB, 256), F32),
            pltpu.VMEM((8, 256, CB), F32),
            pltpu.VMEM((N, N), BF16),
            pltpu.VMEM((N, N), F32),
            pltpu.SemaphoreType.DMA((11,)),
            pltpu.SemaphoreType.DMA((9,)),
        ],
        compiler_params=pltpu.CompilerParams(vmem_limit_bytes=60 * 2**20),
        cost_estimate=pl.CostEstimate(flops=13 * 10**9, bytes_accessed=30 * 2**20, transcendentals=N * N),
        name="led",
    )(pos, *pieces, p, amp, tb["lane_inv"], tb["lane_fwd"], tb["row_inv"], tb["row_fwd"], tb["tw_lane"], tb["tw_row"])


def turn_body(pos_ref, p_ref, token_ref, po_ref, x_ref):
    r0, c0 = pos_ref[0], pos_ref[1]

    @pl.loop(0, N // 16)
    def _(i):
        u = pl.multiple_of(i * 16, 16)
        for q in range(2):
            x_ref[q, pl.ds(u + 256, 16), :] = pltpu.roll(p_ref[q, pl.ds(u, 16), :].astype(F32), c0, 1)

    x_ref[:, 0:256, :] = x_ref[:, N:N + 256, :]
    start = 256 - r0
    shift = jnp.bitwise_and(start, 7)
    base = start - shift
    up = jnp.bitwise_and(8 - shift, 7)
    inside = lax.broadcasted_iota(jnp.int32, (8, N), 0) < 8 - shift

    @pl.loop(0, N // 64)
    def _(i):
        u = pl.multiple_of(i * 64, 64)
        first = pl.multiple_of(u + base, 8)
        for q in range(2):
            turned = [pltpu.roll(x_ref[q, pl.ds(first + 8 * j, 8), :], up, 0) for j in range(9)]
            rows = [jnp.where(inside, turned[j], turned[j + 1]) for j in range(8)]
            po_ref[q, pl.ds(u, 64), :] = jnp.concatenate(rows, axis=0).astype(BF16)


def turn(pos, pupil, token):
    vm = pl.BlockSpec(memory_space=pltpu.VMEM)
    return pl.pallas_call(
        turn_body,
        out_shape=jax.ShapeDtypeStruct((2, N, N), BF16),
        in_specs=[pl.BlockSpec(memory_space=pltpu.SMEM), vm, pl.BlockSpec(memory_space=pl.ANY)],
        out_specs=vm,
        scratch_shapes=[pltpu.VMEM((2, N + 264, N), F32)],
        compiler_params=pltpu.CompilerParams(vmem_limit_bytes=40 * 2**20),
        cost_estimate=pl.CostEstimate(flops=N**3, bytes_accessed=24 * 2**20, transcendentals=0),
        name="turn",
    )(pos, pupil, token)


def order_body(pos_ref, amp_ref, perm_ref, spec_ref, ao_ref, v_ref, vl_ref, vr_ref):
    core = pos_ref[2]
    gap = TILE - RIM
    outer = pl.multiple_of(core * gap, 128)
    ends = ((v_ref, outer, 0, TILE), (vl_ref, outer, gap, RIM), (vr_ref, outer, 0, RIM))
    for out, row, col, wide in ends:
        @pl.loop(0, RIM // 32)
        def _(i):
            src = pl.ds(pl.multiple_of(row + i * 32, 32), 32)
            for q in range(2):
                out[q, pl.ds(pl.multiple_of(i * 32, 32), 32), :] = spec_ref[q, src, col:col + wide]

    for i in range(4):
        part = dot(perm_ref[i * 256:(i + 1) * 256, :], amp_ref[...]).astype(BF16)
        part = lax.dot_general(part, perm_ref[...], (((1,), (1,)), ((), ())), preferred_element_type=F32)
        ao_ref[i * 256:(i + 1) * 256, :] = part.astype(BF16)


def order(pos, amplitude, perm, spectrum):
    vm = pl.BlockSpec(memory_space=pltpu.VMEM)
    ends = [jax.ShapeDtypeStruct((2, RIM, wide), BF16) for wide in (TILE, RIM, RIM)]
    return pl.pallas_call(
        order_body,
        out_shape=[jax.ShapeDtypeStruct((N, N), BF16)] + ends,
        in_specs=[pl.BlockSpec(memory_space=pltpu.SMEM), vm, vm, vm],
        out_specs=[vm] * 4,
        compiler_params=pltpu.CompilerParams(vmem_limit_bytes=40 * 2**20),
        cost_estimate=pl.CostEstimate(flops=4 * N**3, bytes_accessed=12 * 2**20, transcendentals=0),
        name="order",
    )(pos, amplitude, perm, spectrum)


def cut_body(pos_ref, l_ref, r_ref, token_ref, out_ref):
    row = (1 - pos_ref[2]) * (TILE - RIM)

    @pl.loop(0, RIM // 32)
    def _(i):
        dst = pl.ds(pl.multiple_of(i * 32, 32), 32)
        src = pl.ds(pl.multiple_of(row + i * 32, 32), 32)
        for q in range(2):
            out_ref[q, dst, 0:RIM] = l_ref[q, src, :]
            out_ref[q, dst, RIM:2 * RIM] = r_ref[q, src, :]


def cut(pos, l, r, token):
    vm = pl.BlockSpec(memory_space=pltpu.VMEM)
    return pl.pallas_call(
        cut_body,
        out_shape=jax.ShapeDtypeStruct((2, RIM, 2 * RIM), BF16),
        in_specs=[pl.BlockSpec(memory_space=pltpu.SMEM), vm, vm, pl.BlockSpec(memory_space=pl.ANY)],
        out_specs=vm,
        cost_estimate=pl.CostEstimate(flops=0, bytes_accessed=4 * 2**20, transcendentals=0),
        name="cut",
    )(pos, l, r, token)


def sides_body(pos_ref, l_ref, r_ref, i_ref, first_ref, second_ref, ol_ref, or_ref):
    at = (1 - pos_ref[2]) * (TILE - RIM)
    for mid_ref, col, out_ref in ((l_ref, 0, ol_ref), (r_ref, RIM + TILE, or_ref)):
        out_ref[...] = mid_ref[...]

        @pl.loop(0, RIM // 32)
        def _(i):
            src = pl.ds(pl.multiple_of(i * 32, 32), 32)
            dst = pl.ds(pl.multiple_of(at + i * 32, 32), 32)
            for q in range(2):
                add = i_ref[q, src, col:col + RIM].astype(F32)
                out_ref[q, dst, :] = (mid_ref[q, dst, :].astype(F32) + add).astype(BF16)


def sides(pos, l, r, i, first, second):
    vm = pl.BlockSpec(memory_space=pltpu.VMEM)
    return pl.pallas_call(
        sides_body,
        out_shape=[jax.ShapeDtypeStruct(l.shape, BF16)] * 2,
        in_specs=[pl.BlockSpec(memory_space=pltpu.SMEM)] + [vm] * 3 + [pl.BlockSpec(memory_space=pl.ANY)] * 2,
        out_specs=[vm] * 2,
        compiler_params=pltpu.CompilerParams(vmem_limit_bytes=32 * 2**20),
        cost_estimate=pl.CostEstimate(flops=2**20, bytes_accessed=6 * 2**20, transcendentals=0),
        name="sides",
    )(pos, l, r, i, first, second)


def tile_body(pos_ref, c_ref, i_ref, v_ref, l_ref, r_ref, vl_ref, vr_ref, out_ref):
    core = pos_ref[2]
    gap = TILE - RIM
    out_ref[...] = c_ref[...].astype(F32)
    out_ref[0, :, gap:] += l_ref[0].astype(F32)
    out_ref[0, :, :RIM] += r_ref[0].astype(F32)
    at_i = (1 - core) * gap
    at_v = core * gap

    @pl.loop(0, RIM // 32)
    def _(i):
        src = pl.ds(pl.multiple_of(i * 32, 32), 32)
        out_ref[0, pl.ds(pl.multiple_of(at_i + i * 32, 32), 32), :] += i_ref[0, src, RIM:RIM + TILE].astype(F32)
        dst = pl.ds(pl.multiple_of(at_v + i * 32, 32), 32)
        out_ref[0, dst, :] += v_ref[0, src, :].astype(F32)
        out_ref[0, dst, gap:] += vl_ref[0, src, :].astype(F32)
        out_ref[0, dst, :RIM] += vr_ref[0, src, :].astype(F32)


def tile_sum(pos, parts):
    def block(x):
        return pl.BlockSpec((1,) + x.shape[1:], lambda q: (q, 0, 0))

    return pl.pallas_call(
        tile_body,
        grid=(2,),
        out_shape=jax.ShapeDtypeStruct((2, TILE, TILE), F32),
        in_specs=[pl.BlockSpec(memory_space=pltpu.SMEM)] + [block(x) for x in parts],
        out_specs=pl.BlockSpec((1, TILE, TILE), lambda q: (q, 0, 0)),
        compiler_params=pltpu.CompilerParams(vmem_limit_bytes=32 * 2**20),
        cost_estimate=pl.CostEstimate(flops=2**21, bytes_accessed=8 * 2**20, transcendentals=0),
        name="tile_sum",
    )(pos, *parts)


def pair_body(mine_ref, other_ref, out_ref):
    for z in range(8):
        rows = pl.ds(z * 16, 16)
        out_ref[z, 0] = mine_ref[rows, :] + other_ref[rows, :].astype(F32)


def pair_sum(mine, other):
    rows = pl.BlockSpec((128, N), lambda i: (i, 0))
    return pl.pallas_call(
        pair_body,
        grid=(8,),
        out_shape=jax.ShapeDtypeStruct((8, 8, 16, N), F32),
        in_specs=[rows, rows],
        out_specs=pl.BlockSpec((8, 1, 16, N), lambda i: (0, i, 0, 0)),
        cost_estimate=pl.CostEstimate(flops=N * N, bytes_accessed=12 * 2**20, transcendentals=0),
        name="pair_sum",
    )(mine, other)


def after_body(x_ref, token_ref, out_ref):
    out_ref[...] = x_ref[...]


def after(x, token):
    vm = pl.BlockSpec(memory_space=pltpu.VMEM)
    return pl.pallas_call(
        after_body,
        out_shape=jax.ShapeDtypeStruct(x.shape, x.dtype),
        in_specs=[vm, pl.BlockSpec(memory_space=pl.ANY)],
        out_specs=vm,
        cost_estimate=pl.CostEstimate(flops=0, bytes_accessed=2**20, transcendentals=0),
        name="after",
    )(x, token)


KY, KX = ("x", "yh", "core"), ("z", "yl")
ALL = KY + KX


def chain(n):
    up = [(i, i + 1) for i in range(n - 1)]
    return up, [(j, i) for i, j in up]


def between_chips(n):
    return [(i, i + 1) for i in range(1, n - 1, 2)] + [(i, i - 1) for i in range(2, n, 2)]


def both(rows, cols, n_cols):
    return [(a * n_cols + b, c * n_cols + d) for a, c in rows for b, d in cols]


def body(spectrum, pupil, amplitude, offsets):
    tb = {k: jnp.asarray(v) for k, v in tables().items()}
    n_ky, n_kx = lax.axis_size(KY), lax.axis_size(KX)
    iy, ix, core = lax.axis_index(KY), lax.axis_index(KX), lax.axis_index("core")
    first = core == 0
    r0 = offsets[0, 0, 0] - (iy * TILE - RIM)
    c0 = offsets[0, 0, 1] - (ix * TILE - RIM)
    pos = jnp.stack([r0, c0, core])
    right, left = chain(n_kx)
    vert = between_chips(n_ky)
    vert_l, vert_r = both(vert, left, n_kx), both(vert, right, n_kx)
    swap = [(0, 1), (1, 0)]

    in_l = lax.ppermute(spectrum[:, :, TILE - RIM:], KX, right)
    in_r = lax.ppermute(spectrum[:, :, :RIM], KX, left)
    amp, out_v, out_vl, out_vr = order(pos, amplitude, tb["perm"], spectrum)
    in_v = lax.ppermute(out_v, KY, vert)
    in_vl = lax.ppermute(out_vl, ALL, vert_r)
    in_vr = lax.ppermute(out_vr, ALL, vert_l)
    in_i = lax.ppermute(spectrum, "core", swap)
    pupil = turn(pos, pupil, out_v)
    in_c = lax.ppermute(cut(pos, in_l, in_r, pupil), "core", swap)
    pieces = (spectrum, in_l, in_r, in_v, in_vl, in_vr, in_i, in_c)
    c, l, r, v, vl, vr, i, mine, other = led(pos, pieces, pupil, amp, tb)

    i = lax.ppermute(i, "core", swap)
    v = lax.ppermute(v, KY, vert)
    vl = lax.ppermute(vl, ALL, vert_l)
    vr = lax.ppermute(vr, ALL, vert_r)
    total = pair_sum(mine, lax.ppermute(other, "core", swap))
    l, r = sides(pos, l, r, i, total, v)
    l = lax.ppermute(l, KX, left)
    r = lax.ppermute(r, KX, right)
    tile = tile_sum(pos, (c, i, v, l, r, vl, vr))
    total = lax.psum_scatter(total.reshape(8, 128, N), "z", scatter_dimension=0, tiled=True).reshape(16, 8, N)
    total = lax.all_to_all(after(total, tile), ("x", "yh", "yl"), 0, 0)
    return tile, jnp.sum(total, axis=0).reshape(-1)


def solution(mesh):
    fine = Mesh(mesh.devices.reshape(4, 2, 2, 8, 2), ALL)
    return jax.shard_map(
        body,
        mesh=fine,
        in_specs=(P(None, KY, KX), P(), P(KY, KX), P(KY, KX, None)),
        out_specs=(P(None, KY, KX), P(ALL)),
        check_vma=False,
    )
```

```python
import math

import jax
import jax.numpy as jnp
import ml_dtypes
import numpy as np
from jax import lax
from jax.experimental import pallas as pl
from jax.experimental.pallas import tpu as pltpu
from jax.sharding import Mesh
from jax.sharding import PartitionSpec as P

F32 = jnp.float32
BF16 = jnp.bfloat16
N = 1024
TILE = 512
RIM = 384
REGION = TILE + 2 * RIM
FLOOR2 = 0.0625
FREE = pl.CostEstimate(flops=1, bytes_accessed=1, transcendentals=0)


def split_np(t):
    hi = t.astype(np.float32).astype(ml_dtypes.bfloat16)
    lo = (t - hi.astype(np.float64)).astype(np.float32).astype(ml_dtypes.bfloat16)
    return hi, lo


def tables():
    b = np.arange(128)
    ang = 2.0 * np.pi / 128 * ((b[:, None] * b[None, :]) % 128)
    out = {}
    for name, sign in (("inv", 1.0), ("fwd", -1.0)):
        cr, ci = np.cos(ang) / 32.0, sign * np.sin(ang) / 32.0
        block = np.block([[cr, ci], [-ci, cr]])
        hi, lo = split_np(block)
        out["lane_" + name] = np.concatenate([hi, hi, lo], axis=0)
        out["row_" + name] = np.concatenate([hi.T, hi.T, lo.T], axis=1)
    tw = 2.0 * np.pi / N * (np.arange(8)[:, None] * b[None, :])
    tw = np.stack([np.cos(tw), np.sin(tw)]).astype(np.float32)
    out["tw_lane"] = tw.reshape(2, 8, 1, 128)
    out["tw_row"] = np.ascontiguousarray(np.broadcast_to(tw[:, :, :, None], (2, 8, 128, 128)))
    s = np.arange(N)
    perm = np.zeros((N, N), ml_dtypes.bfloat16)
    perm[s, (s // 128) + 8 * (s % 128)] = 1
    out["perm"] = perm
    return out


def cadd(p, q):
    return (p[0] + q[0], p[1] + q[1])


def csub(p, q):
    return (p[0] - q[0], p[1] - q[1])


def crot(p, sign):
    return (-p[1], p[0]) if sign > 0 else (p[1], -p[0])


def fft4(x0, x1, x2, x3, sign):
    t0, t1 = cadd(x0, x2), csub(x0, x2)
    t2, t3 = cadd(x1, x3), crot(csub(x1, x3), sign)
    return [cadd(t0, t2), cadd(t1, t3), csub(t0, t2), csub(t1, t3)]


def fft8(x, sign):
    even = fft4(x[0], x[2], x[4], x[6], sign)
    odd = fft4(x[1], x[3], x[5], x[7], sign)
    h = math.sqrt(0.5)
    r, i = odd[1]
    odd[1] = ((r - i) * h, (r + i) * h) if sign > 0 else ((r + i) * h, (i - r) * h)
    odd[2] = crot(odd[2], sign)
    r, i = odd[3]
    odd[3] = ((-r - i) * h, (r - i) * h) if sign > 0 else ((i - r) * h, (-r - i) * h)
    return [cadd(e, o) for e, o in zip(even, odd)] + [csub(e, o) for e, o in zip(even, odd)]


def split(x):
    hi = x.astype(BF16)
    return hi, (x - hi.astype(F32)).astype(BF16)


def dot(a, b):
    return jnp.dot(a, b, preferred_element_type=F32)


RB = 256
CB = 256


def led_body(
    pos_ref, own_ref, l_ref, r_ref, v_ref, vl_ref, vr_ref, i_ref, c_ref, pup_ref, ampl_ref,
    li_ref, lf_ref, ri_ref, rf_ref, twl_ref, twr_ref,
    oc_ref, ol_ref, or_ref, ov_ref, ovl_ref, ovr_ref, oi_ref, mine_ref, other_ref,
    w_ref, p_ref, amp_ref, a_ref, s_ref, s2_ref, z_ref, z2_ref, to_ref, tm_ref, in_sem, out_sem,
):
    r0, c0, core = pos_ref[0], pos_ref[1], pos_ref[2]
    outer = pl.multiple_of((RIM + TILE) * core, 128)
    inner = pl.multiple_of((RIM + TILE) * (1 - core), 128)
    places = []
    for start, count in ((RIM, TILE), (outer, RIM)):
        for col, wide in ((RIM, TILE), (0, RIM), (RIM + TILE, RIM)):
            places.append(w_ref.at[:, pl.ds(start, count), pl.ds(col, wide)])
    arrivals = [own_ref, l_ref, r_ref, v_ref, vl_ref, vr_ref]
    arrivals.append(i_ref.at[:, pl.ds(pl.multiple_of(core * (TILE - RIM), 128), RIM), :])
    arrivals += [c_ref.at[:, :, pl.ds(0, RIM)], c_ref.at[:, :, pl.ds(RIM, RIM)]]
    sides = [w_ref.at[:, pl.ds(inner, RIM), pl.ds(col, wide)] for col, wide in ((RIM, TILE), (0, RIM), (RIM + TILE, RIM))]
    loads = [pltpu.make_async_copy(x, y, in_sem.at[k]) for k, (x, y) in enumerate(zip(arrivals, places + sides))]
    places.append(w_ref.at[:, pl.ds(inner, RIM), :])
    loads.append(pltpu.make_async_copy(pup_ref, p_ref, in_sem.at[9]))
    amp_load = pltpu.make_async_copy(ampl_ref, amp_ref, in_sem.at[10])
    for load in loads:
        load.start()
    amp_load.start()

    def lane_tile(k):
        return pl.ds(k * 128, 128)

    lane = lax.broadcasted_iota(jnp.int32, (16, 128), 1)
    line = lax.broadcasted_iota(jnp.int32, (16, 128), 0)
    for load in loads:
        load.wait()

    @pl.loop(0, REGION // 16)
    def _(i):
        rows = pl.ds(pl.multiple_of(i * 16, 16), 16)
        for q in range(2):
            for a in range(2):
                here, there = w_ref[q, rows, lane_tile(a)].astype(F32), w_ref[q, rows, lane_tile(a + 8)].astype(F32)
                w_ref[q, rows, lane_tile(a)] = jnp.where(lane + 128 * a >= c0, here, there).astype(BF16)

    @pl.loop(0, 16)
    def _(i):
        k = pl.multiple_of(i * 16, 16)
        for q in range(2):
            for a in range(8):
                here = w_ref[q, pl.ds(k, 16), lane_tile(a)].astype(F32)
                there = w_ref[q, pl.ds(k + N, 16), lane_tile(a)].astype(F32)
                w_ref[q, pl.ds(k, 16), lane_tile(a)] = jnp.where(line + k >= r0, here, there).astype(BF16)

    @pl.loop(0, N // RB)
    def _(rb):
        @pl.loop(0, RB // 16)
        def _(i):
            rows = pl.ds(pl.multiple_of(rb * RB + i * 16, 16), 16)
            sub = pl.ds(pl.multiple_of(i * 16, 16), 16)
            x = []
            for a in range(8):
                pr, pi = p_ref[0, rows, lane_tile(a)].astype(F32), p_ref[1, rows, lane_tile(a)].astype(F32)
                wr, wi = w_ref[0, rows, lane_tile(a)].astype(F32), w_ref[1, rows, lane_tile(a)].astype(F32)
                x.append((pr * wr - pi * wi, pr * wi + pi * wr))
            for c, (yr, yi) in enumerate(fft8(x, 1)):
                if c > 0:
                    tr, ti = twl_ref[0, c], twl_ref[1, c]
                    yr, yi = yr * tr - yi * ti, yr * ti + yi * tr
                (hr, lr), (hi, li) = split(yr), split(yi)
                s_ref[c, sub, 0:128] = hr
                s_ref[c, sub, 128:256] = hi
                s_ref[c, sub, 256:384] = lr
                s_ref[c, sub, 384:512] = li

        rows = pl.ds(pl.multiple_of(rb * RB, RB), RB)
        for c in range(8):
            acc = dot(s_ref[c], li_ref[0:512]) + dot(s_ref[c, :, 0:256], li_ref[512:768])
            a_ref[0, rows, lane_tile(c)] = acc[:, 0:128]
            a_ref[1, rows, lane_tile(c)] = acc[:, 128:256]

    amp_load.wait()

    @pl.loop(0, N // CB)
    def _(cb):
        def lanes(h):
            return pl.ds(pl.multiple_of(cb * CB + h * 128, 128), 128)

        @pl.loop(0, 8)
        def _(i):
            b = pl.multiple_of(i * 16, 16)
            for h in range(CB // 128):
                hs = pl.ds(h * 128, 128)
                x = [tuple(a_ref[q, pl.ds(a * 128 + b, 16), lanes(h)] for q in range(2)) for a in range(8)]
                for c, (yr, yi) in enumerate(fft8(x, 1)):
                    if c > 0:
                        tr, ti = twr_ref[0, c, pl.ds(b, 16)], twr_ref[1, c, pl.ds(b, 16)]
                        yr, yi = yr * tr - yi * ti, yr * ti + yi * tr
                    (hr, lr), (hi, li) = split(yr), split(yi)
                    s2_ref[c, pl.ds(b, 16), hs] = hr
                    s2_ref[c, pl.ds(128 + b, 16), hs] = hi
                    s2_ref[c, pl.ds(256 + b, 16), hs] = lr
                    s2_ref[c, pl.ds(384 + b, 16), hs] = li

        wide = pl.ds(pl.multiple_of(cb * CB, CB), CB)
        for c in range(8):
            acc = dot(ri_ref[:, 0:512], s2_ref[c]) + dot(ri_ref[:, 512:768], s2_ref[c, 0:256])
            ir, ii = acc[0:128], acc[128:256]
            amp = amp_ref[pl.ds(c * 128, 128), wide].astype(F32)
            keep = 1.0 - amp * lax.rsqrt(jnp.maximum(ir * ir + ii * ii, FLOOR2))
            (hr, lr), (hi, li) = split(ir * keep), split(ii * keep)
            s3 = jnp.concatenate([hr, hi, lr, li], axis=0)
            acc = dot(rf_ref[:, 0:512], s3) + dot(rf_ref[:, 512:768], s3[0:256])
            z2_ref[c] = acc

        @pl.loop(0, 16)
        def _(i):
            b = pl.multiple_of(i * 8, 8)
            for h in range(CB // 128):
                hs = pl.ds(h * 128, 128)
                x = []
                for c in range(8):
                    zr, zi = z2_ref[c, pl.ds(b, 8), hs], z2_ref[c, pl.ds(128 + b, 8), hs]
                    if c > 0:
                        tr, ti = twr_ref[0, c, pl.ds(b, 8)], twr_ref[1, c, pl.ds(b, 8)]
                        zr, zi = zr * tr + zi * ti, zi * tr - zr * ti
                    x.append((zr, zi))
                for a, (yr, yi) in enumerate(fft8(x, -1)):
                    a_ref[0, pl.ds(a * 128 + b, 8), lanes(h)] = yr
                    a_ref[1, pl.ds(a * 128 + b, 8), lanes(h)] = yi

    back = jnp.bitwise_and(N - c0, N - 1)

    @pl.loop(0, N // RB)
    def _(rb):
        rows = pl.ds(pl.multiple_of(rb * RB, RB), RB)
        for c in range(8):
            (hr, lr), (hi, li) = split(a_ref[0, rows, lane_tile(c)]), split(a_ref[1, rows, lane_tile(c)])
            h = jnp.concatenate([hr, hi], axis=1)
            acc = dot(h, lf_ref[0:256]) + dot(jnp.concatenate([lr, li], axis=1), lf_ref[256:512])
            z_ref[c] = acc + dot(h, lf_ref[512:768])

        @pl.loop(0, RB // 16)
        def _(i):
            rows = pl.ds(pl.multiple_of(rb * RB + i * 16, 16), 16)
            sub = pl.ds(pl.multiple_of(i * 16, 16), 16)
            x = []
            for c in range(8):
                zr, zi = z_ref[c, sub, 0:128], z_ref[c, sub, 128:256]
                if c > 0:
                    tr, ti = twl_ref[0, c], twl_ref[1, c]
                    zr, zi = zr * tr + zi * ti, zi * tr - zr * ti
                x.append((zr, zi))
            for a, (sr, si) in enumerate(fft8(x, -1)):
                pr, pi = p_ref[0, rows, lane_tile(a)].astype(F32), p_ref[1, rows, lane_tile(a)].astype(F32)
                wr, wi = w_ref[0, rows, lane_tile(a)].astype(F32), w_ref[1, rows, lane_tile(a)].astype(F32)
                w_ref[0, rows, lane_tile(a)] = (pr * sr + pi * si).astype(BF16)
                w_ref[1, rows, lane_tile(a)] = (pr * si - pi * sr).astype(BF16)
                a_ref[0, rows, lane_tile(a)] = (wr * sr + wi * si) * (1.0 / 256)
                a_ref[1, rows, lane_tile(a)] = (wr * si - wi * sr) * (1.0 / 256)
            for q in range(2):
                a_ref[q, rows, :] = pltpu.roll(a_ref[q, rows, :], back, 1)

    @pl.loop(0, N // 16)
    def _(i):
        rows = pl.ds(pl.multiple_of(i * 16, 16), 16)
        for q in range(2):
            for a in range(2):
                x = w_ref[q, rows, lane_tile(a)].astype(F32)
                ahead = lane + 128 * a >= c0
                w_ref[q, rows, lane_tile(a)] = jnp.where(ahead, x, 0.0).astype(BF16)
                w_ref[q, rows, lane_tile(a + 8)] = jnp.where(ahead, 0.0, x).astype(BF16)

    @pl.loop(0, 16)
    def _(i):
        k = pl.multiple_of(i * 16, 16)
        for q in range(2):
            for a in range(10):
                x = w_ref[q, pl.ds(k, 16), lane_tile(a)].astype(F32)
                ahead = line + k >= r0
                w_ref[q, pl.ds(k, 16), lane_tile(a)] = jnp.where(ahead, x, 0.0).astype(BF16)
                w_ref[q, pl.ds(k + N, 16), lane_tile(a)] = jnp.where(ahead, 0.0, x).astype(BF16)

    results = (oc_ref, ol_ref, or_ref, ov_ref, ovl_ref, ovr_ref, oi_ref)
    stores = [pltpu.make_async_copy(x, y, out_sem.at[k]) for k, (x, y) in enumerate(zip(places, results))]
    for store in stores:
        store.start()

    a_ref[:, N:N + 256, :] = a_ref[:, 0:256, :]
    shift = jnp.bitwise_and(r0, 7)
    base = r0 - shift
    up = jnp.bitwise_and(8 - shift, 7)
    inside = lax.broadcasted_iota(jnp.int32, (8, N), 0) < 8 - shift
    for s, (out_ref, t_ref, bit) in enumerate(((other_ref, to_ref, 1 - core), (mine_ref, tm_ref, core))):
        @pl.loop(0, 8)
        def _(i):
            u = jnp.right_shift(i, 1) * 256 + bit * 128 + jnp.bitwise_and(i, 1) * 64
            start = pl.multiple_of(u + base, 8)
            for q in range(2):
                to = pl.multiple_of(q * 512 + i * 64, 64)
                turned = [pltpu.roll(a_ref[q, pl.ds(start + 8 * j, 8), :], up, 0) for j in range(9)]
                lines = [jnp.where(inside, turned[j], turned[j + 1]) for j in range(8)]
                for j in range(0, 8, 2):
                    t_ref[pl.ds(to + 8 * j, 16), :] = jnp.concatenate(lines[j:j + 2], axis=0).astype(t_ref.dtype)

        store = pltpu.make_async_copy(t_ref, out_ref, out_sem.at[7 + s])
        store.start()
        stores.append(store)
    for store in stores:
        store.wait()


def led(pos, pieces, p, amp, tb):
    vm = pl.BlockSpec(memory_space=pltpu.VMEM)
    hbm = pl.BlockSpec(memory_space=pltpu.HBM)

    def rims(rows):
        return [jax.ShapeDtypeStruct((2, rows, cols), BF16) for cols in (TILE, RIM, RIM)]

    return pl.pallas_call(
        led_body,
        out_shape=rims(TILE) + rims(RIM) + [jax.ShapeDtypeStruct((2, RIM, REGION), BF16)]
        + [jax.ShapeDtypeStruct((N, N), F32), jax.ShapeDtypeStruct((N, N), BF16)],
        in_specs=[pl.BlockSpec(memory_space=pltpu.SMEM)] + [hbm] * 10 + [vm] * 6,
        out_specs=[hbm] * 9,
        scratch_shapes=[
            pltpu.VMEM((2, REGION, REGION), BF16),
            pltpu.VMEM((2, N, N), BF16),
            pltpu.VMEM((N, N), BF16),
            pltpu.VMEM((2, N + 264, N), F32),
            pltpu.VMEM((8, RB, 512), BF16),
            pltpu.VMEM((8, 512, CB), BF16),
            pltpu.VMEM((8, RB, 256), F32),
            pltpu.VMEM((8, 256, CB), F32),
            pltpu.VMEM((N, N), BF16),
            pltpu.VMEM((N, N), F32),
            pltpu.SemaphoreType.DMA((11,)),
            pltpu.SemaphoreType.DMA((9,)),
        ],
        compiler_params=pltpu.CompilerParams(vmem_limit_bytes=60 * 2**20),
        cost_estimate=pl.CostEstimate(flops=13 * 10**9, bytes_accessed=30 * 2**20, transcendentals=N * N),
        name="led",
    )(pos, *pieces, p, amp, tb["lane_inv"], tb["lane_fwd"], tb["row_inv"], tb["row_fwd"], tb["tw_lane"], tb["tw_row"])


def turn_body(pos_ref, p_ref, po_ref, x_ref):
    r0, c0 = pos_ref[0], pos_ref[1]

    @pl.loop(0, N // 16)
    def _(i):
        u = pl.multiple_of(i * 16, 16)
        for q in range(2):
            x_ref[q, pl.ds(u + 256, 16), :] = pltpu.roll(p_ref[q, pl.ds(u, 16), :].astype(F32), c0, 1)

    x_ref[:, 0:256, :] = x_ref[:, N:N + 256, :]
    start = 256 - r0
    shift = jnp.bitwise_and(start, 7)
    base = start - shift
    up = jnp.bitwise_and(8 - shift, 7)
    inside = lax.broadcasted_iota(jnp.int32, (8, N), 0) < 8 - shift

    @pl.loop(0, N // 64)
    def _(i):
        u = pl.multiple_of(i * 64, 64)
        first = pl.multiple_of(u + base, 8)
        for q in range(2):
            turned = [pltpu.roll(x_ref[q, pl.ds(first + 8 * j, 8), :], up, 0) for j in range(9)]
            rows = [jnp.where(inside, turned[j], turned[j + 1]) for j in range(8)]
            po_ref[q, pl.ds(u, 64), :] = jnp.concatenate(rows, axis=0).astype(BF16)


def turn(pos, pupil):
    vm = pl.BlockSpec(memory_space=pltpu.VMEM)
    return pl.pallas_call(
        turn_body,
        out_shape=jax.ShapeDtypeStruct((2, N, N), BF16),
        in_specs=[pl.BlockSpec(memory_space=pltpu.SMEM), vm],
        out_specs=vm,
        scratch_shapes=[pltpu.VMEM((2, N + 264, N), F32)],
        compiler_params=pltpu.CompilerParams(vmem_limit_bytes=40 * 2**20),
        cost_estimate=FREE,
        name="turn",
    )(pos, pupil)


def order_body(amp_ref, perm_ref, ao_ref):
    for i in range(4):
        part = dot(perm_ref[i * 256:(i + 1) * 256, :], amp_ref[...]).astype(BF16)
        part = lax.dot_general(part, perm_ref[...], (((1,), (1,)), ((), ())), preferred_element_type=F32)
        ao_ref[i * 256:(i + 1) * 256, :] = part.astype(BF16)


def order(amplitude, perm):
    vm = pl.BlockSpec(memory_space=pltpu.VMEM)
    return pl.pallas_call(
        order_body,
        out_shape=jax.ShapeDtypeStruct((N, N), BF16),
        in_specs=[vm, vm],
        out_specs=vm,
        compiler_params=pltpu.CompilerParams(vmem_limit_bytes=40 * 2**20),
        cost_estimate=FREE,
        name="order",
    )(amplitude, perm)


def ends_body(pos_ref, spec_ref, l_ref, r_ref, v_ref, vl_ref, vr_ref):
    gap = TILE - RIM
    l_ref[...] = spec_ref[:, :, gap:]
    r_ref[...] = spec_ref[:, :, :RIM]
    outer = pos_ref[2] * gap

    @pl.loop(0, RIM // 32)
    def _(i):
        src = pl.ds(pl.multiple_of(outer + i * 32, 32), 32)
        dst = pl.ds(pl.multiple_of(i * 32, 32), 32)
        for q in range(2):
            v_ref[q, dst, :] = spec_ref[q, src, :]
            vl_ref[q, dst, :] = spec_ref[q, src, gap:]
            vr_ref[q, dst, :] = spec_ref[q, src, :RIM]


def ends(pos, spectrum):
    vm = pl.BlockSpec(memory_space=pltpu.VMEM)
    sizes = ((TILE, RIM), (TILE, RIM), (RIM, TILE), (RIM, RIM), (RIM, RIM))
    return pl.pallas_call(
        ends_body,
        out_shape=[jax.ShapeDtypeStruct((2,) + size, BF16) for size in sizes],
        in_specs=[pl.BlockSpec(memory_space=pltpu.SMEM), vm],
        out_specs=[vm] * 5,
        cost_estimate=FREE,
        name="ends",
    )(pos, spectrum)


def cut_body(pos_ref, l_ref, r_ref, *refs):
    out_ref = refs[-1]
    row = (1 - pos_ref[2]) * (TILE - RIM)

    @pl.loop(0, RIM // 32)
    def _(i):
        dst = pl.ds(pl.multiple_of(i * 32, 32), 32)
        src = pl.ds(pl.multiple_of(row + i * 32, 32), 32)
        for q in range(2):
            out_ref[q, dst, 0:RIM] = l_ref[q, src, :]
            out_ref[q, dst, RIM:2 * RIM] = r_ref[q, src, :]


def cut(pos, l, r, *tokens):
    vm = pl.BlockSpec(memory_space=pltpu.VMEM)
    return pl.pallas_call(
        cut_body,
        out_shape=jax.ShapeDtypeStruct((2, RIM, 2 * RIM), BF16),
        in_specs=[pl.BlockSpec(memory_space=pltpu.SMEM), vm, vm] + [pl.BlockSpec(memory_space=pl.ANY)] * len(tokens),
        out_specs=vm,
        cost_estimate=FREE,
        name="cut",
    )(pos, l, r, *tokens)


def sides_body(pos_ref, l_ref, r_ref, i_ref, *refs):
    ol_ref, or_ref = refs[-2:]
    at = (1 - pos_ref[2]) * (TILE - RIM)
    for mid_ref, col, out_ref in ((l_ref, 0, ol_ref), (r_ref, RIM + TILE, or_ref)):
        out_ref[...] = mid_ref[...]

        @pl.loop(0, RIM // 32)
        def _(i):
            src = pl.ds(pl.multiple_of(i * 32, 32), 32)
            dst = pl.ds(pl.multiple_of(at + i * 32, 32), 32)
            for q in range(2):
                add = i_ref[q, src, col:col + RIM].astype(F32)
                out_ref[q, dst, :] = (mid_ref[q, dst, :].astype(F32) + add).astype(BF16)


def sides(pos, l, r, i, *tokens):
    vm = pl.BlockSpec(memory_space=pltpu.VMEM)
    return pl.pallas_call(
        sides_body,
        out_shape=[jax.ShapeDtypeStruct(l.shape, BF16)] * 2,
        in_specs=[pl.BlockSpec(memory_space=pltpu.SMEM)] + [vm] * 3 + [pl.BlockSpec(memory_space=pl.ANY)] * len(tokens),
        out_specs=[vm] * 2,
        compiler_params=pltpu.CompilerParams(vmem_limit_bytes=32 * 2**20),
        cost_estimate=FREE,
        name="sides",
    )(pos, l, r, i, *tokens)


def tile_body(pos_ref, c_ref, i_ref, v_ref, l_ref, r_ref, vl_ref, vr_ref, out_ref):
    core = pos_ref[2]
    gap = TILE - RIM
    out_ref[...] = c_ref[...].astype(F32)
    out_ref[0, :, gap:] += l_ref[0].astype(F32)
    out_ref[0, :, :RIM] += r_ref[0].astype(F32)
    at_i = (1 - core) * gap
    at_v = core * gap

    @pl.loop(0, RIM // 32)
    def _(i):
        src = pl.ds(pl.multiple_of(i * 32, 32), 32)
        out_ref[0, pl.ds(pl.multiple_of(at_i + i * 32, 32), 32), :] += i_ref[0, src, RIM:RIM + TILE].astype(F32)
        dst = pl.ds(pl.multiple_of(at_v + i * 32, 32), 32)
        out_ref[0, dst, :] += v_ref[0, src, :].astype(F32)
        out_ref[0, dst, gap:] += vl_ref[0, src, :].astype(F32)
        out_ref[0, dst, :RIM] += vr_ref[0, src, :].astype(F32)


def tile_sum(pos, parts):
    def block(x):
        return pl.BlockSpec((1,) + x.shape[1:], lambda q: (q, 0, 0))

    return pl.pallas_call(
        tile_body,
        grid=(2,),
        out_shape=jax.ShapeDtypeStruct((2, TILE, TILE), F32),
        in_specs=[pl.BlockSpec(memory_space=pltpu.SMEM)] + [block(x) for x in parts],
        out_specs=pl.BlockSpec((1, TILE, TILE), lambda q: (q, 0, 0)),
        compiler_params=pltpu.CompilerParams(vmem_limit_bytes=32 * 2**20),
        cost_estimate=FREE,
        name="tile_sum",
    )(pos, *parts)


def pair_body(mine_ref, other_ref, out_ref):
    for z in range(8):
        rows = pl.ds(z * 16, 16)
        out_ref[z, 0] = mine_ref[rows, :] + other_ref[rows, :].astype(F32)


def pair_sum(mine, other):
    rows = pl.BlockSpec((128, N), lambda i: (i, 0))
    return pl.pallas_call(
        pair_body,
        grid=(8,),
        out_shape=jax.ShapeDtypeStruct((8, 8, 16, N), F32),
        in_specs=[rows, rows],
        out_specs=pl.BlockSpec((8, 1, 16, N), lambda i: (0, i, 0, 0)),
        cost_estimate=FREE,
        name="pair_sum",
    )(mine, other)


def after_body(x_ref, token_ref, out_ref):
    out_ref[...] = x_ref[...]


def after(x, token):
    vm = pl.BlockSpec(memory_space=pltpu.VMEM)
    return pl.pallas_call(
        after_body,
        out_shape=jax.ShapeDtypeStruct(x.shape, x.dtype),
        in_specs=[vm, pl.BlockSpec(memory_space=pl.ANY)],
        out_specs=vm,
        cost_estimate=FREE,
        name="after",
    )(x, token)


KY, KX = ("x", "yh", "core"), ("z", "yl")
ALL = KY + KX


def chain(n):
    up = [(i, i + 1) for i in range(n - 1)]
    return up, [(j, i) for i, j in up]


def between_chips(n):
    return [(i, i + 1) for i in range(1, n - 1, 2)] + [(i, i - 1) for i in range(2, n, 2)]


def both(rows, cols, n_cols):
    return [(a * n_cols + b, c * n_cols + d) for a, c in rows for b, d in cols]


def body(spectrum, pupil, amplitude, offsets):
    tb = {k: jnp.asarray(v) for k, v in tables().items()}
    n_ky, n_kx = lax.axis_size(KY), lax.axis_size(KX)
    iy, ix, core = lax.axis_index(KY), lax.axis_index(KX), lax.axis_index("core")
    first = core == 0
    r0 = offsets[0, 0, 0] - (iy * TILE - RIM)
    c0 = offsets[0, 0, 1] - (ix * TILE - RIM)
    pos = jnp.stack([r0, c0, core])
    right, left = chain(n_kx)
    vert = between_chips(n_ky)
    vert_l, vert_r = both(vert, left, n_kx), both(vert, right, n_kx)
    swap = [(0, 1), (1, 0)]

    out_l, out_r, out_v, out_vl, out_vr = ends(pos, spectrum)
    in_l = lax.ppermute(out_l, KX, right)
    in_r = lax.ppermute(out_r, KX, left)
    in_v = lax.ppermute(out_v, KY, vert)
    in_vl = lax.ppermute(out_vl, ALL, vert_r)
    in_vr = lax.ppermute(out_vr, ALL, vert_l)
    in_i = lax.ppermute(spectrum, "core", swap)
    amp = order(amplitude, tb["perm"])
    pupil = turn(pos, pupil)
    in_c = lax.ppermute(cut(pos, in_l, in_r, pupil, amp, in_v, in_vl, in_vr), "core", swap)
    pieces = (spectrum, in_l, in_r, in_v, in_vl, in_vr, in_i, in_c)
    c, l, r, v, vl, vr, i, mine, other = led(pos, pieces, pupil, amp, tb)

    i = lax.ppermute(i, "core", swap)
    v = lax.ppermute(v, KY, vert)
    vl = lax.ppermute(vl, ALL, vert_l)
    vr = lax.ppermute(vr, ALL, vert_r)
    total = pair_sum(mine, lax.ppermute(other, "core", swap))
    l, r = sides(pos, l, r, i, v, total)
    l = lax.ppermute(l, KX, left)
    r = lax.ppermute(r, KX, right)
    tile = tile_sum(pos, (c, i, v, l, r, vl, vr))
    total = lax.psum_scatter(total.reshape(8, 128, N), "z", scatter_dimension=0, tiled=True).reshape(16, 8, N)
    total = lax.all_to_all(after(total, tile), ("x", "yh", "yl"), 0, 0)
    return tile, jnp.sum(total, axis=0).reshape(-1)


def solution(mesh):
    fine = Mesh(mesh.devices.reshape(4, 2, 2, 8, 2), ALL)
    return jax.shard_map(
        body,
        mesh=fine,
        in_specs=(P(None, KY, KX), P(), P(KY, KX), P(KY, KX, None)),
        out_specs=(P(None, KY, KX), P(ALL)),
        check_vma=False,
    )
```

```python
import math

import jax
import jax.numpy as jnp
import ml_dtypes
import numpy as np
from jax import lax
from jax.experimental import pallas as pl
from jax.experimental.pallas import tpu as pltpu
from jax.sharding import Mesh
from jax.sharding import PartitionSpec as P

F32 = jnp.float32
BF16 = jnp.bfloat16
N = 1024
TILE = 512
RIM = 384
REGION = TILE + 2 * RIM
FLOOR2 = 0.0625
FREE = pl.CostEstimate(flops=1, bytes_accessed=1, transcendentals=0)


def split_np(t):
    hi = t.astype(np.float32).astype(ml_dtypes.bfloat16)
    lo = (t - hi.astype(np.float64)).astype(np.float32).astype(ml_dtypes.bfloat16)
    return hi, lo


def tables():
    b = np.arange(128)
    ang = 2.0 * np.pi / 128 * ((b[:, None] * b[None, :]) % 128)
    out = {}
    for name, sign in (("inv", 1.0), ("fwd", -1.0)):
        cr, ci = np.cos(ang) / 32.0, sign * np.sin(ang) / 32.0
        block = np.block([[cr, ci], [-ci, cr]])
        hi, lo = split_np(block)
        out["lane_" + name] = np.concatenate([hi, hi, lo], axis=0)
        out["row_" + name] = np.concatenate([hi.T, hi.T, lo.T], axis=1)
    tw = 2.0 * np.pi / N * (np.arange(8)[:, None] * b[None, :])
    tw = np.stack([np.cos(tw), np.sin(tw)]).astype(np.float32)
    out["tw_lane"] = tw.reshape(2, 8, 1, 128)
    out["tw_row"] = np.ascontiguousarray(np.broadcast_to(tw[:, :, :, None], (2, 8, 128, 128)))
    s = np.arange(N)
    perm = np.zeros((N, N), ml_dtypes.bfloat16)
    perm[s, (s // 128) + 8 * (s % 128)] = 1
    out["perm"] = perm
    return out


def cadd(p, q):
    return (p[0] + q[0], p[1] + q[1])


def csub(p, q):
    return (p[0] - q[0], p[1] - q[1])


def crot(p, sign):
    return (-p[1], p[0]) if sign > 0 else (p[1], -p[0])


def fft4(x0, x1, x2, x3, sign):
    t0, t1 = cadd(x0, x2), csub(x0, x2)
    t2, t3 = cadd(x1, x3), crot(csub(x1, x3), sign)
    return [cadd(t0, t2), cadd(t1, t3), csub(t0, t2), csub(t1, t3)]


def fft8(x, sign):
    even = fft4(x[0], x[2], x[4], x[6], sign)
    odd = fft4(x[1], x[3], x[5], x[7], sign)
    h = math.sqrt(0.5)
    r, i = odd[1]
    odd[1] = ((r - i) * h, (r + i) * h) if sign > 0 else ((r + i) * h, (i - r) * h)
    odd[2] = crot(odd[2], sign)
    r, i = odd[3]
    odd[3] = ((-r - i) * h, (r - i) * h) if sign > 0 else ((i - r) * h, (-r - i) * h)
    return [cadd(e, o) for e, o in zip(even, odd)] + [csub(e, o) for e, o in zip(even, odd)]


def split(x):
    hi = x.astype(BF16)
    return hi, (x - hi.astype(F32)).astype(BF16)


def dot(a, b):
    return jnp.dot(a, b, preferred_element_type=F32)


RB = 64
CB = 256


def led_body(
    pos_ref, own_ref, l_ref, r_ref, v_ref, vl_ref, vr_ref, i_ref, c_ref, p_ref, amp_ref,
    li_ref, lf_ref, ri_ref, rf_ref, twl_ref, twr_ref,
    oc_ref, ol_ref, or_ref, ov_ref, ovl_ref, ovr_ref, oi_ref, mine_ref, other_ref,
    w_ref, a_ref, s_refs, z_refs, s2_refs, z2_refs, to_ref, tm_ref, in_sem, out_sem,
):
    r0, c0, core = pos_ref[0], pos_ref[1], pos_ref[2]
    outer = pl.multiple_of((RIM + TILE) * core, 128)
    inner = pl.multiple_of((RIM + TILE) * (1 - core), 128)
    places = []
    for start, count in ((RIM, TILE), (outer, RIM)):
        for col, wide in ((RIM, TILE), (0, RIM), (RIM + TILE, RIM)):
            places.append(w_ref.at[:, pl.ds(start, count), pl.ds(col, wide)])
    arrivals = [own_ref, l_ref, r_ref, v_ref, vl_ref, vr_ref]
    arrivals.append(i_ref.at[:, pl.ds(pl.multiple_of(core * (TILE - RIM), 128), RIM), :])
    arrivals += [c_ref.at[:, :, pl.ds(0, RIM)], c_ref.at[:, :, pl.ds(RIM, RIM)]]
    sides = [w_ref.at[:, pl.ds(inner, RIM), pl.ds(col, wide)] for col, wide in ((RIM, TILE), (0, RIM), (RIM + TILE, RIM))]
    loads = [pltpu.make_async_copy(x, y, in_sem.at[k]) for k, (x, y) in enumerate(zip(arrivals, places + sides))]
    places.append(w_ref.at[:, pl.ds(inner, RIM), :])
    for load in loads:
        load.start()

    def lane_tile(k):
        return pl.ds(k * 128, 128)

    lane = lax.broadcasted_iota(jnp.int32, (16, 128), 1)
    line = lax.broadcasted_iota(jnp.int32, (16, 128), 0)
    for load in loads:
        load.wait()

    @pl.loop(0, REGION // 16, unroll=4)
    def _(i):
        rows = pl.ds(pl.multiple_of(i * 16, 16), 16)
        for q in range(2):
            for a in range(2):
                here, there = w_ref[q, rows, lane_tile(a)].astype(F32), w_ref[q, rows, lane_tile(a + 8)].astype(F32)
                w_ref[q, rows, lane_tile(a)] = jnp.where(lane + 128 * a >= c0, here, there).astype(BF16)

    @pl.loop(0, 16, unroll=2)
    def _(i):
        k = pl.multiple_of(i * 16, 16)
        for q in range(2):
            for a in range(8):
                here = w_ref[q, pl.ds(k, 16), lane_tile(a)].astype(F32)
                there = w_ref[q, pl.ds(k + N, 16), lane_tile(a)].astype(F32)
                w_ref[q, pl.ds(k, 16), lane_tile(a)] = jnp.where(line + k >= r0, here, there).astype(BF16)

    def put(ref, at, hs, yr, yi, step):
        (hr, lr), (hi, li) = split(yr), split(yi)
        for k, part in enumerate((hr, hi, lr, li)):
            if step is None:
                ref[at, k * 128:(k + 1) * 128] = part
            else:
                ref[at[0], pl.ds(at[1] + k * step, 16), hs] = part

    def first_vpu(n, s_ref):
        for i in range(RB // 16):
            rows = pl.ds(pl.multiple_of(n * RB + i * 16, 16), 16)
            x = []
            for a in range(8):
                pr, pi = p_ref[0, rows, lane_tile(a)].astype(F32), p_ref[1, rows, lane_tile(a)].astype(F32)
                wr, wi = w_ref[0, rows, lane_tile(a)].astype(F32), w_ref[1, rows, lane_tile(a)].astype(F32)
                x.append((pr * wr - pi * wi, pr * wi + pi * wr))
            for c, (yr, yi) in enumerate(fft8(x, 1)):
                if c > 0:
                    tr, ti = twl_ref[0, c], twl_ref[1, c]
                    yr, yi = yr * tr - yi * ti, yr * ti + yi * tr
                put(s_ref, pl.ds(c * RB + i * 16, 16), None, yr, yi, None)

    def first_mxu(n, s_ref):
        rows = pl.ds(pl.multiple_of(n * RB, RB), RB)
        acc = dot(s_ref[...], li_ref[0:512]) + dot(s_ref[:, 0:256], li_ref[512:768])
        for c in range(8):
            a_ref[0, rows, lane_tile(c)] = acc[c * RB:(c + 1) * RB, 0:128]
            a_ref[1, rows, lane_tile(c)] = acc[c * RB:(c + 1) * RB, 128:256]

    last = N // RB - 1
    first_vpu(0, s_refs[0])

    @pl.loop(0, N // RB // 2)
    def _(j):
        first_mxu(2 * j, s_refs[0])
        first_vpu(2 * j + 1, s_refs[1])
        first_mxu(2 * j + 1, s_refs[1])
        first_vpu(jnp.minimum(2 * j + 2, last), s_refs[0])

    def lanes(cb, h):
        return pl.ds(pl.multiple_of(cb * CB + h * 128, 128), 128)

    def second_in(cb, part, s2_ref):
        b = pl.multiple_of(part * 16, 16)
        for h in range(CB // 128):
            x = [tuple(a_ref[q, pl.ds(a * 128 + b, 16), lanes(cb, h)] for q in range(2)) for a in range(8)]
            for c, (yr, yi) in enumerate(fft8(x, 1)):
                if c > 0:
                    tr, ti = twr_ref[0, c, pl.ds(b, 16)], twr_ref[1, c, pl.ds(b, 16)]
                    yr, yi = yr * tr - yi * ti, yr * ti + yi * tr
                put(s2_ref, (c, b), pl.ds(h * 128, 128), yr, yi, 128)

    def second_mxu(cb, c, s2_ref, z2_ref):
        wide = pl.ds(pl.multiple_of(cb * CB, CB), CB)
        acc = dot(ri_ref[:, 0:512], s2_ref[c]) + dot(ri_ref[:, 512:768], s2_ref[c, 0:256])
        ir, ii = acc[0:128], acc[128:256]
        amp = amp_ref[pl.ds(pl.multiple_of(c * 128, 128), 128), wide].astype(F32)
        keep = 1.0 - amp * lax.rsqrt(jnp.maximum(ir * ir + ii * ii, FLOOR2))
        (hr, lr), (hi, li) = split(ir * keep), split(ii * keep)
        s3 = jnp.concatenate([hr, hi, lr, li], axis=0)
        z2_ref[c] = dot(rf_ref[:, 0:512], s3) + dot(rf_ref[:, 512:768], s3[0:256])

    def second_out(cb, part, z2_ref):
        for half in range(2):
            b = pl.multiple_of(part * 16 + half * 8, 8)
            for h in range(CB // 128):
                hs = pl.ds(h * 128, 128)
                x = []
                for c in range(8):
                    zr, zi = z2_ref[c, pl.ds(b, 8), hs], z2_ref[c, pl.ds(128 + b, 8), hs]
                    if c > 0:
                        tr, ti = twr_ref[0, c, pl.ds(b, 8)], twr_ref[1, c, pl.ds(b, 8)]
                        zr, zi = zr * tr + zi * ti, zi * tr - zr * ti
                    x.append((zr, zi))
                for a, (yr, yi) in enumerate(fft8(x, -1)):
                    a_ref[0, pl.ds(a * 128 + b, 8), lanes(cb, h)] = yr
                    a_ref[1, pl.ds(a * 128 + b, 8), lanes(cb, h)] = yi

    @pl.loop(0, 8)
    def _(c):
        second_in(0, c, s2_refs[0])

    for cb in range(N // CB):
        @pl.loop(0, 8, unroll=8)
        def _(c):
            if cb + 1 < N // CB:
                second_in(cb + 1, c, s2_refs[(cb + 1) % 2])
            second_mxu(cb, c, s2_refs[cb % 2], z2_refs[cb % 2])
            if cb > 0:
                second_out(cb - 1, c, z2_refs[(cb - 1) % 2])

    @pl.loop(0, 8)
    def _(c):
        second_out(N // CB - 1, c, z2_refs[(N // CB - 1) % 2])

    back = jnp.bitwise_and(N - c0, N - 1)

    def third_mxu(n, s_ref, z_ref):
        rows = pl.ds(pl.multiple_of(n * RB, RB), RB)
        for c in range(8):
            put(s_ref, pl.ds(c * RB, RB), None, a_ref[0, rows, lane_tile(c)], a_ref[1, rows, lane_tile(c)], None)
        z_ref[...] = dot(s_ref[...], lf_ref[0:512]) + dot(s_ref[:, 0:256], lf_ref[512:768])

    def third_vpu(n, z_ref):
        for i in range(RB // 16):
            rows = pl.ds(pl.multiple_of(n * RB + i * 16, 16), 16)
            x = []
            for c in range(8):
                sub = pl.ds(c * RB + i * 16, 16)
                zr, zi = z_ref[sub, 0:128], z_ref[sub, 128:256]
                if c > 0:
                    tr, ti = twl_ref[0, c], twl_ref[1, c]
                    zr, zi = zr * tr + zi * ti, zi * tr - zr * ti
                x.append((zr, zi))
            for a, (sr, si) in enumerate(fft8(x, -1)):
                pr, pi = p_ref[0, rows, lane_tile(a)].astype(F32), p_ref[1, rows, lane_tile(a)].astype(F32)
                wr, wi = w_ref[0, rows, lane_tile(a)].astype(F32), w_ref[1, rows, lane_tile(a)].astype(F32)
                w_ref[0, rows, lane_tile(a)] = (pr * sr + pi * si).astype(BF16)
                w_ref[1, rows, lane_tile(a)] = (pr * si - pi * sr).astype(BF16)
                a_ref[0, rows, lane_tile(a)] = (wr * sr + wi * si) * (1.0 / 256)
                a_ref[1, rows, lane_tile(a)] = (wr * si - wi * sr) * (1.0 / 256)
            for q in range(2):
                a_ref[q, rows, :] = pltpu.roll(a_ref[q, rows, :], back, 1)

    third_mxu(0, s_refs[0], z_refs[0])

    @pl.loop(0, N // RB // 2 - 1)
    def _(j):
        third_mxu(2 * j + 1, s_refs[1], z_refs[1])
        third_vpu(2 * j, z_refs[0])
        third_mxu(2 * j + 2, s_refs[0], z_refs[0])
        third_vpu(2 * j + 1, z_refs[1])

    third_mxu(last, s_refs[1], z_refs[1])
    third_vpu(last - 1, z_refs[0])
    third_vpu(last, z_refs[1])

    @pl.loop(0, N // 16, unroll=4)
    def _(i):
        rows = pl.ds(pl.multiple_of(i * 16, 16), 16)
        for q in range(2):
            for a in range(2):
                x = w_ref[q, rows, lane_tile(a)].astype(F32)
                ahead = lane + 128 * a >= c0
                w_ref[q, rows, lane_tile(a)] = jnp.where(ahead, x, 0.0).astype(BF16)
                w_ref[q, rows, lane_tile(a + 8)] = jnp.where(ahead, 0.0, x).astype(BF16)

    @pl.loop(0, 16, unroll=2)
    def _(i):
        k = pl.multiple_of(i * 16, 16)
        for q in range(2):
            for a in range(10):
                x = w_ref[q, pl.ds(k, 16), lane_tile(a)].astype(F32)
                ahead = line + k >= r0
                w_ref[q, pl.ds(k, 16), lane_tile(a)] = jnp.where(ahead, x, 0.0).astype(BF16)
                w_ref[q, pl.ds(k + N, 16), lane_tile(a)] = jnp.where(ahead, 0.0, x).astype(BF16)

    results = (oc_ref, ol_ref, or_ref, ov_ref, ovl_ref, ovr_ref, oi_ref)
    stores = [pltpu.make_async_copy(x, y, out_sem.at[k]) for k, (x, y) in enumerate(zip(places, results))]
    for store in stores:
        store.start()

    a_ref[:, N:N + 256, :] = a_ref[:, 0:256, :]
    shift = jnp.bitwise_and(r0, 7)
    base = r0 - shift
    up = jnp.bitwise_and(8 - shift, 7)
    inside = lax.broadcasted_iota(jnp.int32, (8, N), 0) < 8 - shift
    for s, (out_ref, t_ref, bit) in enumerate(((other_ref, to_ref, 1 - core), (mine_ref, tm_ref, core))):
        @pl.loop(0, 8)
        def _(i):
            u = jnp.right_shift(i, 1) * 256 + bit * 128 + jnp.bitwise_and(i, 1) * 64
            start = pl.multiple_of(u + base, 8)
            for q in range(2):
                to = pl.multiple_of(q * 512 + i * 64, 64)
                turned = [pltpu.roll(a_ref[q, pl.ds(start + 8 * j, 8), :], up, 0) for j in range(9)]
                lines = [jnp.where(inside, turned[j], turned[j + 1]) for j in range(8)]
                for j in range(0, 8, 2):
                    t_ref[pl.ds(to + 8 * j, 16), :] = jnp.concatenate(lines[j:j + 2], axis=0).astype(t_ref.dtype)

        store = pltpu.make_async_copy(t_ref, out_ref, out_sem.at[7 + s])
        store.start()
        stores.append(store)
    for store in stores:
        store.wait()


def led(pos, pieces, p, amp, tb):
    vm = pl.BlockSpec(memory_space=pltpu.VMEM)
    hbm = pl.BlockSpec(memory_space=pltpu.HBM)

    def rims(rows):
        return [jax.ShapeDtypeStruct((2, rows, cols), BF16) for cols in (TILE, RIM, RIM)]

    return pl.pallas_call(
        led_body,
        out_shape=rims(TILE) + rims(RIM) + [jax.ShapeDtypeStruct((2, RIM, REGION), BF16)]
        + [jax.ShapeDtypeStruct((N, N), F32), jax.ShapeDtypeStruct((N, N), BF16)],
        in_specs=[pl.BlockSpec(memory_space=pltpu.SMEM)] + [hbm] * 8 + [vm] * 8,
        out_specs=[hbm] * 9,
        scratch_shapes=[
            pltpu.VMEM((2, REGION, REGION), BF16),
            pltpu.VMEM((2, N + 264, N), F32),
            [pltpu.VMEM((8 * RB, 512), BF16)] * 2,
            [pltpu.VMEM((8 * RB, 256), F32)] * 2,
            [pltpu.VMEM((8, 512, CB), BF16)] * 2,
            [pltpu.VMEM((8, 256, CB), F32)] * 2,
            pltpu.VMEM((N, N), BF16),
            pltpu.VMEM((N, N), F32),
            pltpu.SemaphoreType.DMA((9,)),
            pltpu.SemaphoreType.DMA((9,)),
        ],
        compiler_params=pltpu.CompilerParams(vmem_limit_bytes=52 * 2**20),
        cost_estimate=pl.CostEstimate(flops=13 * 10**9, bytes_accessed=30 * 2**20, transcendentals=N * N),
        name="led",
    )(pos, *pieces, p, amp, tb["lane_inv"], tb["lane_fwd"], tb["row_inv"], tb["row_fwd"], tb["tw_lane"], tb["tw_row"])


def turn_body(pos_ref, p_ref, po_ref, x_ref):
    r0, c0 = pos_ref[0], pos_ref[1]

    @pl.loop(0, N // 16)
    def _(i):
        u = pl.multiple_of(i * 16, 16)
        for q in range(2):
            x_ref[q, pl.ds(u + 256, 16), :] = pltpu.roll(p_ref[q, pl.ds(u, 16), :].astype(F32), c0, 1)

    x_ref[:, 0:256, :] = x_ref[:, N:N + 256, :]
    start = 256 - r0
    shift = jnp.bitwise_and(start, 7)
    base = start - shift
    up = jnp.bitwise_and(8 - shift, 7)
    inside = lax.broadcasted_iota(jnp.int32, (8, N), 0) < 8 - shift

    @pl.loop(0, N // 64)
    def _(i):
        u = pl.multiple_of(i * 64, 64)
        first = pl.multiple_of(u + base, 8)
        for q in range(2):
            turned = [pltpu.roll(x_ref[q, pl.ds(first + 8 * j, 8), :], up, 0) for j in range(9)]
            rows = [jnp.where(inside, turned[j], turned[j + 1]) for j in range(8)]
            po_ref[q, pl.ds(u, 64), :] = jnp.concatenate(rows, axis=0).astype(BF16)


def turn(pos, pupil):
    vm = pl.BlockSpec(memory_space=pltpu.VMEM)
    return pl.pallas_call(
        turn_body,
        out_shape=jax.ShapeDtypeStruct((2, N, N), BF16),
        in_specs=[pl.BlockSpec(memory_space=pltpu.SMEM), vm],
        out_specs=vm,
        scratch_shapes=[pltpu.VMEM((2, N + 264, N), F32)],
        compiler_params=pltpu.CompilerParams(vmem_limit_bytes=40 * 2**20),
        cost_estimate=FREE,
        name="turn",
    )(pos, pupil)


def order_body(amp_ref, perm_ref, ao_ref):
    for i in range(4):
        part = dot(perm_ref[i * 256:(i + 1) * 256, :], amp_ref[...]).astype(BF16)
        part = lax.dot_general(part, perm_ref[...], (((1,), (1,)), ((), ())), preferred_element_type=F32)
        ao_ref[i * 256:(i + 1) * 256, :] = part.astype(BF16)


def order(amplitude, perm):
    vm = pl.BlockSpec(memory_space=pltpu.VMEM)
    return pl.pallas_call(
        order_body,
        out_shape=jax.ShapeDtypeStruct((N, N), BF16),
        in_specs=[vm, vm],
        out_specs=vm,
        compiler_params=pltpu.CompilerParams(vmem_limit_bytes=40 * 2**20),
        cost_estimate=FREE,
        name="order",
    )(amplitude, perm)


def ends_body(pos_ref, spec_ref, l_ref, r_ref, v_ref, vl_ref, vr_ref):
    gap = TILE - RIM
    l_ref[...] = spec_ref[:, :, gap:]
    r_ref[...] = spec_ref[:, :, :RIM]
    outer = pos_ref[2] * gap

    @pl.loop(0, RIM // 32)
    def _(i):
        src = pl.ds(pl.multiple_of(outer + i * 32, 32), 32)
        dst = pl.ds(pl.multiple_of(i * 32, 32), 32)
        for q in range(2):
            v_ref[q, dst, :] = spec_ref[q, src, :]
            vl_ref[q, dst, :] = spec_ref[q, src, gap:]
            vr_ref[q, dst, :] = spec_ref[q, src, :RIM]


def ends(pos, spectrum):
    vm = pl.BlockSpec(memory_space=pltpu.VMEM)
    sizes = ((TILE, RIM), (TILE, RIM), (RIM, TILE), (RIM, RIM), (RIM, RIM))
    return pl.pallas_call(
        ends_body,
        out_shape=[jax.ShapeDtypeStruct((2,) + size, BF16) for size in sizes],
        in_specs=[pl.BlockSpec(memory_space=pltpu.SMEM), vm],
        out_specs=[vm] * 5,
        cost_estimate=FREE,
        name="ends",
    )(pos, spectrum)


def cut_body(pos_ref, l_ref, r_ref, *refs):
    out_ref = refs[-1]
    row = (1 - pos_ref[2]) * (TILE - RIM)

    @pl.loop(0, RIM // 32)
    def _(i):
        dst = pl.ds(pl.multiple_of(i * 32, 32), 32)
        src = pl.ds(pl.multiple_of(row + i * 32, 32), 32)
        for q in range(2):
            out_ref[q, dst, 0:RIM] = l_ref[q, src, :]
            out_ref[q, dst, RIM:2 * RIM] = r_ref[q, src, :]


def cut(pos, l, r, *tokens):
    vm = pl.BlockSpec(memory_space=pltpu.VMEM)
    return pl.pallas_call(
        cut_body,
        out_shape=jax.ShapeDtypeStruct((2, RIM, 2 * RIM), BF16),
        in_specs=[pl.BlockSpec(memory_space=pltpu.SMEM), vm, vm] + [pl.BlockSpec(memory_space=pl.ANY)] * len(tokens),
        out_specs=vm,
        cost_estimate=FREE,
        name="cut",
    )(pos, l, r, *tokens)


def sides_body(pos_ref, l_ref, r_ref, i_ref, *refs):
    ol_ref, or_ref = refs[-2:]
    at = (1 - pos_ref[2]) * (TILE - RIM)
    for mid_ref, col, out_ref in ((l_ref, 0, ol_ref), (r_ref, RIM + TILE, or_ref)):
        out_ref[...] = mid_ref[...]

        @pl.loop(0, RIM // 32)
        def _(i):
            src = pl.ds(pl.multiple_of(i * 32, 32), 32)
            dst = pl.ds(pl.multiple_of(at + i * 32, 32), 32)
            for q in range(2):
                add = i_ref[q, src, col:col + RIM].astype(F32)
                out_ref[q, dst, :] = (mid_ref[q, dst, :].astype(F32) + add).astype(BF16)


def sides(pos, l, r, i, *tokens):
    vm = pl.BlockSpec(memory_space=pltpu.VMEM)
    return pl.pallas_call(
        sides_body,
        out_shape=[jax.ShapeDtypeStruct(l.shape, BF16)] * 2,
        in_specs=[pl.BlockSpec(memory_space=pltpu.SMEM)] + [vm] * 3 + [pl.BlockSpec(memory_space=pl.ANY)] * len(tokens),
        out_specs=[vm] * 2,
        compiler_params=pltpu.CompilerParams(vmem_limit_bytes=32 * 2**20),
        cost_estimate=FREE,
        name="sides",
    )(pos, l, r, i, *tokens)


def tile_body(pos_ref, c_ref, i_ref, v_ref, l_ref, r_ref, vl_ref, vr_ref, out_ref):
    core = pos_ref[2]
    gap = TILE - RIM
    out_ref[...] = c_ref[...].astype(F32)
    out_ref[0, :, gap:] += l_ref[0].astype(F32)
    out_ref[0, :, :RIM] += r_ref[0].astype(F32)
    at_i = (1 - core) * gap
    at_v = core * gap

    @pl.loop(0, RIM // 32)
    def _(i):
        src = pl.ds(pl.multiple_of(i * 32, 32), 32)
        out_ref[0, pl.ds(pl.multiple_of(at_i + i * 32, 32), 32), :] += i_ref[0, src, RIM:RIM + TILE].astype(F32)
        dst = pl.ds(pl.multiple_of(at_v + i * 32, 32), 32)
        out_ref[0, dst, :] += v_ref[0, src, :].astype(F32)
        out_ref[0, dst, gap:] += vl_ref[0, src, :].astype(F32)
        out_ref[0, dst, :RIM] += vr_ref[0, src, :].astype(F32)


def tile_sum(pos, parts):
    def block(x):
        return pl.BlockSpec((1,) + x.shape[1:], lambda q: (q, 0, 0))

    return pl.pallas_call(
        tile_body,
        grid=(2,),
        out_shape=jax.ShapeDtypeStruct((2, TILE, TILE), F32),
        in_specs=[pl.BlockSpec(memory_space=pltpu.SMEM)] + [block(x) for x in parts],
        out_specs=pl.BlockSpec((1, TILE, TILE), lambda q: (q, 0, 0)),
        compiler_params=pltpu.CompilerParams(vmem_limit_bytes=32 * 2**20),
        cost_estimate=FREE,
        name="tile_sum",
    )(pos, *parts)


def pair_body(mine_ref, other_ref, out_ref):
    for z in range(8):
        rows = pl.ds(z * 16, 16)
        out_ref[0, z, 0] = (mine_ref[rows, :] + other_ref[rows, :].astype(F32)).astype(BF16)


def pair_sum(mine, other):
    rows = pl.BlockSpec((128, N), lambda x, y: (2 * x + y, 0))
    return pl.pallas_call(
        pair_body,
        grid=(4, 2),
        out_shape=jax.ShapeDtypeStruct((4, 8, 2, 16, N), BF16),
        in_specs=[rows, rows],
        out_specs=pl.BlockSpec((1, 8, 1, 16, N), lambda x, y: (x, 0, y, 0, 0)),
        cost_estimate=FREE,
        name="pair_sum",
    )(mine, other)


def gather_body(x_ref, token_ref, out_ref):
    for i in range(2):
        rows = pl.ds(i * 16, 16)
        total = x_ref[0, rows, :].astype(F32)
        for k in range(1, 32):
            total += x_ref[k, rows, :].astype(F32)
        out_ref[rows, :] = total


def gather_sum(x, token):
    vm = pl.BlockSpec(memory_space=pltpu.VMEM)
    return pl.pallas_call(
        gather_body,
        out_shape=jax.ShapeDtypeStruct((32, N), F32),
        in_specs=[vm, pl.BlockSpec(memory_space=pl.ANY)],
        out_specs=vm,
        cost_estimate=FREE,
        name="gather_sum",
    )(x, token)


KY, KX = ("x", "yh", "core"), ("z", "yl")
ALL = KY + KX


def chain(n):
    up = [(i, i + 1) for i in range(n - 1)]
    return up, [(j, i) for i, j in up]


def between_chips(n):
    return [(i, i + 1) for i in range(1, n - 1, 2)] + [(i, i - 1) for i in range(2, n, 2)]


def both(rows, cols, n_cols):
    return [(a * n_cols + b, c * n_cols + d) for a, c in rows for b, d in cols]


def body(spectrum, pupil, amplitude, offsets):
    tb = {k: jnp.asarray(v) for k, v in tables().items()}
    n_ky, n_kx = lax.axis_size(KY), lax.axis_size(KX)
    iy, ix, core = lax.axis_index(KY), lax.axis_index(KX), lax.axis_index("core")
    first = core == 0
    r0 = offsets[0, 0, 0] - (iy * TILE - RIM)
    c0 = offsets[0, 0, 1] - (ix * TILE - RIM)
    pos = jnp.stack([r0, c0, core])
    right, left = chain(n_kx)
    vert = between_chips(n_ky)
    vert_l, vert_r = both(vert, left, n_kx), both(vert, right, n_kx)
    swap = [(0, 1), (1, 0)]

    out_l, out_r, out_v, out_vl, out_vr = ends(pos, spectrum)
    in_l = lax.ppermute(out_l, KX, right)
    in_r = lax.ppermute(out_r, KX, left)
    in_v = lax.ppermute(out_v, KY, vert)
    in_vl = lax.ppermute(out_vl, ALL, vert_r)
    in_vr = lax.ppermute(out_vr, ALL, vert_l)
    in_i = lax.ppermute(spectrum, "core", swap)
    amp = order(amplitude, tb["perm"])
    pupil = turn(pos, pupil)
    in_c = lax.ppermute(cut(pos, in_l, in_r, pupil, amp, in_v, in_vl, in_vr), "core", swap)
    pieces = (spectrum, in_l, in_r, in_v, in_vl, in_vr, in_i, in_c)
    c, l, r, v, vl, vr, i, mine, other = led(pos, pieces, pupil, amp, tb)

    i = lax.ppermute(i, "core", swap)
    v = lax.ppermute(v, KY, vert)
    vl = lax.ppermute(vl, ALL, vert_l)
    vr = lax.ppermute(vr, ALL, vert_r)
    total = pair_sum(mine, lax.ppermute(other, "core", swap))
    l, r = sides(pos, l, r, i, v, total)
    l = lax.ppermute(l, KX, left)
    r = lax.ppermute(r, KX, right)
    tile = tile_sum(pos, (c, i, v, l, r, vl, vr))
    total = lax.all_to_all(total.reshape(32, 32, N), ("x", "z"), 0, 0)
    total = gather_sum(total, tile).reshape(4, 8, N)
    total = lax.all_to_all(total, ("yh", "yl"), 0, 0)
    return tile, jnp.sum(total, axis=0).reshape(-1)


def solution(mesh):
    fine = Mesh(mesh.devices.reshape(4, 2, 2, 8, 2), ALL)
    return jax.shard_map(
        body,
        mesh=fine,
        in_specs=(P(None, KY, KX), P(), P(KY, KX), P(KY, KX, None)),
        out_specs=(P(None, KY, KX), P(ALL)),
        check_vma=False,
    )
```

```python
import math

import jax
import jax.numpy as jnp
import ml_dtypes
import numpy as np
from jax import lax
from jax.experimental import pallas as pl
from jax.experimental.pallas import tpu as pltpu
from jax.sharding import Mesh
from jax.sharding import PartitionSpec as P

F32 = jnp.float32
BF16 = jnp.bfloat16
N = 1024
TILE = 512
RIM = 384
REGION = TILE + 2 * RIM
FLOOR2 = 0.0625
FREE = pl.CostEstimate(flops=1, bytes_accessed=1, transcendentals=0)


def split_np(t):
    hi = t.astype(np.float32).astype(ml_dtypes.bfloat16)
    lo = (t - hi.astype(np.float64)).astype(np.float32).astype(ml_dtypes.bfloat16)
    return hi, lo


def tables():
    b = np.arange(128)
    ang = 2.0 * np.pi / 128 * ((b[:, None] * b[None, :]) % 128)
    out = {}
    for name, sign in (("inv", 1.0), ("fwd", -1.0)):
        cr, ci = np.cos(ang) / 32.0, sign * np.sin(ang) / 32.0
        block = np.block([[cr, ci], [-ci, cr]])
        hi, lo = split_np(block)
        out["lane_" + name] = np.concatenate([hi, hi, lo], axis=0)
        out["row_" + name] = np.concatenate([hi.T, hi.T, lo.T], axis=1)
    tw = 2.0 * np.pi / N * (np.arange(8)[:, None] * b[None, :])
    tw = np.stack([np.cos(tw), np.sin(tw)]).astype(np.float32)
    out["tw_lane"] = tw.reshape(2, 8, 1, 128)
    out["tw_row"] = np.ascontiguousarray(np.broadcast_to(tw[:, :, :, None], (2, 8, 128, 128)))
    s = np.arange(N)
    perm = np.zeros((N, N), ml_dtypes.bfloat16)
    perm[s, (s // 128) + 8 * (s % 128)] = 1
    out["perm"] = perm
    return out


def cadd(p, q):
    return (p[0] + q[0], p[1] + q[1])


def csub(p, q):
    return (p[0] - q[0], p[1] - q[1])


def crot(p, sign):
    return (-p[1], p[0]) if sign > 0 else (p[1], -p[0])


def fft4(x0, x1, x2, x3, sign):
    t0, t1 = cadd(x0, x2), csub(x0, x2)
    t2, t3 = cadd(x1, x3), crot(csub(x1, x3), sign)
    return [cadd(t0, t2), cadd(t1, t3), csub(t0, t2), csub(t1, t3)]


def fft8(x, sign):
    even = fft4(x[0], x[2], x[4], x[6], sign)
    odd = fft4(x[1], x[3], x[5], x[7], sign)
    h = math.sqrt(0.5)
    r, i = odd[1]
    odd[1] = ((r - i) * h, (r + i) * h) if sign > 0 else ((r + i) * h, (i - r) * h)
    odd[2] = crot(odd[2], sign)
    r, i = odd[3]
    odd[3] = ((-r - i) * h, (r - i) * h) if sign > 0 else ((i - r) * h, (-r - i) * h)
    return [cadd(e, o) for e, o in zip(even, odd)] + [csub(e, o) for e, o in zip(even, odd)]


def split(x):
    hi = x.astype(BF16)
    return hi, (x - hi.astype(F32)).astype(BF16)


def dot(a, b):
    return jnp.dot(a, b, preferred_element_type=F32)


RB = 64
CB = 256


def led_body(
    pos_ref, own_ref, l_ref, r_ref, v_ref, vl_ref, vr_ref, i_ref, c_ref, p_ref, amp_ref,
    li_ref, lf_ref, ri_ref, rf_ref, twl_ref, twr_ref,
    oc_ref, ol_ref, or_ref, ov_ref, ovl_ref, ovr_ref, oi_ref, mine_ref, other_ref,
    w_ref, a_ref, s_refs, z_refs, s2_refs, z2_refs, to_ref, tm_ref, in_sem, out_sem,
):
    r0, c0, core = pos_ref[0], pos_ref[1], pos_ref[2]
    outer = pl.multiple_of((RIM + TILE) * core, 128)
    inner = pl.multiple_of((RIM + TILE) * (1 - core), 128)
    places = []
    for start, count in ((RIM, TILE), (outer, RIM)):
        for col, wide in ((RIM, TILE), (0, RIM), (RIM + TILE, RIM)):
            places.append(w_ref.at[:, pl.ds(start, count), pl.ds(col, wide)])
    arrivals = [own_ref, l_ref, r_ref, v_ref, vl_ref, vr_ref]
    arrivals.append(i_ref.at[:, pl.ds(pl.multiple_of(core * (TILE - RIM), 128), RIM), :])
    arrivals += [c_ref.at[:, :, pl.ds(0, RIM)], c_ref.at[:, :, pl.ds(RIM, RIM)]]
    sides = [w_ref.at[:, pl.ds(inner, RIM), pl.ds(col, wide)] for col, wide in ((RIM, TILE), (0, RIM), (RIM + TILE, RIM))]
    loads = [pltpu.make_async_copy(x, y, in_sem.at[k]) for k, (x, y) in enumerate(zip(arrivals, places + sides))]
    places.append(w_ref.at[:, pl.ds(inner, RIM), :])
    for load in loads:
        load.start()

    def lane_tile(k):
        return pl.ds(k * 128, 128)

    lane = lax.broadcasted_iota(jnp.int32, (16, 128), 1)
    line = lax.broadcasted_iota(jnp.int32, (16, 128), 0)
    for load in loads:
        load.wait()

    @pl.loop(0, REGION // 16, unroll=4)
    def _(i):
        rows = pl.ds(pl.multiple_of(i * 16, 16), 16)
        for q in range(2):
            for a in range(2):
                here, there = w_ref[q, rows, lane_tile(a)].astype(F32), w_ref[q, rows, lane_tile(a + 8)].astype(F32)
                w_ref[q, rows, lane_tile(a)] = jnp.where(lane + 128 * a >= c0, here, there).astype(BF16)

    @pl.loop(0, 16, unroll=2)
    def _(i):
        k = pl.multiple_of(i * 16, 16)
        for q in range(2):
            for a in range(8):
                here = w_ref[q, pl.ds(k, 16), lane_tile(a)].astype(F32)
                there = w_ref[q, pl.ds(k + N, 16), lane_tile(a)].astype(F32)
                w_ref[q, pl.ds(k, 16), lane_tile(a)] = jnp.where(line + k >= r0, here, there).astype(BF16)

    def put(ref, at, hs, yr, yi, step):
        (hr, lr), (hi, li) = split(yr), split(yi)
        for k, part in enumerate((hr, hi, lr, li)):
            if step is None:
                ref[at, k * 128:(k + 1) * 128] = part
            else:
                ref[at[0], pl.ds(at[1] + k * step, 16), hs] = part

    def first_vpu(n, s_ref):
        for i in range(RB // 16):
            rows = pl.ds(pl.multiple_of(n * RB + i * 16, 16), 16)
            x = []
            for a in range(8):
                pr, pi = p_ref[0, rows, lane_tile(a)].astype(F32), p_ref[1, rows, lane_tile(a)].astype(F32)
                wr, wi = w_ref[0, rows, lane_tile(a)].astype(F32), w_ref[1, rows, lane_tile(a)].astype(F32)
                x.append((pr * wr - pi * wi, pr * wi + pi * wr))
            for c, (yr, yi) in enumerate(fft8(x, 1)):
                if c > 0:
                    tr, ti = twl_ref[0, c], twl_ref[1, c]
                    yr, yi = yr * tr - yi * ti, yr * ti + yi * tr
                put(s_ref, pl.ds(c * RB + i * 16, 16), None, yr, yi, None)

    def first_mxu(n, s_ref):
        rows = pl.ds(pl.multiple_of(n * RB, RB), RB)
        acc = dot(s_ref[...], li_ref[0:512]) + dot(s_ref[:, 0:256], li_ref[512:768])
        for c in range(8):
            a_ref[0, rows, lane_tile(c)] = acc[c * RB:(c + 1) * RB, 0:128]
            a_ref[1, rows, lane_tile(c)] = acc[c * RB:(c + 1) * RB, 128:256]

    last = N // RB - 1
    first_vpu(0, s_refs[0])

    @pl.loop(0, N // RB // 2)
    def _(j):
        first_mxu(2 * j, s_refs[0])
        first_vpu(2 * j + 1, s_refs[1])
        first_mxu(2 * j + 1, s_refs[1])
        first_vpu(jnp.minimum(2 * j + 2, last), s_refs[0])

    def lanes(cb, h):
        return pl.ds(pl.multiple_of(cb * CB + h * 128, 128), 128)

    def second_in(cb, part, s2_ref):
        b = pl.multiple_of(part * 16, 16)
        for h in range(CB // 128):
            x = [tuple(a_ref[q, pl.ds(a * 128 + b, 16), lanes(cb, h)] for q in range(2)) for a in range(8)]
            for c, (yr, yi) in enumerate(fft8(x, 1)):
                if c > 0:
                    tr, ti = twr_ref[0, c, pl.ds(b, 16)], twr_ref[1, c, pl.ds(b, 16)]
                    yr, yi = yr * tr - yi * ti, yr * ti + yi * tr
                put(s2_ref, (c, b), pl.ds(h * 128, 128), yr, yi, 128)

    def second_mxu(cb, c, s2_ref, z2_ref):
        wide = pl.ds(pl.multiple_of(cb * CB, CB), CB)
        acc = dot(ri_ref[:, 0:512], s2_ref[c]) + dot(ri_ref[:, 512:768], s2_ref[c, 0:256])
        ir, ii = acc[0:128], acc[128:256]
        amp = amp_ref[pl.ds(pl.multiple_of(c * 128, 128), 128), wide].astype(F32)
        keep = 1.0 - amp * lax.rsqrt(jnp.maximum(ir * ir + ii * ii, FLOOR2))
        (hr, lr), (hi, li) = split(ir * keep), split(ii * keep)
        s3 = jnp.concatenate([hr, hi, lr, li], axis=0)
        z2_ref[c] = dot(rf_ref[:, 0:512], s3) + dot(rf_ref[:, 512:768], s3[0:256])

    def second_out(cb, part, z2_ref):
        for half in range(2):
            b = pl.multiple_of(part * 16 + half * 8, 8)
            for h in range(CB // 128):
                hs = pl.ds(h * 128, 128)
                x = []
                for c in range(8):
                    zr, zi = z2_ref[c, pl.ds(b, 8), hs], z2_ref[c, pl.ds(128 + b, 8), hs]
                    if c > 0:
                        tr, ti = twr_ref[0, c, pl.ds(b, 8)], twr_ref[1, c, pl.ds(b, 8)]
                        zr, zi = zr * tr + zi * ti, zi * tr - zr * ti
                    x.append((zr, zi))
                for a, (yr, yi) in enumerate(fft8(x, -1)):
                    a_ref[0, pl.ds(a * 128 + b, 8), lanes(cb, h)] = yr
                    a_ref[1, pl.ds(a * 128 + b, 8), lanes(cb, h)] = yi

    @pl.loop(0, 8)
    def _(c):
        second_in(0, c, s2_refs[0])

    for cb in range(N // CB):
        @pl.loop(0, 8, unroll=8)
        def _(c):
            if cb + 1 < N // CB:
                second_in(cb + 1, c, s2_refs[(cb + 1) % 2])
            second_mxu(cb, c, s2_refs[cb % 2], z2_refs[cb % 2])
            if cb > 0:
                second_out(cb - 1, c, z2_refs[(cb - 1) % 2])

    @pl.loop(0, 8)
    def _(c):
        second_out(N // CB - 1, c, z2_refs[(N // CB - 1) % 2])

    back = jnp.bitwise_and(N - c0, N - 1)

    def third_mxu(n, s_ref, z_ref):
        rows = pl.ds(pl.multiple_of(n * RB, RB), RB)
        for c in range(8):
            put(s_ref, pl.ds(c * RB, RB), None, a_ref[0, rows, lane_tile(c)], a_ref[1, rows, lane_tile(c)], None)
        z_ref[...] = dot(s_ref[...], lf_ref[0:512]) + dot(s_ref[:, 0:256], lf_ref[512:768])

    def third_vpu(n, z_ref):
        for i in range(RB // 16):
            rows = pl.ds(pl.multiple_of(n * RB + i * 16, 16), 16)
            x = []
            for c in range(8):
                sub = pl.ds(c * RB + i * 16, 16)
                zr, zi = z_ref[sub, 0:128], z_ref[sub, 128:256]
                if c > 0:
                    tr, ti = twl_ref[0, c], twl_ref[1, c]
                    zr, zi = zr * tr + zi * ti, zi * tr - zr * ti
                x.append((zr, zi))
            for a, (sr, si) in enumerate(fft8(x, -1)):
                pr, pi = p_ref[0, rows, lane_tile(a)].astype(F32), p_ref[1, rows, lane_tile(a)].astype(F32)
                wr, wi = w_ref[0, rows, lane_tile(a)].astype(F32), w_ref[1, rows, lane_tile(a)].astype(F32)
                w_ref[0, rows, lane_tile(a)] = (pr * sr + pi * si).astype(BF16)
                w_ref[1, rows, lane_tile(a)] = (pr * si - pi * sr).astype(BF16)
                a_ref[0, rows, lane_tile(a)] = (wr * sr + wi * si) * (1.0 / 256)
                a_ref[1, rows, lane_tile(a)] = (wr * si - wi * sr) * (1.0 / 256)
            for q in range(2):
                a_ref[q, rows, :] = pltpu.roll(a_ref[q, rows, :], back, 1)

    third_mxu(0, s_refs[0], z_refs[0])

    @pl.loop(0, N // RB // 2 - 1)
    def _(j):
        third_mxu(2 * j + 1, s_refs[1], z_refs[1])
        third_vpu(2 * j, z_refs[0])
        third_mxu(2 * j + 2, s_refs[0], z_refs[0])
        third_vpu(2 * j + 1, z_refs[1])

    third_mxu(last, s_refs[1], z_refs[1])
    third_vpu(last - 1, z_refs[0])
    third_vpu(last, z_refs[1])

    @pl.loop(0, N // 16, unroll=4)
    def _(i):
        rows = pl.ds(pl.multiple_of(i * 16, 16), 16)
        for q in range(2):
            for a in range(2):
                x = w_ref[q, rows, lane_tile(a)].astype(F32)
                ahead = lane + 128 * a >= c0
                w_ref[q, rows, lane_tile(a)] = jnp.where(ahead, x, 0.0).astype(BF16)
                w_ref[q, rows, lane_tile(a + 8)] = jnp.where(ahead, 0.0, x).astype(BF16)

    @pl.loop(0, 16, unroll=2)
    def _(i):
        k = pl.multiple_of(i * 16, 16)
        for q in range(2):
            for a in range(10):
                x = w_ref[q, pl.ds(k, 16), lane_tile(a)].astype(F32)
                ahead = line + k >= r0
                w_ref[q, pl.ds(k, 16), lane_tile(a)] = jnp.where(ahead, x, 0.0).astype(BF16)
                w_ref[q, pl.ds(k + N, 16), lane_tile(a)] = jnp.where(ahead, 0.0, x).astype(BF16)

    results = (oc_ref, ol_ref, or_ref, ov_ref, ovl_ref, ovr_ref, oi_ref)
    stores = [pltpu.make_async_copy(x, y, out_sem.at[k]) for k, (x, y) in enumerate(zip(places, results))]
    for store in stores:
        store.start()

    a_ref[:, N:N + 256, :] = a_ref[:, 0:256, :]
    shift = jnp.bitwise_and(r0, 7)
    base = r0 - shift
    up = jnp.bitwise_and(8 - shift, 7)
    inside = lax.broadcasted_iota(jnp.int32, (8, N), 0) < 8 - shift
    for s, (out_ref, t_ref, bit) in enumerate(((other_ref, to_ref, 1 - core), (mine_ref, tm_ref, core))):
        @pl.loop(0, 8)
        def _(i):
            u = jnp.right_shift(i, 1) * 256 + bit * 128 + jnp.bitwise_and(i, 1) * 64
            start = pl.multiple_of(u + base, 8)
            for q in range(2):
                to = pl.multiple_of(q * 512 + i * 64, 64)
                turned = [pltpu.roll(a_ref[q, pl.ds(start + 8 * j, 8), :], up, 0) for j in range(9)]
                lines = [jnp.where(inside, turned[j], turned[j + 1]) for j in range(8)]
                for j in range(0, 8, 2):
                    t_ref[pl.ds(to + 8 * j, 16), :] = jnp.concatenate(lines[j:j + 2], axis=0).astype(t_ref.dtype)

        store = pltpu.make_async_copy(t_ref, out_ref, out_sem.at[7 + s])
        store.start()
        stores.append(store)
    for store in stores:
        store.wait()


def led(pos, pieces, p, amp, tb):
    vm = pl.BlockSpec(memory_space=pltpu.VMEM)
    hbm = pl.BlockSpec(memory_space=pltpu.HBM)

    def rims(rows):
        return [jax.ShapeDtypeStruct((2, rows, cols), BF16) for cols in (TILE, RIM, RIM)]

    return pl.pallas_call(
        led_body,
        out_shape=rims(TILE) + rims(RIM) + [jax.ShapeDtypeStruct((2, RIM, REGION), BF16)]
        + [jax.ShapeDtypeStruct((N, N), F32), jax.ShapeDtypeStruct((N, N), BF16)],
        in_specs=[pl.BlockSpec(memory_space=pltpu.SMEM)] + [hbm] * 8 + [vm] * 8,
        out_specs=[hbm] * 9,
        scratch_shapes=[
            pltpu.VMEM((2, REGION, REGION), BF16),
            pltpu.VMEM((2, N + 264, N), F32),
            [pltpu.VMEM((8 * RB, 512), BF16)] * 2,
            [pltpu.VMEM((8 * RB, 256), F32)] * 2,
            [pltpu.VMEM((8, 512, CB), BF16)] * 2,
            [pltpu.VMEM((8, 256, CB), F32)] * 2,
            pltpu.VMEM((N, N), BF16),
            pltpu.VMEM((N, N), F32),
            pltpu.SemaphoreType.DMA((9,)),
            pltpu.SemaphoreType.DMA((9,)),
        ],
        compiler_params=pltpu.CompilerParams(vmem_limit_bytes=52 * 2**20),
        cost_estimate=pl.CostEstimate(flops=13 * 10**9, bytes_accessed=30 * 2**20, transcendentals=N * N),
        name="led",
    )(pos, *pieces, p, amp, tb["lane_inv"], tb["lane_fwd"], tb["row_inv"], tb["row_fwd"], tb["tw_lane"], tb["tw_row"])


def turn_body(pos_ref, p_ref, po_ref, x_ref):
    r0, c0 = pos_ref[0], pos_ref[1]

    @pl.loop(0, N // 16)
    def _(i):
        u = pl.multiple_of(i * 16, 16)
        for q in range(2):
            x_ref[q, pl.ds(u + 256, 16), :] = pltpu.roll(p_ref[q, pl.ds(u, 16), :].astype(F32), c0, 1)

    x_ref[:, 0:256, :] = x_ref[:, N:N + 256, :]
    start = 256 - r0
    shift = jnp.bitwise_and(start, 7)
    base = start - shift
    up = jnp.bitwise_and(8 - shift, 7)
    inside = lax.broadcasted_iota(jnp.int32, (8, N), 0) < 8 - shift

    @pl.loop(0, N // 64)
    def _(i):
        u = pl.multiple_of(i * 64, 64)
        first = pl.multiple_of(u + base, 8)
        for q in range(2):
            turned = [pltpu.roll(x_ref[q, pl.ds(first + 8 * j, 8), :], up, 0) for j in range(9)]
            rows = [jnp.where(inside, turned[j], turned[j + 1]) for j in range(8)]
            po_ref[q, pl.ds(u, 64), :] = jnp.concatenate(rows, axis=0).astype(BF16)


def turn(pos, pupil):
    vm = pl.BlockSpec(memory_space=pltpu.VMEM)
    return pl.pallas_call(
        turn_body,
        out_shape=jax.ShapeDtypeStruct((2, N, N), BF16),
        in_specs=[pl.BlockSpec(memory_space=pltpu.SMEM), vm],
        out_specs=vm,
        scratch_shapes=[pltpu.VMEM((2, N + 264, N), F32)],
        compiler_params=pltpu.CompilerParams(vmem_limit_bytes=40 * 2**20),
        cost_estimate=FREE,
        name="turn",
    )(pos, pupil)


def order_body(amp_ref, perm_ref, ao_ref):
    for i in range(4):
        part = dot(perm_ref[i * 256:(i + 1) * 256, :], amp_ref[...]).astype(BF16)
        part = lax.dot_general(part, perm_ref[...], (((1,), (1,)), ((), ())), preferred_element_type=F32)
        ao_ref[i * 256:(i + 1) * 256, :] = part.astype(BF16)


def order(amplitude, perm):
    vm = pl.BlockSpec(memory_space=pltpu.VMEM)
    return pl.pallas_call(
        order_body,
        out_shape=jax.ShapeDtypeStruct((N, N), BF16),
        in_specs=[vm, vm],
        out_specs=vm,
        compiler_params=pltpu.CompilerParams(vmem_limit_bytes=40 * 2**20),
        cost_estimate=FREE,
        name="order",
    )(amplitude, perm)


def ends_body(pos_ref, spec_ref, v_ref, vl_ref, vr_ref):
    gap = TILE - RIM
    outer = pos_ref[2] * gap

    @pl.loop(0, RIM // 32)
    def _(i):
        src = pl.ds(pl.multiple_of(outer + i * 32, 32), 32)
        dst = pl.ds(pl.multiple_of(i * 32, 32), 32)
        for q in range(2):
            v_ref[q, dst, :] = spec_ref[q, src, :]
            vl_ref[q, dst, :] = spec_ref[q, src, gap:]
            vr_ref[q, dst, :] = spec_ref[q, src, :RIM]


def ends(pos, spectrum):
    vm = pl.BlockSpec(memory_space=pltpu.VMEM)
    sizes = ((RIM, TILE), (RIM, RIM), (RIM, RIM))
    return pl.pallas_call(
        ends_body,
        out_shape=[jax.ShapeDtypeStruct((2,) + size, BF16) for size in sizes],
        in_specs=[pl.BlockSpec(memory_space=pltpu.SMEM), vm],
        out_specs=[vm] * 3,
        cost_estimate=FREE,
        name="ends",
    )(pos, spectrum)


def cut_body(pos_ref, l_ref, r_ref, *refs):
    out_ref = refs[-1]
    row = (1 - pos_ref[2]) * (TILE - RIM)

    @pl.loop(0, RIM // 32)
    def _(i):
        dst = pl.ds(pl.multiple_of(i * 32, 32), 32)
        src = pl.ds(pl.multiple_of(row + i * 32, 32), 32)
        for q in range(2):
            out_ref[q, dst, 0:RIM] = l_ref[q, src, :]
            out_ref[q, dst, RIM:2 * RIM] = r_ref[q, src, :]


def cut(pos, l, r, *tokens):
    vm = pl.BlockSpec(memory_space=pltpu.VMEM)
    return pl.pallas_call(
        cut_body,
        out_shape=jax.ShapeDtypeStruct((2, RIM, 2 * RIM), BF16),
        in_specs=[pl.BlockSpec(memory_space=pltpu.SMEM), vm, vm] + [pl.BlockSpec(memory_space=pl.ANY)] * len(tokens),
        out_specs=vm,
        cost_estimate=FREE,
        name="cut",
    )(pos, l, r, *tokens)


def sides_body(pos_ref, l_ref, r_ref, i_ref, *refs):
    ol_ref, or_ref = refs[-2:]
    at = (1 - pos_ref[2]) * (TILE - RIM)
    for mid_ref, col, out_ref in ((l_ref, 0, ol_ref), (r_ref, RIM + TILE, or_ref)):
        out_ref[...] = mid_ref[...]

        @pl.loop(0, RIM // 32)
        def _(i):
            src = pl.ds(pl.multiple_of(i * 32, 32), 32)
            dst = pl.ds(pl.multiple_of(at + i * 32, 32), 32)
            for q in range(2):
                add = i_ref[q, src, col:col + RIM].astype(F32)
                out_ref[q, dst, :] = (mid_ref[q, dst, :].astype(F32) + add).astype(BF16)


def sides(pos, l, r, i, *tokens):
    vm = pl.BlockSpec(memory_space=pltpu.VMEM)
    return pl.pallas_call(
        sides_body,
        out_shape=[jax.ShapeDtypeStruct(l.shape, BF16)] * 2,
        in_specs=[pl.BlockSpec(memory_space=pltpu.SMEM)] + [vm] * 3 + [pl.BlockSpec(memory_space=pl.ANY)] * len(tokens),
        out_specs=[vm] * 2,
        compiler_params=pltpu.CompilerParams(vmem_limit_bytes=32 * 2**20),
        cost_estimate=FREE,
        name="sides",
    )(pos, l, r, i, *tokens)


def tile_body(pos_ref, c_ref, i_ref, v_ref, l_ref, r_ref, vl_ref, vr_ref, out_ref):
    core = pos_ref[2]
    gap = TILE - RIM
    out_ref[...] = c_ref[...].astype(F32)
    out_ref[0, :, gap:] += l_ref[0].astype(F32)
    out_ref[0, :, :RIM] += r_ref[0].astype(F32)
    at_i = (1 - core) * gap
    at_v = core * gap

    @pl.loop(0, RIM // 32)
    def _(i):
        src = pl.ds(pl.multiple_of(i * 32, 32), 32)
        out_ref[0, pl.ds(pl.multiple_of(at_i + i * 32, 32), 32), :] += i_ref[0, src, RIM:RIM + TILE].astype(F32)
        dst = pl.ds(pl.multiple_of(at_v + i * 32, 32), 32)
        out_ref[0, dst, :] += v_ref[0, src, :].astype(F32)
        out_ref[0, dst, gap:] += vl_ref[0, src, :].astype(F32)
        out_ref[0, dst, :RIM] += vr_ref[0, src, :].astype(F32)


def tile_sum(pos, parts):
    def block(x):
        return pl.BlockSpec((1,) + x.shape[1:], lambda q: (q, 0, 0))

    return pl.pallas_call(
        tile_body,
        grid=(2,),
        out_shape=jax.ShapeDtypeStruct((2, TILE, TILE), F32),
        in_specs=[pl.BlockSpec(memory_space=pltpu.SMEM)] + [block(x) for x in parts],
        out_specs=pl.BlockSpec((1, TILE, TILE), lambda q: (q, 0, 0)),
        compiler_params=pltpu.CompilerParams(vmem_limit_bytes=32 * 2**20),
        cost_estimate=FREE,
        name="tile_sum",
    )(pos, *parts)


def pair_body(mine_ref, other_ref, token_ref, out_ref):
    @pl.loop(0, 4)
    def _(x):
        for y in range(2):
            for z in range(8):
                rows = pl.ds(pl.multiple_of(x * 256 + y * 128 + z * 16, 16), 16)
                out_ref[x, z, y] = (mine_ref[rows, :] + other_ref[rows, :].astype(F32)).astype(BF16)


def pair_sum(mine, other, token):
    vm = pl.BlockSpec(memory_space=pltpu.VMEM)
    return pl.pallas_call(
        pair_body,
        out_shape=jax.ShapeDtypeStruct((4, 8, 2, 16, N), BF16),
        in_specs=[vm, vm, pl.BlockSpec(memory_space=pl.ANY)],
        out_specs=vm,
        compiler_params=pltpu.CompilerParams(vmem_limit_bytes=24 * 2**20),
        cost_estimate=FREE,
        name="pair_sum",
    )(mine, other, token)


def gather_body(x_ref, *refs):
    out_ref = refs[-1]
    for i in range(2):
        rows = pl.ds(i * 16, 16)
        total = x_ref[0, rows, :].astype(F32)
        for k in range(1, 32):
            total += x_ref[k, rows, :].astype(F32)
        out_ref[rows, :] = total


def gather_sum(x, *tokens):
    vm = pl.BlockSpec(memory_space=pltpu.VMEM)
    return pl.pallas_call(
        gather_body,
        out_shape=jax.ShapeDtypeStruct((32, N), F32),
        in_specs=[vm] + [pl.BlockSpec(memory_space=pl.ANY)] * len(tokens),
        out_specs=vm,
        cost_estimate=FREE,
        name="gather_sum",
    )(x, *tokens)


KY, KX = ("x", "yh", "core"), ("z", "yl")
ALL = KY + KX


def chain(n):
    up = [(i, i + 1) for i in range(n - 1)]
    return up, [(j, i) for i, j in up]


def between_chips(n):
    return [(i, i + 1) for i in range(1, n - 1, 2)] + [(i, i - 1) for i in range(2, n, 2)]


def both(rows, cols, n_cols):
    return [(a * n_cols + b, c * n_cols + d) for a, c in rows for b, d in cols]


def body(spectrum, pupil, amplitude, offsets):
    tb = {k: jnp.asarray(v) for k, v in tables().items()}
    n_ky, n_kx = lax.axis_size(KY), lax.axis_size(KX)
    iy, ix, core = lax.axis_index(KY), lax.axis_index(KX), lax.axis_index("core")
    first = core == 0
    r0 = offsets[0, 0, 0] - (iy * TILE - RIM)
    c0 = offsets[0, 0, 1] - (ix * TILE - RIM)
    pos = jnp.stack([r0, c0, core])
    right, left = chain(n_kx)
    vert = between_chips(n_ky)
    vert_l, vert_r = both(vert, left, n_kx), both(vert, right, n_kx)
    swap = [(0, 1), (1, 0)]

    in_l = lax.ppermute(spectrum[:, :, TILE - RIM:], KX, right)
    in_r = lax.ppermute(spectrum[:, :, :RIM], KX, left)
    out_v, out_vl, out_vr = ends(pos, spectrum)
    in_v = lax.ppermute(out_v, KY, vert)
    in_vl = lax.ppermute(out_vl, ALL, vert_r)
    in_vr = lax.ppermute(out_vr, ALL, vert_l)
    in_i = lax.ppermute(spectrum, "core", swap)
    amp = order(amplitude, tb["perm"])
    pupil = turn(pos, pupil)
    in_c = lax.ppermute(cut(pos, in_l, in_r, pupil, amp, in_v, in_vl, in_vr), "core", swap)
    pieces = (spectrum, in_l, in_r, in_v, in_vl, in_vr, in_i, in_c)
    c, l, r, v, vl, vr, i, mine, other = led(pos, pieces, pupil, amp, tb)

    i = lax.ppermute(i, "core", swap)
    v = lax.ppermute(v, KY, vert)
    vl = lax.ppermute(vl, ALL, vert_l)
    vr = lax.ppermute(vr, ALL, vert_r)
    total = pair_sum(mine, lax.ppermute(other, "core", swap), i)
    l, r = sides(pos, l, r, i)
    l = lax.ppermute(l, KX, left)
    r = lax.ppermute(r, KX, right)
    tile = tile_sum(pos, (c, i, v, l, r, vl, vr))
    total = lax.all_to_all(total.reshape(32, 32, N), ("x", "z"), 0, 0)
    total = gather_sum(total, l, r, v, vl, vr).reshape(4, 8, N)
    total = lax.all_to_all(total, ("yh", "yl"), 0, 0)
    return tile, jnp.sum(total, axis=0).reshape(-1)


def solution(mesh):
    fine = Mesh(mesh.devices.reshape(4, 2, 2, 8, 2), ALL)
    return jax.shard_map(
        body,
        mesh=fine,
        in_specs=(P(None, KY, KX), P(), P(KY, KX), P(KY, KX, None)),
        out_specs=(P(None, KY, KX), P(ALL)),
        check_vma=False,
    )
```

```python
import math

import jax
import jax.numpy as jnp
import ml_dtypes
import numpy as np
from jax import lax
from jax.experimental import pallas as pl
from jax.experimental.pallas import tpu as pltpu
from jax.sharding import Mesh
from jax.sharding import PartitionSpec as P

F32 = jnp.float32
BF16 = jnp.bfloat16
N = 1024
TILE = 512
RIM = 384
REGION = TILE + 2 * RIM
FLOOR2 = 0.0625
FREE = pl.CostEstimate(flops=1, bytes_accessed=1, transcendentals=0)


def split_np(t):
    hi = t.astype(np.float32).astype(ml_dtypes.bfloat16)
    lo = (t - hi.astype(np.float64)).astype(np.float32).astype(ml_dtypes.bfloat16)
    return hi, lo


def tables():
    b = np.arange(128)
    ang = 2.0 * np.pi / 128 * ((b[:, None] * b[None, :]) % 128)
    out = {}
    for name, sign in (("inv", 1.0), ("fwd", -1.0)):
        cr, ci = np.cos(ang) / 32.0, sign * np.sin(ang) / 32.0
        block = np.block([[cr, ci], [-ci, cr]])
        hi, lo = split_np(block)
        out["lane_" + name] = np.concatenate([hi, hi, lo], axis=0)
        out["row_" + name] = np.concatenate([hi.T, hi.T, lo.T], axis=1)
    tw = 2.0 * np.pi / N * (np.arange(8)[:, None] * b[None, :])
    tw = np.stack([np.cos(tw), np.sin(tw)]).astype(np.float32)
    out["tw_lane"] = tw.reshape(2, 8, 1, 128)
    out["tw_row"] = np.ascontiguousarray(np.broadcast_to(tw[:, :, :, None], (2, 8, 128, 128)))
    s = np.arange(N)
    perm = np.zeros((N, N), ml_dtypes.bfloat16)
    perm[s, (s // 128) + 8 * (s % 128)] = 1
    out["perm"] = perm
    return out


def cadd(p, q):
    return (p[0] + q[0], p[1] + q[1])


def csub(p, q):
    return (p[0] - q[0], p[1] - q[1])


def crot(p, sign):
    return (-p[1], p[0]) if sign > 0 else (p[1], -p[0])


def fft4(x0, x1, x2, x3, sign):
    t0, t1 = cadd(x0, x2), csub(x0, x2)
    t2, t3 = cadd(x1, x3), crot(csub(x1, x3), sign)
    return [cadd(t0, t2), cadd(t1, t3), csub(t0, t2), csub(t1, t3)]


def fft8(x, sign):
    even = fft4(x[0], x[2], x[4], x[6], sign)
    odd = fft4(x[1], x[3], x[5], x[7], sign)
    h = math.sqrt(0.5)
    r, i = odd[1]
    odd[1] = ((r - i) * h, (r + i) * h) if sign > 0 else ((r + i) * h, (i - r) * h)
    odd[2] = crot(odd[2], sign)
    r, i = odd[3]
    odd[3] = ((-r - i) * h, (r - i) * h) if sign > 0 else ((i - r) * h, (-r - i) * h)
    return [cadd(e, o) for e, o in zip(even, odd)] + [csub(e, o) for e, o in zip(even, odd)]


def split(x):
    hi = x.astype(BF16)
    return hi, (x - hi.astype(F32)).astype(BF16)


def dot(a, b):
    return jnp.dot(a, b, preferred_element_type=F32)


RB = 64
CB = 256


def led_body(
    pos_ref, own_ref, l_ref, r_ref, v_ref, vl_ref, vr_ref, c_ref, p_ref, amp_ref,
    li_ref, lf_ref, ri_ref, rf_ref, twl_ref, twr_ref,
    oc_ref, ol_ref, or_ref, ov_ref, ovl_ref, ovr_ref, oi_ref, mine_ref, other_ref,
    w_ref, a_ref, s_refs, z_refs, s2_refs, z2_refs, to_ref, tm_ref, in_sem, out_sem,
):
    r0, c0, core = pos_ref[0], pos_ref[1], pos_ref[2]
    outer = pl.multiple_of((RIM + TILE) * core, 128)
    inner = pl.multiple_of((RIM + TILE) * (1 - core), 128)
    places = []
    for start, count in ((RIM, TILE), (outer, RIM)):
        for col, wide in ((RIM, TILE), (0, RIM), (RIM + TILE, RIM)):
            places.append(w_ref.at[:, pl.ds(start, count), pl.ds(col, wide)])
    places.append(w_ref.at[:, pl.ds(inner, RIM), :])
    arrivals = (own_ref, l_ref, r_ref, v_ref, vl_ref, vr_ref, c_ref)
    loads = [pltpu.make_async_copy(x, y, in_sem.at[k]) for k, (x, y) in enumerate(zip(arrivals, places))]
    for load in loads:
        load.start()

    def lane_tile(k):
        return pl.ds(k * 128, 128)

    lane = lax.broadcasted_iota(jnp.int32, (16, 128), 1)
    line = lax.broadcasted_iota(jnp.int32, (16, 128), 0)
    for load in loads:
        load.wait()

    @pl.loop(0, REGION // 16, unroll=4)
    def _(i):
        rows = pl.ds(pl.multiple_of(i * 16, 16), 16)
        for q in range(2):
            for a in range(2):
                here, there = w_ref[q, rows, lane_tile(a)].astype(F32), w_ref[q, rows, lane_tile(a + 8)].astype(F32)
                w_ref[q, rows, lane_tile(a)] = jnp.where(lane + 128 * a >= c0, here, there).astype(BF16)

    @pl.loop(0, 16, unroll=2)
    def _(i):
        k = pl.multiple_of(i * 16, 16)
        for q in range(2):
            for a in range(8):
                here = w_ref[q, pl.ds(k, 16), lane_tile(a)].astype(F32)
                there = w_ref[q, pl.ds(k + N, 16), lane_tile(a)].astype(F32)
                w_ref[q, pl.ds(k, 16), lane_tile(a)] = jnp.where(line + k >= r0, here, there).astype(BF16)

    def put(ref, at, hs, yr, yi, step):
        (hr, lr), (hi, li) = split(yr), split(yi)
        for k, part in enumerate((hr, hi, lr, li)):
            if step is None:
                ref[at, k * 128:(k + 1) * 128] = part
            else:
                ref[at[0], pl.ds(at[1] + k * step, 16), hs] = part

    def first_vpu(n, s_ref):
        for i in range(RB // 16):
            rows = pl.ds(pl.multiple_of(n * RB + i * 16, 16), 16)
            x = []
            for a in range(8):
                pr, pi = p_ref[0, rows, lane_tile(a)].astype(F32), p_ref[1, rows, lane_tile(a)].astype(F32)
                wr, wi = w_ref[0, rows, lane_tile(a)].astype(F32), w_ref[1, rows, lane_tile(a)].astype(F32)
                x.append((pr * wr - pi * wi, pr * wi + pi * wr))
            for c, (yr, yi) in enumerate(fft8(x, 1)):
                if c > 0:
                    tr, ti = twl_ref[0, c], twl_ref[1, c]
                    yr, yi = yr * tr - yi * ti, yr * ti + yi * tr
                put(s_ref, pl.ds(c * RB + i * 16, 16), None, yr, yi, None)

    def first_mxu(n, s_ref):
        rows = pl.ds(pl.multiple_of(n * RB, RB), RB)
        acc = dot(s_ref[...], li_ref[0:512]) + dot(s_ref[:, 0:256], li_ref[512:768])
        for c in range(8):
            a_ref[0, rows, lane_tile(c)] = acc[c * RB:(c + 1) * RB, 0:128]
            a_ref[1, rows, lane_tile(c)] = acc[c * RB:(c + 1) * RB, 128:256]

    last = N // RB - 1
    first_vpu(0, s_refs[0])

    @pl.loop(0, N // RB // 2)
    def _(j):
        first_mxu(2 * j, s_refs[0])
        first_vpu(2 * j + 1, s_refs[1])
        first_mxu(2 * j + 1, s_refs[1])
        first_vpu(jnp.minimum(2 * j + 2, last), s_refs[0])

    def lanes(cb, h):
        return pl.ds(pl.multiple_of(cb * CB + h * 128, 128), 128)

    def second_in(cb, part, s2_ref):
        b = pl.multiple_of(part * 16, 16)
        for h in range(CB // 128):
            x = [tuple(a_ref[q, pl.ds(a * 128 + b, 16), lanes(cb, h)] for q in range(2)) for a in range(8)]
            for c, (yr, yi) in enumerate(fft8(x, 1)):
                if c > 0:
                    tr, ti = twr_ref[0, c, pl.ds(b, 16)], twr_ref[1, c, pl.ds(b, 16)]
                    yr, yi = yr * tr - yi * ti, yr * ti + yi * tr
                put(s2_ref, (c, b), pl.ds(h * 128, 128), yr, yi, 128)

    def second_mxu(cb, c, s2_ref, z2_ref):
        wide = pl.ds(pl.multiple_of(cb * CB, CB), CB)
        acc = dot(ri_ref[:, 0:512], s2_ref[c]) + dot(ri_ref[:, 512:768], s2_ref[c, 0:256])
        ir, ii = acc[0:128], acc[128:256]
        amp = amp_ref[pl.ds(pl.multiple_of(c * 128, 128), 128), wide].astype(F32)
        keep = 1.0 - amp * lax.rsqrt(jnp.maximum(ir * ir + ii * ii, FLOOR2))
        (hr, lr), (hi, li) = split(ir * keep), split(ii * keep)
        s3 = jnp.concatenate([hr, hi, lr, li], axis=0)
        z2_ref[c] = dot(rf_ref[:, 0:512], s3) + dot(rf_ref[:, 512:768], s3[0:256])

    def second_out(cb, part, z2_ref):
        for half in range(2):
            b = pl.multiple_of(part * 16 + half * 8, 8)
            for h in range(CB // 128):
                hs = pl.ds(h * 128, 128)
                x = []
                for c in range(8):
                    zr, zi = z2_ref[c, pl.ds(b, 8), hs], z2_ref[c, pl.ds(128 + b, 8), hs]
                    if c > 0:
                        tr, ti = twr_ref[0, c, pl.ds(b, 8)], twr_ref[1, c, pl.ds(b, 8)]
                        zr, zi = zr * tr + zi * ti, zi * tr - zr * ti
                    x.append((zr, zi))
                for a, (yr, yi) in enumerate(fft8(x, -1)):
                    a_ref[0, pl.ds(a * 128 + b, 8), lanes(cb, h)] = yr
                    a_ref[1, pl.ds(a * 128 + b, 8), lanes(cb, h)] = yi

    @pl.loop(0, 8)
    def _(c):
        second_in(0, c, s2_refs[0])

    for cb in range(N // CB):
        @pl.loop(0, 8, unroll=8)
        def _(c):
            if cb + 1 < N // CB:
                second_in(cb + 1, c, s2_refs[(cb + 1) % 2])
            second_mxu(cb, c, s2_refs[cb % 2], z2_refs[cb % 2])
            if cb > 0:
                second_out(cb - 1, c, z2_refs[(cb - 1) % 2])

    @pl.loop(0, 8)
    def _(c):
        second_out(N // CB - 1, c, z2_refs[(N // CB - 1) % 2])

    back = jnp.bitwise_and(N - c0, N - 1)

    def third_mxu(n, s_ref, z_ref):
        rows = pl.ds(pl.multiple_of(n * RB, RB), RB)
        for c in range(8):
            put(s_ref, pl.ds(c * RB, RB), None, a_ref[0, rows, lane_tile(c)], a_ref[1, rows, lane_tile(c)], None)
        z_ref[...] = dot(s_ref[...], lf_ref[0:512]) + dot(s_ref[:, 0:256], lf_ref[512:768])

    def third_vpu(n, z_ref):
        for i in range(RB // 16):
            rows = pl.ds(pl.multiple_of(n * RB + i * 16, 16), 16)
            x = []
            for c in range(8):
                sub = pl.ds(c * RB + i * 16, 16)
                zr, zi = z_ref[sub, 0:128], z_ref[sub, 128:256]
                if c > 0:
                    tr, ti = twl_ref[0, c], twl_ref[1, c]
                    zr, zi = zr * tr + zi * ti, zi * tr - zr * ti
                x.append((zr, zi))
            for a, (sr, si) in enumerate(fft8(x, -1)):
                pr, pi = p_ref[0, rows, lane_tile(a)].astype(F32), p_ref[1, rows, lane_tile(a)].astype(F32)
                wr, wi = w_ref[0, rows, lane_tile(a)].astype(F32), w_ref[1, rows, lane_tile(a)].astype(F32)
                w_ref[0, rows, lane_tile(a)] = (pr * sr + pi * si).astype(BF16)
                w_ref[1, rows, lane_tile(a)] = (pr * si - pi * sr).astype(BF16)
                a_ref[0, rows, lane_tile(a)] = (wr * sr + wi * si) * (1.0 / 256)
                a_ref[1, rows, lane_tile(a)] = (wr * si - wi * sr) * (1.0 / 256)
            for q in range(2):
                a_ref[q, rows, :] = pltpu.roll(a_ref[q, rows, :], back, 1)

    third_mxu(0, s_refs[0], z_refs[0])

    @pl.loop(0, N // RB // 2 - 1)
    def _(j):
        third_mxu(2 * j + 1, s_refs[1], z_refs[1])
        third_vpu(2 * j, z_refs[0])
        third_mxu(2 * j + 2, s_refs[0], z_refs[0])
        third_vpu(2 * j + 1, z_refs[1])

    third_mxu(last, s_refs[1], z_refs[1])
    third_vpu(last - 1, z_refs[0])
    third_vpu(last, z_refs[1])

    @pl.loop(0, N // 16, unroll=4)
    def _(i):
        rows = pl.ds(pl.multiple_of(i * 16, 16), 16)
        for q in range(2):
            for a in range(2):
                x = w_ref[q, rows, lane_tile(a)].astype(F32)
                ahead = lane + 128 * a >= c0
                w_ref[q, rows, lane_tile(a)] = jnp.where(ahead, x, 0.0).astype(BF16)
                w_ref[q, rows, lane_tile(a + 8)] = jnp.where(ahead, 0.0, x).astype(BF16)

    @pl.loop(0, 16, unroll=2)
    def _(i):
        k = pl.multiple_of(i * 16, 16)
        for q in range(2):
            for a in range(10):
                x = w_ref[q, pl.ds(k, 16), lane_tile(a)].astype(F32)
                ahead = line + k >= r0
                w_ref[q, pl.ds(k, 16), lane_tile(a)] = jnp.where(ahead, x, 0.0).astype(BF16)
                w_ref[q, pl.ds(k + N, 16), lane_tile(a)] = jnp.where(ahead, 0.0, x).astype(BF16)

    results = (oc_ref, ol_ref, or_ref, ov_ref, ovl_ref, ovr_ref, oi_ref)
    stores = [pltpu.make_async_copy(x, y, out_sem.at[k]) for k, (x, y) in enumerate(zip(places, results))]
    for store in stores:
        store.start()

    a_ref[:, N:N + 256, :] = a_ref[:, 0:256, :]
    shift = jnp.bitwise_and(r0, 7)
    base = r0 - shift
    up = jnp.bitwise_and(8 - shift, 7)
    inside = lax.broadcasted_iota(jnp.int32, (8, N), 0) < 8 - shift
    for s, (out_ref, t_ref, bit) in enumerate(((other_ref, to_ref, 1 - core), (mine_ref, tm_ref, core))):
        @pl.loop(0, 8)
        def _(i):
            u = jnp.right_shift(i, 1) * 256 + bit * 128 + jnp.bitwise_and(i, 1) * 64
            start = pl.multiple_of(u + base, 8)
            for q in range(2):
                to = pl.multiple_of(q * 512 + i * 64, 64)
                turned = [pltpu.roll(a_ref[q, pl.ds(start + 8 * j, 8), :], up, 0) for j in range(9)]
                lines = [jnp.where(inside, turned[j], turned[j + 1]) for j in range(8)]
                for j in range(0, 8, 2):
                    t_ref[pl.ds(to + 8 * j, 16), :] = jnp.concatenate(lines[j:j + 2], axis=0).astype(t_ref.dtype)

        store = pltpu.make_async_copy(t_ref, out_ref, out_sem.at[7 + s])
        store.start()
        stores.append(store)
    for store in stores:
        store.wait()


def led(pos, pieces, p, amp, tb):
    vm = pl.BlockSpec(memory_space=pltpu.VMEM)
    hbm = pl.BlockSpec(memory_space=pltpu.HBM)

    def rims(rows):
        return [jax.ShapeDtypeStruct((2, rows, cols), BF16) for cols in (TILE, RIM, RIM)]

    return pl.pallas_call(
        led_body,
        out_shape=rims(TILE) + rims(RIM) + [jax.ShapeDtypeStruct((2, RIM, REGION), BF16)]
        + [jax.ShapeDtypeStruct((N, N), F32), jax.ShapeDtypeStruct((N, N), BF16)],
        in_specs=[pl.BlockSpec(memory_space=pltpu.SMEM)] + [hbm] * 7 + [vm] * 8,
        out_specs=[hbm] * 9,
        scratch_shapes=[
            pltpu.VMEM((2, REGION, REGION), BF16),
            pltpu.VMEM((2, N + 264, N), F32),
            [pltpu.VMEM((8 * RB, 512), BF16)] * 2,
            [pltpu.VMEM((8 * RB, 256), F32)] * 2,
            [pltpu.VMEM((8, 512, CB), BF16)] * 2,
            [pltpu.VMEM((8, 256, CB), F32)] * 2,
            pltpu.VMEM((N, N), BF16),
            pltpu.VMEM((N, N), F32),
            pltpu.SemaphoreType.DMA((7,)),
            pltpu.SemaphoreType.DMA((9,)),
        ],
        compiler_params=pltpu.CompilerParams(vmem_limit_bytes=52 * 2**20),
        cost_estimate=pl.CostEstimate(flops=13 * 10**9, bytes_accessed=30 * 2**20, transcendentals=N * N),
        name="led",
    )(pos, *pieces, p, amp, tb["lane_inv"], tb["lane_fwd"], tb["row_inv"], tb["row_fwd"], tb["tw_lane"], tb["tw_row"])


def turn_body(pos_ref, p_ref, po_ref, x_ref):
    r0, c0 = pos_ref[0], pos_ref[1]

    @pl.loop(0, N // 16)
    def _(i):
        u = pl.multiple_of(i * 16, 16)
        for q in range(2):
            x_ref[q, pl.ds(u + 256, 16), :] = pltpu.roll(p_ref[q, pl.ds(u, 16), :].astype(F32), c0, 1)

    x_ref[:, 0:256, :] = x_ref[:, N:N + 256, :]
    start = 256 - r0
    shift = jnp.bitwise_and(start, 7)
    base = start - shift
    up = jnp.bitwise_and(8 - shift, 7)
    inside = lax.broadcasted_iota(jnp.int32, (8, N), 0) < 8 - shift

    @pl.loop(0, N // 64)
    def _(i):
        u = pl.multiple_of(i * 64, 64)
        first = pl.multiple_of(u + base, 8)
        for q in range(2):
            turned = [pltpu.roll(x_ref[q, pl.ds(first + 8 * j, 8), :], up, 0) for j in range(9)]
            rows = [jnp.where(inside, turned[j], turned[j + 1]) for j in range(8)]
            po_ref[q, pl.ds(u, 64), :] = jnp.concatenate(rows, axis=0).astype(BF16)


def turn(pos, pupil):
    vm = pl.BlockSpec(memory_space=pltpu.VMEM)
    return pl.pallas_call(
        turn_body,
        out_shape=jax.ShapeDtypeStruct((2, N, N), BF16),
        in_specs=[pl.BlockSpec(memory_space=pltpu.SMEM), vm],
        out_specs=vm,
        scratch_shapes=[pltpu.VMEM((2, N + 264, N), F32)],
        compiler_params=pltpu.CompilerParams(vmem_limit_bytes=40 * 2**20),
        cost_estimate=FREE,
        name="turn",
    )(pos, pupil)


def order_body(amp_ref, perm_ref, ao_ref):
    for i in range(4):
        part = dot(perm_ref[i * 256:(i + 1) * 256, :], amp_ref[...]).astype(BF16)
        part = lax.dot_general(part, perm_ref[...], (((1,), (1,)), ((), ())), preferred_element_type=F32)
        ao_ref[i * 256:(i + 1) * 256, :] = part.astype(BF16)


def order(amplitude, perm):
    vm = pl.BlockSpec(memory_space=pltpu.VMEM)
    return pl.pallas_call(
        order_body,
        out_shape=jax.ShapeDtypeStruct((N, N), BF16),
        in_specs=[vm, vm],
        out_specs=vm,
        compiler_params=pltpu.CompilerParams(vmem_limit_bytes=40 * 2**20),
        cost_estimate=FREE,
        name="order",
    )(amplitude, perm)


def ends_body(pos_ref, spec_ref, v_ref, vl_ref, vr_ref):
    gap = TILE - RIM
    outer = pos_ref[2] * gap

    @pl.loop(0, RIM // 32)
    def _(i):
        src = pl.ds(pl.multiple_of(outer + i * 32, 32), 32)
        dst = pl.ds(pl.multiple_of(i * 32, 32), 32)
        for q in range(2):
            v_ref[q, dst, :] = spec_ref[q, src, :]
            vl_ref[q, dst, :] = spec_ref[q, src, gap:]
            vr_ref[q, dst, :] = spec_ref[q, src, :RIM]


def ends(pos, spectrum):
    vm = pl.BlockSpec(memory_space=pltpu.VMEM)
    sizes = ((RIM, TILE), (RIM, RIM), (RIM, RIM))
    return pl.pallas_call(
        ends_body,
        out_shape=[jax.ShapeDtypeStruct((2,) + size, BF16) for size in sizes],
        in_specs=[pl.BlockSpec(memory_space=pltpu.SMEM), vm],
        out_specs=[vm] * 3,
        cost_estimate=FREE,
        name="ends",
    )(pos, spectrum)


def cut_body(pos_ref, own_ref, l_ref, r_ref, *refs):
    out_ref = refs[-1]
    row = (1 - pos_ref[2]) * (TILE - RIM)

    @pl.loop(0, RIM // 32)
    def _(i):
        dst = pl.ds(pl.multiple_of(i * 32, 32), 32)
        src = pl.ds(pl.multiple_of(row + i * 32, 32), 32)
        for q in range(2):
            out_ref[q, dst, 0:RIM] = l_ref[q, src, :]
            out_ref[q, dst, RIM:RIM + TILE] = own_ref[q, src, :]
            out_ref[q, dst, RIM + TILE:] = r_ref[q, src, :]


def cut(pos, spectrum, l, r, *tokens):
    vm = pl.BlockSpec(memory_space=pltpu.VMEM)
    return pl.pallas_call(
        cut_body,
        out_shape=jax.ShapeDtypeStruct((2, RIM, REGION), BF16),
        in_specs=[pl.BlockSpec(memory_space=pltpu.SMEM)] + [vm] * 3 + [pl.BlockSpec(memory_space=pl.ANY)] * len(tokens),
        out_specs=vm,
        compiler_params=pltpu.CompilerParams(vmem_limit_bytes=24 * 2**20),
        cost_estimate=FREE,
        name="cut",
    )(pos, spectrum, l, r, *tokens)


def sides_body(pos_ref, l_ref, r_ref, i_ref, *refs):
    ol_ref, or_ref = refs[-2:]
    at = (1 - pos_ref[2]) * (TILE - RIM)
    for mid_ref, col, out_ref in ((l_ref, 0, ol_ref), (r_ref, RIM + TILE, or_ref)):
        out_ref[...] = mid_ref[...]

        @pl.loop(0, RIM // 32)
        def _(i):
            src = pl.ds(pl.multiple_of(i * 32, 32), 32)
            dst = pl.ds(pl.multiple_of(at + i * 32, 32), 32)
            for q in range(2):
                add = i_ref[q, src, col:col + RIM].astype(F32)
                out_ref[q, dst, :] = (mid_ref[q, dst, :].astype(F32) + add).astype(BF16)


def sides(pos, l, r, i, *tokens):
    vm = pl.BlockSpec(memory_space=pltpu.VMEM)
    return pl.pallas_call(
        sides_body,
        out_shape=[jax.ShapeDtypeStruct(l.shape, BF16)] * 2,
        in_specs=[pl.BlockSpec(memory_space=pltpu.SMEM)] + [vm] * 3 + [pl.BlockSpec(memory_space=pl.ANY)] * len(tokens),
        out_specs=[vm] * 2,
        compiler_params=pltpu.CompilerParams(vmem_limit_bytes=32 * 2**20),
        cost_estimate=FREE,
        name="sides",
    )(pos, l, r, i, *tokens)


def tile_body(pos_ref, c_ref, i_ref, v_ref, l_ref, r_ref, vl_ref, vr_ref, out_ref):
    core = pos_ref[2]
    gap = TILE - RIM
    out_ref[...] = c_ref[...].astype(F32)
    out_ref[0, :, gap:] += l_ref[0].astype(F32)
    out_ref[0, :, :RIM] += r_ref[0].astype(F32)
    at_i = (1 - core) * gap
    at_v = core * gap

    @pl.loop(0, RIM // 32)
    def _(i):
        src = pl.ds(pl.multiple_of(i * 32, 32), 32)
        out_ref[0, pl.ds(pl.multiple_of(at_i + i * 32, 32), 32), :] += i_ref[0, src, RIM:RIM + TILE].astype(F32)
        dst = pl.ds(pl.multiple_of(at_v + i * 32, 32), 32)
        out_ref[0, dst, :] += v_ref[0, src, :].astype(F32)
        out_ref[0, dst, gap:] += vl_ref[0, src, :].astype(F32)
        out_ref[0, dst, :RIM] += vr_ref[0, src, :].astype(F32)


def tile_sum(pos, parts):
    def block(x):
        return pl.BlockSpec((1,) + x.shape[1:], lambda q: (q, 0, 0))

    return pl.pallas_call(
        tile_body,
        grid=(2,),
        out_shape=jax.ShapeDtypeStruct((2, TILE, TILE), F32),
        in_specs=[pl.BlockSpec(memory_space=pltpu.SMEM)] + [block(x) for x in parts],
        out_specs=pl.BlockSpec((1, TILE, TILE), lambda q: (q, 0, 0)),
        compiler_params=pltpu.CompilerParams(vmem_limit_bytes=32 * 2**20),
        cost_estimate=FREE,
        name="tile_sum",
    )(pos, *parts)


def pair_body(mine_ref, other_ref, token_ref, out_ref):
    @pl.loop(0, 4)
    def _(x):
        for y in range(2):
            for z in range(8):
                rows = pl.ds(pl.multiple_of(x * 256 + y * 128 + z * 16, 16), 16)
                out_ref[x, z, y] = (mine_ref[rows, :] + other_ref[rows, :].astype(F32)).astype(BF16)


def pair_sum(mine, other, token):
    vm = pl.BlockSpec(memory_space=pltpu.VMEM)
    return pl.pallas_call(
        pair_body,
        out_shape=jax.ShapeDtypeStruct((4, 8, 2, 16, N), BF16),
        in_specs=[vm, vm, pl.BlockSpec(memory_space=pl.ANY)],
        out_specs=vm,
        compiler_params=pltpu.CompilerParams(vmem_limit_bytes=24 * 2**20),
        cost_estimate=FREE,
        name="pair_sum",
    )(mine, other, token)


def gather_body(x_ref, *refs):
    out_ref = refs[-1]
    for i in range(2):
        rows = pl.ds(i * 16, 16)
        total = x_ref[0, rows, :].astype(F32)
        for k in range(1, 32):
            total += x_ref[k, rows, :].astype(F32)
        out_ref[rows, :] = total


def gather_sum(x, *tokens):
    vm = pl.BlockSpec(memory_space=pltpu.VMEM)
    return pl.pallas_call(
        gather_body,
        out_shape=jax.ShapeDtypeStruct((32, N), F32),
        in_specs=[vm] + [pl.BlockSpec(memory_space=pl.ANY)] * len(tokens),
        out_specs=vm,
        cost_estimate=FREE,
        name="gather_sum",
    )(x, *tokens)


KY, KX = ("x", "yh", "core"), ("z", "yl")
ALL = KY + KX


def chain(n):
    up = [(i, i + 1) for i in range(n - 1)]
    return up, [(j, i) for i, j in up]


def between_chips(n):
    return [(i, i + 1) for i in range(1, n - 1, 2)] + [(i, i - 1) for i in range(2, n, 2)]


def both(rows, cols, n_cols):
    return [(a * n_cols + b, c * n_cols + d) for a, c in rows for b, d in cols]


def body(spectrum, pupil, amplitude, offsets):
    tb = {k: jnp.asarray(v) for k, v in tables().items()}
    n_ky, n_kx = lax.axis_size(KY), lax.axis_size(KX)
    iy, ix, core = lax.axis_index(KY), lax.axis_index(KX), lax.axis_index("core")
    first = core == 0
    r0 = offsets[0, 0, 0] - (iy * TILE - RIM)
    c0 = offsets[0, 0, 1] - (ix * TILE - RIM)
    pos = jnp.stack([r0, c0, core])
    right, left = chain(n_kx)
    vert = between_chips(n_ky)
    vert_l, vert_r = both(vert, left, n_kx), both(vert, right, n_kx)
    swap = [(0, 1), (1, 0)]

    in_l = lax.ppermute(spectrum[:, :, TILE - RIM:], KX, right)
    in_r = lax.ppermute(spectrum[:, :, :RIM], KX, left)
    out_v, out_vl, out_vr = ends(pos, spectrum)
    in_v = lax.ppermute(out_v, KY, vert)
    in_vl = lax.ppermute(out_vl, ALL, vert_r)
    in_vr = lax.ppermute(out_vr, ALL, vert_l)
    amp = order(amplitude, tb["perm"])
    pupil = turn(pos, pupil)
    in_c = lax.ppermute(cut(pos, spectrum, in_l, in_r, pupil, amp, in_v, in_vl, in_vr), "core", swap)
    pieces = (spectrum, in_l, in_r, in_v, in_vl, in_vr, in_c)
    c, l, r, v, vl, vr, i, mine, other = led(pos, pieces, pupil, amp, tb)

    i = lax.ppermute(i, "core", swap)
    v = lax.ppermute(v, KY, vert)
    vl = lax.ppermute(vl, ALL, vert_l)
    vr = lax.ppermute(vr, ALL, vert_r)
    total = pair_sum(mine, lax.ppermute(other, "core", swap), i)
    l, r = sides(pos, l, r, i)
    l = lax.ppermute(l, KX, left)
    r = lax.ppermute(r, KX, right)
    tile = tile_sum(pos, (c, i, v, l, r, vl, vr))
    total = lax.all_to_all(total.reshape(32, 32, N), ("x", "z"), 0, 0)
    corner = sum(x[0, :16, :128].astype(F32) for x in (l, r, v, vl, vr))
    total = gather_sum(total, corner).reshape(4, 8, N)
    total = lax.all_to_all(total, ("yh", "yl"), 0, 0)
    return tile, jnp.sum(total, axis=0).reshape(-1)


def solution(mesh):
    fine = Mesh(mesh.devices.reshape(4, 2, 2, 8, 2), ALL)
    return jax.shard_map(
        body,
        mesh=fine,
        in_specs=(P(None, KY, KX), P(), P(KY, KX), P(KY, KX, None)),
        out_specs=(P(None, KY, KX), P(ALL)),
        check_vma=False,
    )
```

```python
import math

import jax
import jax.numpy as jnp
import ml_dtypes
import numpy as np
from jax import lax
from jax.experimental import pallas as pl
from jax.experimental.pallas import tpu as pltpu
from jax.sharding import Mesh
from jax.sharding import PartitionSpec as P

F32 = jnp.float32
BF16 = jnp.bfloat16
N = 1024
TILE = 512
RIM = 384
REGION = TILE + 2 * RIM
FLOOR2 = 0.0625
FREE = pl.CostEstimate(flops=1, bytes_accessed=1, transcendentals=0)


def split_np(t):
    hi = t.astype(np.float32).astype(ml_dtypes.bfloat16)
    lo = (t - hi.astype(np.float64)).astype(np.float32).astype(ml_dtypes.bfloat16)
    return hi, lo


def tables():
    b = np.arange(128)
    ang = 2.0 * np.pi / 128 * ((b[:, None] * b[None, :]) % 128)
    out = {}
    for name, sign in (("inv", 1.0), ("fwd", -1.0)):
        cr, ci = np.cos(ang) / 32.0, sign * np.sin(ang) / 32.0
        block = np.block([[cr, ci], [-ci, cr]])
        hi, lo = split_np(block)
        out["lane_" + name] = np.concatenate([hi, hi, lo], axis=0)
        out["row_" + name] = np.concatenate([hi.T, hi.T, lo.T], axis=1)
    tw = 2.0 * np.pi / N * (np.arange(8)[:, None] * b[None, :])
    tw = np.stack([np.cos(tw), np.sin(tw)]).astype(np.float32)
    out["tw_lane"] = tw.reshape(2, 8, 1, 128)
    out["tw_row"] = np.ascontiguousarray(np.broadcast_to(tw[:, :, :, None], (2, 8, 128, 128)))
    s = np.arange(N)
    perm = np.zeros((N, N), ml_dtypes.bfloat16)
    perm[s, (s // 128) + 8 * (s % 128)] = 1
    out["perm"] = perm
    return out


def cadd(p, q):
    return (p[0] + q[0], p[1] + q[1])


def csub(p, q):
    return (p[0] - q[0], p[1] - q[1])


def crot(p, sign):
    return (-p[1], p[0]) if sign > 0 else (p[1], -p[0])


def fft4(x0, x1, x2, x3, sign):
    t0, t1 = cadd(x0, x2), csub(x0, x2)
    t2, t3 = cadd(x1, x3), crot(csub(x1, x3), sign)
    return [cadd(t0, t2), cadd(t1, t3), csub(t0, t2), csub(t1, t3)]


def fft8(x, sign):
    even = fft4(x[0], x[2], x[4], x[6], sign)
    odd = fft4(x[1], x[3], x[5], x[7], sign)
    h = math.sqrt(0.5)
    r, i = odd[1]
    odd[1] = ((r - i) * h, (r + i) * h) if sign > 0 else ((r + i) * h, (i - r) * h)
    odd[2] = crot(odd[2], sign)
    r, i = odd[3]
    odd[3] = ((-r - i) * h, (r - i) * h) if sign > 0 else ((i - r) * h, (-r - i) * h)
    return [cadd(e, o) for e, o in zip(even, odd)] + [csub(e, o) for e, o in zip(even, odd)]


def split(x):
    hi = x.astype(BF16)
    return hi, (x - hi.astype(F32)).astype(BF16)


def dot(a, b):
    return jnp.dot(a, b, preferred_element_type=F32)


RB = 64
CB = 256


def led_body(
    pos_ref, own_ref, l_ref, r_ref, v_ref, vl_ref, vr_ref, c_ref, p_ref, amp_ref,
    li_ref, lf_ref, ri_ref, rf_ref, twl_ref, twr_ref,
    oc_ref, ol_ref, or_ref, ov_ref, ovl_ref, ovr_ref, oi_ref, mine_ref, other_ref,
    w_ref, a_ref, s_refs, z_refs, s2_refs, z2_refs, to_ref, tm_ref, in_sem, out_sem,
):
    r0, c0, core = pos_ref[0], pos_ref[1], pos_ref[2]
    outer = pl.multiple_of((RIM + TILE) * core, 128)
    inner = pl.multiple_of((RIM + TILE) * (1 - core), 128)
    places = []
    for start, count in ((RIM, TILE), (outer, RIM)):
        for col, wide in ((RIM, TILE), (0, RIM), (RIM + TILE, RIM)):
            places.append(w_ref.at[:, pl.ds(start, count), pl.ds(col, wide)])
    places.append(w_ref.at[:, pl.ds(inner, RIM), :])
    arrivals = (own_ref, l_ref, r_ref, v_ref, vl_ref, vr_ref, c_ref)
    loads = [pltpu.make_async_copy(x, y, in_sem.at[k]) for k, (x, y) in enumerate(zip(arrivals, places))]
    for load in loads:
        load.start()

    def lane_tile(k):
        return pl.ds(k * 128, 128)

    lane = lax.broadcasted_iota(jnp.int32, (16, 128), 1)
    line = lax.broadcasted_iota(jnp.int32, (16, 128), 0)
    for load in loads:
        load.wait()

    @pl.loop(0, REGION // 16, unroll=4)
    def _(i):
        rows = pl.ds(pl.multiple_of(i * 16, 16), 16)
        for q in range(2):
            for a in range(2):
                here, there = w_ref[q, rows, lane_tile(a)].astype(F32), w_ref[q, rows, lane_tile(a + 8)].astype(F32)
                w_ref[q, rows, lane_tile(a)] = jnp.where(lane + 128 * a >= c0, here, there).astype(BF16)

    @pl.loop(0, 16, unroll=2)
    def _(i):
        k = pl.multiple_of(i * 16, 16)
        for q in range(2):
            for a in range(8):
                here = w_ref[q, pl.ds(k, 16), lane_tile(a)].astype(F32)
                there = w_ref[q, pl.ds(k + N, 16), lane_tile(a)].astype(F32)
                w_ref[q, pl.ds(k, 16), lane_tile(a)] = jnp.where(line + k >= r0, here, there).astype(BF16)

    def put(ref, at, hs, yr, yi, step):
        (hr, lr), (hi, li) = split(yr), split(yi)
        for k, part in enumerate((hr, hi, lr, li)):
            if step is None:
                ref[at, k * 128:(k + 1) * 128] = part
            else:
                ref[at[0], pl.ds(at[1] + k * step, 16), hs] = part

    def first_vpu(n, s_ref):
        for i in range(RB // 16):
            rows = pl.ds(pl.multiple_of(n * RB + i * 16, 16), 16)
            x = []
            for a in range(8):
                pr, pi = p_ref[0, rows, lane_tile(a)].astype(F32), p_ref[1, rows, lane_tile(a)].astype(F32)
                wr, wi = w_ref[0, rows, lane_tile(a)].astype(F32), w_ref[1, rows, lane_tile(a)].astype(F32)
                x.append((pr * wr - pi * wi, pr * wi + pi * wr))
            for c, (yr, yi) in enumerate(fft8(x, 1)):
                if c > 0:
                    tr, ti = twl_ref[0, c], twl_ref[1, c]
                    yr, yi = yr * tr - yi * ti, yr * ti + yi * tr
                put(s_ref, pl.ds(c * RB + i * 16, 16), None, yr, yi, None)

    def first_mxu(n, s_ref):
        rows = pl.ds(pl.multiple_of(n * RB, RB), RB)
        acc = dot(s_ref[...], li_ref[0:512]) + dot(s_ref[:, 0:256], li_ref[512:768])
        for c in range(8):
            a_ref[0, rows, lane_tile(c)] = acc[c * RB:(c + 1) * RB, 0:128]
            a_ref[1, rows, lane_tile(c)] = acc[c * RB:(c + 1) * RB, 128:256]

    last = N // RB - 1
    first_vpu(0, s_refs[0])

    @pl.loop(0, N // RB // 2)
    def _(j):
        first_mxu(2 * j, s_refs[0])
        first_vpu(2 * j + 1, s_refs[1])
        first_mxu(2 * j + 1, s_refs[1])
        first_vpu(jnp.minimum(2 * j + 2, last), s_refs[0])

    def lanes(cb, h):
        return pl.ds(pl.multiple_of(cb * CB + h * 128, 128), 128)

    def second_in(cb, part, s2_ref):
        b = pl.multiple_of(part * 16, 16)
        for h in range(CB // 128):
            x = [tuple(a_ref[q, pl.ds(a * 128 + b, 16), lanes(cb, h)] for q in range(2)) for a in range(8)]
            for c, (yr, yi) in enumerate(fft8(x, 1)):
                if c > 0:
                    tr, ti = twr_ref[0, c, pl.ds(b, 16)], twr_ref[1, c, pl.ds(b, 16)]
                    yr, yi = yr * tr - yi * ti, yr * ti + yi * tr
                put(s2_ref, (c, b), pl.ds(h * 128, 128), yr, yi, 128)

    def second_mxu(cb, c, s2_ref, z2_ref):
        wide = pl.ds(pl.multiple_of(cb * CB, CB), CB)
        acc = dot(ri_ref[:, 0:512], s2_ref[c]) + dot(ri_ref[:, 512:768], s2_ref[c, 0:256])
        ir, ii = acc[0:128], acc[128:256]
        amp = amp_ref[pl.ds(pl.multiple_of(c * 128, 128), 128), wide].astype(F32)
        keep = 1.0 - amp * lax.rsqrt(jnp.maximum(ir * ir + ii * ii, FLOOR2))
        (hr, lr), (hi, li) = split(ir * keep), split(ii * keep)
        s3 = jnp.concatenate([hr, hi, lr, li], axis=0)
        z2_ref[c] = dot(rf_ref[:, 0:512], s3) + dot(rf_ref[:, 512:768], s3[0:256])

    def second_out(cb, part, z2_ref):
        for half in range(2):
            b = pl.multiple_of(part * 16 + half * 8, 8)
            for h in range(CB // 128):
                hs = pl.ds(h * 128, 128)
                x = []
                for c in range(8):
                    zr, zi = z2_ref[c, pl.ds(b, 8), hs], z2_ref[c, pl.ds(128 + b, 8), hs]
                    if c > 0:
                        tr, ti = twr_ref[0, c, pl.ds(b, 8)], twr_ref[1, c, pl.ds(b, 8)]
                        zr, zi = zr * tr + zi * ti, zi * tr - zr * ti
                    x.append((zr, zi))
                for a, (yr, yi) in enumerate(fft8(x, -1)):
                    a_ref[0, pl.ds(a * 128 + b, 8), lanes(cb, h)] = yr
                    a_ref[1, pl.ds(a * 128 + b, 8), lanes(cb, h)] = yi

    @pl.loop(0, 8)
    def _(c):
        second_in(0, c, s2_refs[0])

    for cb in range(N // CB):
        @pl.loop(0, 8, unroll=8)
        def _(c):
            if cb + 1 < N // CB:
                second_in(cb + 1, c, s2_refs[(cb + 1) % 2])
            second_mxu(cb, c, s2_refs[cb % 2], z2_refs[cb % 2])
            if cb > 0:
                second_out(cb - 1, c, z2_refs[(cb - 1) % 2])

    @pl.loop(0, 8)
    def _(c):
        second_out(N // CB - 1, c, z2_refs[(N // CB - 1) % 2])

    back = jnp.bitwise_and(N - c0, N - 1)

    def third_mxu(n, s_ref, z_ref):
        rows = pl.ds(pl.multiple_of(n * RB, RB), RB)
        for c in range(8):
            put(s_ref, pl.ds(c * RB, RB), None, a_ref[0, rows, lane_tile(c)], a_ref[1, rows, lane_tile(c)], None)
        z_ref[...] = dot(s_ref[...], lf_ref[0:512]) + dot(s_ref[:, 0:256], lf_ref[512:768])

    def third_vpu(n, z_ref):
        for i in range(RB // 16):
            rows = pl.ds(pl.multiple_of(n * RB + i * 16, 16), 16)
            x = []
            for c in range(8):
                sub = pl.ds(c * RB + i * 16, 16)
                zr, zi = z_ref[sub, 0:128], z_ref[sub, 128:256]
                if c > 0:
                    tr, ti = twl_ref[0, c], twl_ref[1, c]
                    zr, zi = zr * tr + zi * ti, zi * tr - zr * ti
                x.append((zr, zi))
            for a, (sr, si) in enumerate(fft8(x, -1)):
                pr, pi = p_ref[0, rows, lane_tile(a)].astype(F32), p_ref[1, rows, lane_tile(a)].astype(F32)
                wr, wi = w_ref[0, rows, lane_tile(a)].astype(F32), w_ref[1, rows, lane_tile(a)].astype(F32)
                w_ref[0, rows, lane_tile(a)] = (pr * sr + pi * si).astype(BF16)
                w_ref[1, rows, lane_tile(a)] = (pr * si - pi * sr).astype(BF16)
                a_ref[0, rows, lane_tile(a)] = (wr * sr + wi * si) * (1.0 / 256)
                a_ref[1, rows, lane_tile(a)] = (wr * si - wi * sr) * (1.0 / 256)
            for q in range(2):
                a_ref[q, rows, :] = pltpu.roll(a_ref[q, rows, :], back, 1)

    third_mxu(0, s_refs[0], z_refs[0])

    @pl.loop(0, N // RB // 2 - 1)
    def _(j):
        third_mxu(2 * j + 1, s_refs[1], z_refs[1])
        third_vpu(2 * j, z_refs[0])
        third_mxu(2 * j + 2, s_refs[0], z_refs[0])
        third_vpu(2 * j + 1, z_refs[1])

    third_mxu(last, s_refs[1], z_refs[1])
    third_vpu(last - 1, z_refs[0])
    third_vpu(last, z_refs[1])

    @pl.loop(0, N // 16, unroll=4)
    def _(i):
        rows = pl.ds(pl.multiple_of(i * 16, 16), 16)
        for q in range(2):
            for a in range(2):
                x = w_ref[q, rows, lane_tile(a)].astype(F32)
                ahead = lane + 128 * a >= c0
                w_ref[q, rows, lane_tile(a)] = jnp.where(ahead, x, 0.0).astype(BF16)
                w_ref[q, rows, lane_tile(a + 8)] = jnp.where(ahead, 0.0, x).astype(BF16)

    @pl.loop(0, 16, unroll=2)
    def _(i):
        k = pl.multiple_of(i * 16, 16)
        for q in range(2):
            for a in range(10):
                x = w_ref[q, pl.ds(k, 16), lane_tile(a)].astype(F32)
                ahead = line + k >= r0
                w_ref[q, pl.ds(k, 16), lane_tile(a)] = jnp.where(ahead, x, 0.0).astype(BF16)
                w_ref[q, pl.ds(k + N, 16), lane_tile(a)] = jnp.where(ahead, 0.0, x).astype(BF16)

    results = (oc_ref, ol_ref, or_ref, ov_ref, ovl_ref, ovr_ref, oi_ref)
    stores = [pltpu.make_async_copy(x, y, out_sem.at[k]) for k, (x, y) in enumerate(zip(places, results))]
    for store in stores:
        store.start()

    a_ref[:, N:N + 256, :] = a_ref[:, 0:256, :]
    shift = jnp.bitwise_and(r0, 7)
    base = r0 - shift
    up = jnp.bitwise_and(8 - shift, 7)
    inside = lax.broadcasted_iota(jnp.int32, (8, N), 0) < 8 - shift
    for s, (out_ref, t_ref, bit) in enumerate(((other_ref, to_ref, 1 - core), (mine_ref, tm_ref, core))):
        @pl.loop(0, 8)
        def _(i):
            u = jnp.right_shift(i, 1) * 256 + bit * 128 + jnp.bitwise_and(i, 1) * 64
            start = pl.multiple_of(u + base, 8)
            for q in range(2):
                to = pl.multiple_of(q * 512 + i * 64, 64)
                turned = [pltpu.roll(a_ref[q, pl.ds(start + 8 * j, 8), :], up, 0) for j in range(9)]
                lines = [jnp.where(inside, turned[j], turned[j + 1]) for j in range(8)]
                for j in range(0, 8, 2):
                    t_ref[pl.ds(to + 8 * j, 16), :] = jnp.concatenate(lines[j:j + 2], axis=0).astype(t_ref.dtype)

        store = pltpu.make_async_copy(t_ref, out_ref, out_sem.at[7 + s])
        store.start()
        stores.append(store)
    for store in stores:
        store.wait()


def led(pos, pieces, p, amp, tb):
    vm = pl.BlockSpec(memory_space=pltpu.VMEM)
    hbm = pl.BlockSpec(memory_space=pltpu.HBM)

    def rims(rows):
        return [jax.ShapeDtypeStruct((2, rows, cols), BF16) for cols in (TILE, RIM, RIM)]

    return pl.pallas_call(
        led_body,
        out_shape=rims(TILE) + rims(RIM) + [jax.ShapeDtypeStruct((2, RIM, REGION), BF16)]
        + [jax.ShapeDtypeStruct((N, N), F32), jax.ShapeDtypeStruct((N, N), BF16)],
        in_specs=[pl.BlockSpec(memory_space=pltpu.SMEM)] + [hbm] * 7 + [vm] * 8,
        out_specs=[hbm] * 9,
        scratch_shapes=[
            pltpu.VMEM((2, REGION, REGION), BF16),
            pltpu.VMEM((2, N + 264, N), F32),
            [pltpu.VMEM((8 * RB, 512), BF16)] * 2,
            [pltpu.VMEM((8 * RB, 256), F32)] * 2,
            [pltpu.VMEM((8, 512, CB), BF16)] * 2,
            [pltpu.VMEM((8, 256, CB), F32)] * 2,
            pltpu.VMEM((N, N), BF16),
            pltpu.VMEM((N, N), F32),
            pltpu.SemaphoreType.DMA((7,)),
            pltpu.SemaphoreType.DMA((9,)),
        ],
        compiler_params=pltpu.CompilerParams(vmem_limit_bytes=52 * 2**20),
        cost_estimate=pl.CostEstimate(flops=13 * 10**9, bytes_accessed=30 * 2**20, transcendentals=N * N),
        name="led",
    )(pos, *pieces, p, amp, tb["lane_inv"], tb["lane_fwd"], tb["row_inv"], tb["row_fwd"], tb["tw_lane"], tb["tw_row"])


def turn_body(pos_ref, p_ref, po_ref, x_ref):
    r0, c0 = pos_ref[0], pos_ref[1]

    @pl.loop(0, N // 16)
    def _(i):
        u = pl.multiple_of(i * 16, 16)
        for q in range(2):
            x_ref[q, pl.ds(u + 256, 16), :] = pltpu.roll(p_ref[q, pl.ds(u, 16), :].astype(F32), c0, 1)

    x_ref[:, 0:256, :] = x_ref[:, N:N + 256, :]
    start = 256 - r0
    shift = jnp.bitwise_and(start, 7)
    base = start - shift
    up = jnp.bitwise_and(8 - shift, 7)
    inside = lax.broadcasted_iota(jnp.int32, (8, N), 0) < 8 - shift

    @pl.loop(0, N // 64)
    def _(i):
        u = pl.multiple_of(i * 64, 64)
        first = pl.multiple_of(u + base, 8)
        for q in range(2):
            turned = [pltpu.roll(x_ref[q, pl.ds(first + 8 * j, 8), :], up, 0) for j in range(9)]
            rows = [jnp.where(inside, turned[j], turned[j + 1]) for j in range(8)]
            po_ref[q, pl.ds(u, 64), :] = jnp.concatenate(rows, axis=0).astype(BF16)


def turn(pos, pupil):
    vm = pl.BlockSpec(memory_space=pltpu.VMEM)
    return pl.pallas_call(
        turn_body,
        out_shape=jax.ShapeDtypeStruct((2, N, N), BF16),
        in_specs=[pl.BlockSpec(memory_space=pltpu.SMEM), vm],
        out_specs=vm,
        scratch_shapes=[pltpu.VMEM((2, N + 264, N), F32)],
        compiler_params=pltpu.CompilerParams(vmem_limit_bytes=40 * 2**20),
        cost_estimate=FREE,
        name="turn",
    )(pos, pupil)


def order_body(amp_ref, perm_ref, ao_ref):
    for i in range(4):
        part = dot(perm_ref[i * 256:(i + 1) * 256, :], amp_ref[...]).astype(BF16)
        part = lax.dot_general(part, perm_ref[...], (((1,), (1,)), ((), ())), preferred_element_type=F32)
        ao_ref[i * 256:(i + 1) * 256, :] = part.astype(BF16)


def order(amplitude, perm):
    vm = pl.BlockSpec(memory_space=pltpu.VMEM)
    return pl.pallas_call(
        order_body,
        out_shape=jax.ShapeDtypeStruct((N, N), BF16),
        in_specs=[vm, vm],
        out_specs=vm,
        compiler_params=pltpu.CompilerParams(vmem_limit_bytes=40 * 2**20),
        cost_estimate=FREE,
        name="order",
    )(amplitude, perm)


def ends_body(pos_ref, spec_ref, v_ref, vl_ref, vr_ref):
    gap = TILE - RIM
    outer = pos_ref[2] * gap

    @pl.loop(0, RIM // 32)
    def _(i):
        src = pl.ds(pl.multiple_of(outer + i * 32, 32), 32)
        dst = pl.ds(pl.multiple_of(i * 32, 32), 32)
        for q in range(2):
            v_ref[q, dst, :] = spec_ref[q, src, :]
            vl_ref[q, dst, :] = spec_ref[q, src, gap:]
            vr_ref[q, dst, :] = spec_ref[q, src, :RIM]


def ends(pos, spectrum):
    vm = pl.BlockSpec(memory_space=pltpu.VMEM)
    sizes = ((RIM, TILE), (RIM, RIM), (RIM, RIM))
    return pl.pallas_call(
        ends_body,
        out_shape=[jax.ShapeDtypeStruct((2,) + size, BF16) for size in sizes],
        in_specs=[pl.BlockSpec(memory_space=pltpu.SMEM), vm],
        out_specs=[vm] * 3,
        cost_estimate=FREE,
        name="ends",
    )(pos, spectrum)


def cut_body(pos_ref, own_ref, l_ref, r_ref, *refs):
    out_ref = refs[-1]
    row = (1 - pos_ref[2]) * (TILE - RIM)

    @pl.loop(0, RIM // 32)
    def _(i):
        dst = pl.ds(pl.multiple_of(i * 32, 32), 32)
        src = pl.ds(pl.multiple_of(row + i * 32, 32), 32)
        for q in range(2):
            out_ref[q, dst, 0:RIM] = l_ref[q, src, :]
            out_ref[q, dst, RIM:RIM + TILE] = own_ref[q, src, :]
            out_ref[q, dst, RIM + TILE:] = r_ref[q, src, :]


def cut(pos, spectrum, l, r, *tokens):
    vm = pl.BlockSpec(memory_space=pltpu.VMEM)
    return pl.pallas_call(
        cut_body,
        out_shape=jax.ShapeDtypeStruct((2, RIM, REGION), BF16),
        in_specs=[pl.BlockSpec(memory_space=pltpu.SMEM)] + [vm] * 3 + [pl.BlockSpec(memory_space=pl.ANY)] * len(tokens),
        out_specs=vm,
        compiler_params=pltpu.CompilerParams(vmem_limit_bytes=24 * 2**20),
        cost_estimate=FREE,
        name="cut",
    )(pos, spectrum, l, r, *tokens)


def sides_body(pos_ref, l_ref, r_ref, i_ref, *refs):
    ol_ref, or_ref = refs[-2:]
    at = (1 - pos_ref[2]) * (TILE - RIM)
    for mid_ref, col, out_ref in ((l_ref, 0, ol_ref), (r_ref, RIM + TILE, or_ref)):
        out_ref[...] = mid_ref[...]

        @pl.loop(0, RIM // 32)
        def _(i):
            src = pl.ds(pl.multiple_of(i * 32, 32), 32)
            dst = pl.ds(pl.multiple_of(at + i * 32, 32), 32)
            for q in range(2):
                add = i_ref[q, src, col:col + RIM].astype(F32)
                out_ref[q, dst, :] = (mid_ref[q, dst, :].astype(F32) + add).astype(BF16)


def sides(pos, l, r, i, *tokens):
    vm = pl.BlockSpec(memory_space=pltpu.VMEM)
    return pl.pallas_call(
        sides_body,
        out_shape=[jax.ShapeDtypeStruct(l.shape, BF16)] * 2,
        in_specs=[pl.BlockSpec(memory_space=pltpu.SMEM)] + [vm] * 3 + [pl.BlockSpec(memory_space=pl.ANY)] * len(tokens),
        out_specs=[vm] * 2,
        compiler_params=pltpu.CompilerParams(vmem_limit_bytes=32 * 2**20),
        cost_estimate=FREE,
        name="sides",
    )(pos, l, r, i, *tokens)


def tile_body(pos_ref, c_ref, i_ref, v_ref, l_ref, r_ref, vl_ref, vr_ref, out_ref):
    core = pos_ref[2]
    gap = TILE - RIM
    out_ref[...] = c_ref[...].astype(F32)
    out_ref[0, :, gap:] += l_ref[0].astype(F32)
    out_ref[0, :, :RIM] += r_ref[0].astype(F32)
    at_i = (1 - core) * gap
    at_v = core * gap

    @pl.loop(0, RIM // 32)
    def _(i):
        src = pl.ds(pl.multiple_of(i * 32, 32), 32)
        out_ref[0, pl.ds(pl.multiple_of(at_i + i * 32, 32), 32), :] += i_ref[0, src, RIM:RIM + TILE].astype(F32)
        dst = pl.ds(pl.multiple_of(at_v + i * 32, 32), 32)
        out_ref[0, dst, :] += v_ref[0, src, :].astype(F32)
        out_ref[0, dst, gap:] += vl_ref[0, src, :].astype(F32)
        out_ref[0, dst, :RIM] += vr_ref[0, src, :].astype(F32)


def tile_sum(pos, parts):
    def block(x):
        return pl.BlockSpec((1,) + x.shape[1:], lambda q: (q, 0, 0))

    return pl.pallas_call(
        tile_body,
        grid=(2,),
        out_shape=jax.ShapeDtypeStruct((2, TILE, TILE), F32),
        in_specs=[pl.BlockSpec(memory_space=pltpu.SMEM)] + [block(x) for x in parts],
        out_specs=pl.BlockSpec((1, TILE, TILE), lambda q: (q, 0, 0)),
        compiler_params=pltpu.CompilerParams(vmem_limit_bytes=32 * 2**20),
        cost_estimate=FREE,
        name="tile_sum",
    )(pos, *parts)


def pair_body(mine_ref, other_ref, token_ref, out_ref):
    @pl.loop(0, 4)
    def _(x):
        for y in range(2):
            for z in range(8):
                rows = pl.ds(pl.multiple_of(x * 256 + y * 128 + z * 16, 16), 16)
                out_ref[x, z, y] = (mine_ref[rows, :] + other_ref[rows, :].astype(F32)).astype(BF16)


def pair_sum(mine, other, token):
    vm = pl.BlockSpec(memory_space=pltpu.VMEM)
    return pl.pallas_call(
        pair_body,
        out_shape=jax.ShapeDtypeStruct((4, 8, 2, 16, N), BF16),
        in_specs=[vm, vm, pl.BlockSpec(memory_space=pl.ANY)],
        out_specs=vm,
        compiler_params=pltpu.CompilerParams(vmem_limit_bytes=24 * 2**20),
        cost_estimate=FREE,
        name="pair_sum",
    )(mine, other, token)


def gather_body(pos_ref, x_ref, token_ref, *refs):
    sum_ref = refs[-1]
    for i in range(2):
        rows = pl.ds(i * 16, 16)
        total = x_ref[0, rows, :].astype(F32)
        for k in range(1, 32):
            total += x_ref[k, rows, :].astype(F32)
        sum_ref[rows, :] = total
    for k, out_ref in enumerate(refs[:-1]):
        out_ref[...] = sum_ref[pl.ds(pl.multiple_of(jnp.bitwise_xor(pos_ref[3], k) * 8, 8), 8), :]


def gather_sum(pos, x, token):
    vm = pl.BlockSpec(memory_space=pltpu.VMEM)
    return pl.pallas_call(
        gather_body,
        out_shape=[jax.ShapeDtypeStruct((8, N), F32)] * 4,
        in_specs=[pl.BlockSpec(memory_space=pltpu.SMEM), vm, pl.BlockSpec(memory_space=pl.ANY)],
        out_specs=[vm] * 4,
        scratch_shapes=[pltpu.VMEM((32, N), F32)],
        cost_estimate=FREE,
        name="gather_sum",
    )(pos, x, token)


KY, KX = ("x", "yh", "core"), ("z", "yl")
ALL = KY + KX


def chain(n):
    up = [(i, i + 1) for i in range(n - 1)]
    return up, [(j, i) for i, j in up]


def between_chips(n):
    return [(i, i + 1) for i in range(1, n - 1, 2)] + [(i, i - 1) for i in range(2, n, 2)]


def both(rows, cols, n_cols):
    return [(a * n_cols + b, c * n_cols + d) for a, c in rows for b, d in cols]


def body(spectrum, pupil, amplitude, offsets):
    tb = {k: jnp.asarray(v) for k, v in tables().items()}
    n_ky, n_kx = lax.axis_size(KY), lax.axis_size(KX)
    iy, ix, core = lax.axis_index(KY), lax.axis_index(KX), lax.axis_index("core")
    first = core == 0
    r0 = offsets[0, 0, 0] - (iy * TILE - RIM)
    c0 = offsets[0, 0, 1] - (ix * TILE - RIM)
    pos = jnp.stack([r0, c0, core, lax.axis_index(("yh", "yl"))])
    right, left = chain(n_kx)
    vert = between_chips(n_ky)
    vert_l, vert_r = both(vert, left, n_kx), both(vert, right, n_kx)
    swap = [(0, 1), (1, 0)]

    in_l = lax.ppermute(spectrum[:, :, TILE - RIM:], KX, right)
    in_r = lax.ppermute(spectrum[:, :, :RIM], KX, left)
    out_v, out_vl, out_vr = ends(pos, spectrum)
    in_v = lax.ppermute(out_v, KY, vert)
    in_vl = lax.ppermute(out_vl, ALL, vert_r)
    in_vr = lax.ppermute(out_vr, ALL, vert_l)
    amp = order(amplitude, tb["perm"])
    pupil = turn(pos, pupil)
    in_c = lax.ppermute(cut(pos, spectrum, in_l, in_r, pupil, amp, in_v, in_vl, in_vr), "core", swap)
    pieces = (spectrum, in_l, in_r, in_v, in_vl, in_vr, in_c)
    c, l, r, v, vl, vr, i, mine, other = led(pos, pieces, pupil, amp, tb)

    i = lax.ppermute(i, "core", swap)
    v = lax.ppermute(v, KY, vert)
    vl = lax.ppermute(vl, ALL, vert_l)
    vr = lax.ppermute(vr, ALL, vert_r)
    total = pair_sum(mine, lax.ppermute(other, "core", swap), i)
    l, r = sides(pos, l, r, i)
    l = lax.ppermute(l, KX, left)
    r = lax.ppermute(r, KX, right)
    tile = tile_sum(pos, (c, i, v, l, r, vl, vr))
    total = lax.all_to_all(total.reshape(32, 32, N), ("x", "z"), 0, 0)
    mine, *others = gather_sum(pos, total, tile)
    for k, other in enumerate(others, 1):
        mine = mine + lax.ppermute(other, ("yh", "yl"), [(i, i ^ k) for i in range(4)])
    return tile, mine.reshape(-1)


def solution(mesh):
    fine = Mesh(mesh.devices.reshape(4, 2, 2, 8, 2), ALL)
    return jax.shard_map(
        body,
        mesh=fine,
        in_specs=(P(None, KY, KX), P(), P(KY, KX), P(KY, KX, None)),
        out_specs=(P(None, KY, KX), P(ALL)),
        check_vma=False,
    )
```
